32 devices in a mesh: groups: 2 (over y), row: 4 (over z), col: 4 (over x, core).
Axes of the slice: x: 2, y: 2, z: 4, core: 2. Of those that a mesh axis runs over, the one named last changes fastest.
Arguments:
- features: bfloat16 [8, 2048, 256], P(('groups', 'row'), 'col'), parts along dimension 0, may hold values from -6 to 6
- tile_values: bfloat16 [8, 4, 1024, 4096], P(('groups', 'row'), 'col'), parts along dimension 0, may hold values from -0.125 to 0.125
- tile_rows: int32 [8, 4, 1024], P(('groups', 'row'), 'col'), parts along dimension 0, may hold values from 0 to 31
- tile_cols: int32 [8, 4, 1024], P(('groups', 'row'), 'col'), parts along dimension 0, may hold values from 0 to 31
- counts: int32 [8, 4], P(('groups', 'row'), 'col'), parts along dimension 0, may hold values from 128 to 1024, as said below
- weight: bfloat16 [256, 256], replicated, may hold values from -0.375 to 0.375
- bias: float32 [256], replicated, may hold values from -3 to 3
Outputs:
- layer_out: bfloat16 [8, 2048, 256], P(('groups', 'col'), 'row'), parts along dimension 0
The draws below stay inside these ranges and needn't reach their ends.
There are 2 independent parts, one for each index of `groups`. The reference program is written for one: setup_inputs(seed, part) draws one part's arguments, and reference() takes and returns one part's arrays. A program takes and returns all parts, laid end to end along the dimension named above; an argument that names none is the same for every part. Nothing has to cross between parts.
Inputs may be any that keep to these rules, and one draw needn't show every extreme that they name: Slots at or past counts[r, c] hold values that are to be ignored; coordinate pairs may repeat within a cell, and repeated tiles add. In every draw one grid cell has exactly 1024 live slots.
All inputs are finite; a program needn't handle non-finite values.
Results may differ from the reference program's by a relative error of at most 0.0046.
Values may be sent and summed in bfloat16 or wider, within the bound.
No kernel may reach another device: no remote copies, remote signals or barrier semaphores. Data moves between devices by JAX's collectives and lax.ppermute only.
A program may use at most 128 MiB of HBM per device.

```python
import jax
import jax.numpy as jnp
from jax import lax

F = 256
TILE = 64
P_SIZE = 512
TILES = 1024
N_ROW = 4
N_COL = 4


def draw_counts(key, part):
    first_key = jax.random.fold_in(key, 11)
    second_key = jax.random.fold_in(key, 23)
    third_key = jax.random.fold_in(key, 37)
    left_draw = jax.random.randint(first_key, (N_ROW * N_COL,), 1, TILES + 1, dtype=jnp.int32)
    right_draw = jax.random.randint(second_key, (N_ROW * N_COL,), 1, TILES + 1, dtype=jnp.int32)
    loads = jnp.maximum(left_draw * right_draw // TILES, TILES // 8)
    chosen = jax.random.randint(third_key, (), 0, N_ROW * N_COL, dtype=jnp.int32)
    loads = loads.at[chosen].set(TILES)
    return loads.reshape(N_ROW, N_COL).astype(jnp.int32)


def touch_ends(array, key, low, top_value):
    longest = array.shape.index(max(array.shape))
    spots = []
    for shift in (0, 1):
        where = [jax.random.randint(jax.random.fold_in(key, axis), (), 0, length) for axis, length in enumerate(array.shape)]
        where[longest] = (where[longest] + shift) % array.shape[longest]
        spots.append(tuple(where))
    return array.at[spots[0]].set(low).at[spots[1]].set(top_value)


def level_of(own_key, extent, split, least, high):
    def one(axis_at, blocks):
        heights = jax.random.uniform(jax.random.fold_in(jax.random.fold_in(own_key, 6), axis_at), (blocks,), jnp.float32, least / len(split), high / len(split))
        return jnp.repeat(jnp.exp(heights), extent[axis_at] // blocks).reshape((-1,) + (1,) * (len(extent) - axis_at - 1))

    gain = one(*split[0])
    for cut in split[1:]:
        gain = gain * one(*cut)
    return gain


def scatter_about(stream_key, shape, width, bound, shards=(), held_as=jnp.bfloat16):
    gain = level_of(stream_key, shape, shards, -0.22, 0.18) if shards else 1.0
    entries = jax.random.normal(stream_key, shape, jnp.float32) * width * gain
    return jnp.minimum(jnp.maximum(entries, -bound), bound).astype(held_as)


def setup_inputs(seed: int = 0, part: int = 0) -> dict:
    key_list = jax.random.split(jax.random.key(seed), 8)
    own_keys = jax.random.split(jax.random.fold_in(key_list[7], part), 8)
    return {
        "features": scatter_about(own_keys[0], (N_ROW, N_COL * P_SIZE, F), 1.0, 6.0, ((0, 4), (1, 4))),
        "tile_values": scatter_about(own_keys[1], (N_ROW, N_COL, TILES, TILE * TILE), (TILES * TILE * TILE // (4 * P_SIZE)) ** -0.5, 0.125, ((0, 4), (1, 4))),
        "tile_rows": touch_ends(jax.random.randint(own_keys[2], (N_ROW, N_COL, TILES), 0, N_ROW * P_SIZE // TILE), jax.random.fold_in(own_keys[2], 1), 0, (N_ROW * P_SIZE // TILE) - 1).astype(jnp.int32),
        "tile_cols": touch_ends(jax.random.randint(own_keys[3], (N_ROW, N_COL, TILES), 0, N_COL * P_SIZE // TILE), jax.random.fold_in(own_keys[3], 1), 0, (N_COL * P_SIZE // TILE) - 1).astype(jnp.int32),
        "counts": draw_counts(jax.random.fold_in(jax.random.fold_in(key_list[7], part), 71), part),
        "weight": scatter_about(key_list[5], (F, F), F ** -0.5, 0.375),
        "bias": scatter_about(key_list[6], (F,), 0.5, 3.0, (), jnp.float32),
    }


def reference(features, tile_values, tile_rows, tile_cols, counts, weight, bias):
    block_size = min(128, TILES)
    out_tiles = N_ROW * P_SIZE // TILE
    running = jnp.zeros((N_COL, out_tiles, TILE, F), jnp.float32)
    cells = N_ROW * N_COL
    all_values = tile_values.reshape(cells, TILES, TILE * TILE)
    all_rows = tile_rows.reshape(cells, TILES).astype(jnp.int32)
    all_cols = tile_cols.reshape(cells, TILES).astype(jnp.int32)
    all_counts = counts.reshape(cells).astype(jnp.int32)
    cell_index = jnp.arange(cells, dtype=jnp.int32)
    grid_rows = cell_index // N_COL
    grid_cols = cell_index % N_COL

    def cell_step(running, item):
        values, tile_row, tile_col, live_count, grid_row, grid_col = item
        source = lax.dynamic_index_in_dim(features, grid_row, 0, keepdims=False).reshape(N_COL * P_SIZE // TILE, TILE, F)

        def block_step(block_index, running):
            first_slot = (block_index * block_size).astype(jnp.int32)
            tile_block = lax.dynamic_slice_in_dim(values, first_slot, block_size, 0).reshape(block_size, TILE, TILE).astype(jnp.float32)
            target_rows = lax.dynamic_slice_in_dim(tile_row, first_slot, block_size, 0)
            source_cols = lax.dynamic_slice_in_dim(tile_col, first_slot, block_size, 0)
            inputs = source[source_cols].astype(jnp.float32)
            products = jnp.einsum('bij,bjf->bif', tile_block, inputs, precision=lax.Precision.HIGHEST)
            is_live = first_slot + jnp.arange(block_size, dtype=jnp.int32) < live_count
            target = jnp.where(is_live, target_rows, out_tiles)
            return running.at[grid_col, target].add(products, mode="drop")

        block_count = (live_count + block_size - 1) // block_size
        running = lax.fori_loop(0, block_count, block_step, running)
        return running, None

    running, unused = lax.scan(cell_step, running, (all_values, all_rows, all_cols, all_counts, grid_rows, grid_cols))
    hidden = running.reshape(N_COL * N_ROW * P_SIZE, F).astype(jnp.bfloat16)
    mixed = jnp.dot(hidden, weight, preferred_element_type=jnp.float32) + bias.astype(jnp.float32)
    return jnp.maximum(mixed, 0.0).astype(jnp.bfloat16).reshape(N_COL, N_ROW * P_SIZE, F)
```

```python
import functools

import jax
import jax.numpy as jnp
from jax import lax
from jax.experimental import pallas as pl
from jax.experimental.pallas import tpu as pltpu
from jax.sharding import PartitionSpec as P

TILE = 64
LANES = 128
SUB = 8


def densify_kernel(
    tiles_per_chunk, src_tiles, counts_ref, rows_ref, cols_ref, values_ref, out_ref, pick_ref
):
    chunks = out_ref.shape[0]
    pairs = out_ref.shape[1]
    cells, slots = pick_ref.shape

    @pl.when(pl.program_id(1) == 0)
    def build():
        target = rows_ref[...]
        chunk = target // tiles_per_chunk
        local = target - chunk * tiles_per_chunk
        cell = (chunk * src_tiles + cols_ref[...]) * tiles_per_chunk + local
        slot = lax.broadcasted_iota(jnp.int32, (1, slots), 1)
        cell = jnp.where(slot < counts_ref[0], cell, -1) - pl.program_id(0) * cells
        index = lax.broadcasted_iota(jnp.int32, (cells, slots), 0)
        pick_ref[...] = jnp.where(index == cell, 1.0, 0.0).astype(pick_ref.dtype)

    summed = jnp.dot(pick_ref[...], values_ref[...], preferred_element_type=jnp.float32)
    per_chunk = cells // chunks
    low = lax.broadcasted_iota(jnp.int32, (src_tiles // 2, SUB, LANES), 2) < TILE
    for pair in range(pairs):
        for chunk in range(chunks):
            block = summed[
                chunk * per_chunk : (chunk + 1) * per_chunk, pair * LANES : (pair + 1) * LANES
            ].reshape(src_tiles // 2, 2, SUB, LANES)
            left, right = block[:, 0], block[:, 1]
            even = jnp.where(low, left, pltpu.roll(right, TILE, 2))
            odd = jnp.where(low, pltpu.roll(left, TILE, 2), right)
            both = jnp.concatenate([even, odd], axis=1).astype(out_ref.dtype)
            for k in range(src_tiles // 2):
                out_ref[chunk, pair, :, k * LANES : (k + 1) * LANES] = both[k]


def densify(values, tile_row, tile_col, counts, chunks, tiles_per_chunk, src_tiles):
    slots, width = values.shape
    pairs = width // LANES
    pair_block = 4
    group = max(1, min(chunks, 1024 // (tiles_per_chunk * src_tiles)))
    cells = group * tiles_per_chunk * src_tiles
    return pl.pallas_call(
        functools.partial(densify_kernel, tiles_per_chunk, src_tiles),
        grid=(chunks // group, pairs // pair_block),
        in_specs=[
            pl.BlockSpec(memory_space=pltpu.SMEM),
            pl.BlockSpec((1, slots), lambda g, p: (0, 0)),
            pl.BlockSpec((1, slots), lambda g, p: (0, 0)),
            pl.BlockSpec((slots, pair_block * LANES), lambda g, p: (0, p)),
        ],
        out_specs=pl.BlockSpec(
            (group, pair_block, 2 * SUB, src_tiles * TILE), lambda g, p: (g, p, 0, 0)
        ),
        out_shape=jax.ShapeDtypeStruct(
            (chunks, pairs, 2 * SUB, src_tiles * TILE), jnp.bfloat16
        ),
        scratch_shapes=[pltpu.VMEM((cells, slots), jnp.bfloat16)],
        compiler_params=pltpu.CompilerParams(vmem_limit_bytes=48 * 1024 * 1024),
        cost_estimate=pl.CostEstimate(
            flops=2 * chunks * tiles_per_chunk * src_tiles * slots * width,
            bytes_accessed=2 * slots * width * 2,
            transcendentals=0,
        ),
        name="densify",
    )(counts, tile_row, tile_col, values)


def on_device(features, tile_values, tile_rows, tile_cols, counts, weight, bias):
    piece_rows = features.shape[1]
    feat_width = features.shape[2]
    chunks = lax.axis_size("row")
    tiles_per_chunk = piece_rows // TILE
    src_tiles = lax.axis_size("col") * tiles_per_chunk
    slots = tile_values.shape[2]
    gathered = lax.all_gather(features, "col", axis=1, tiled=True)[0]
    dense = densify(
        tile_values.reshape(slots, TILE * TILE),
        tile_rows.reshape(1, slots),
        tile_cols.reshape(1, slots),
        counts.reshape(1),
        chunks,
        tiles_per_chunk,
        src_tiles,
    ).reshape(chunks * piece_rows, src_tiles * TILE)
    partial_value = jnp.dot(dense, gathered, preferred_element_type=jnp.float32)
    own_rows = lax.psum_scatter(
        partial_value.astype(jnp.bfloat16), "row", scatter_dimension=0, tiled=True
    )
    hidden = own_rows.astype(jnp.bfloat16)
    mixed = jnp.dot(hidden, weight, preferred_element_type=jnp.float32) + bias
    out = jnp.maximum(mixed, 0.0).astype(jnp.bfloat16)
    out = out.reshape(TILE, tiles_per_chunk, feat_width).transpose(1, 0, 2)
    return out.reshape(1, piece_rows, feat_width)


def solution(mesh):
    in_specs = (
        P(("groups", "row"), "col", None),
        P(("groups", "row"), "col", None, None),
        P(("groups", "row"), "col", None),
        P(("groups", "row"), "col", None),
        P(("groups", "row"), "col"),
        P(),
        P(),
    )
    out_specs = P(("groups", "col"), "row", None)
    return jax.shard_map(
        on_device, mesh=mesh, in_specs=in_specs, out_specs=out_specs, check_vma=False
    )
```

```python
import functools

import jax
import jax.numpy as jnp
from jax import lax
from jax.experimental import pallas as pl
from jax.experimental.pallas import tpu as pltpu
from jax.sharding import PartitionSpec as P

TILE = 64
LANES = 128
SUB = 8
PAIR_BLOCK = 4
VMEM_LIMIT = 48 * 1024 * 1024


def cell_ids(where_ref, rows, cols, first, rows_axis, cols_axis, chunk_tiles):
    live, z, me = where_ref[0], where_ref[1], where_ref[2]
    chunk = rows // chunk_tiles
    local = rows - chunk * chunk_tiles
    gap = jnp.abs(chunk - z)
    order = jnp.maximum(z - gap, 0) + jnp.maximum(rows_axis - 1 - z - gap, 0)
    order = order + jnp.where((chunk < z) & (gap <= rows_axis - 1 - z), 1, 0)
    block = cols // chunk_tiles
    col_local = cols - block * chunk_tiles
    hop = me // 2 - block // 2
    hop = jnp.where(hop < 0, hop + cols_axis // 2, hop)
    near = 2 * hop + jnp.abs(block % 2 - me % 2)
    source = near * chunk_tiles + col_local
    cell = ((order - first) * (cols_axis * chunk_tiles) + source) * chunk_tiles + local
    slot = lax.broadcasted_iota(jnp.int32, rows.shape, 1)
    return jnp.where(slot < live, cell, -1)


def densify_step(axes, first, where_ref, rows_ref, cols_ref, values_ref, pick_ref, store):
    rows_axis, cols_axis, chunk_tiles, chunks = axes
    cells, slots = pick_ref.shape

    @pl.when(pl.program_id(0) == 0)
    def build():
        cell = cell_ids(
            where_ref, rows_ref[...], cols_ref[...], first, rows_axis, cols_axis, chunk_tiles
        )
        index = lax.broadcasted_iota(jnp.int32, (cells, slots), 0)
        pick_ref[...] = jnp.where(index == cell, 1.0, 0.0).astype(pick_ref.dtype)

    summed = jnp.dot(pick_ref[...], values_ref[...], preferred_element_type=jnp.float32)
    per_chunk = cells // chunks
    halves = per_chunk // (2 * SUB)
    low = lax.broadcasted_iota(jnp.int32, (halves, SUB, LANES), 2) < TILE
    for pair in range(PAIR_BLOCK):
        for chunk in range(chunks):
            block = summed[
                chunk * per_chunk : (chunk + 1) * per_chunk, pair * LANES : (pair + 1) * LANES
            ].reshape(halves, 2, SUB, LANES)
            left, right = block[:, 0], block[:, 1]
            even = jnp.where(low, left, pltpu.roll(right, TILE, 2))
            odd = jnp.where(low, pltpu.roll(left, TILE, 2), right)
            both = jnp.concatenate([even, odd], axis=1).astype(jnp.bfloat16)
            for k in range(halves):
                store(chunk, pair, k, both[k])


def densify_kernel(axes, first, where_ref, rows_ref, cols_ref, values_ref, out_ref, pick_ref):
    def store(chunk, pair, k, part):
        out_ref[chunk, pair, :, k * LANES : (k + 1) * LANES] = part

    densify_step(axes, first, where_ref, rows_ref, cols_ref, values_ref, pick_ref, store)


def densify_apply_kernel(axes, first, where_ref, rows_ref, cols_ref, values_ref, *rest):
    blocks, (out_ref, pick_ref, dense_ref) = rest[:-3], rest[-3:]
    step = pl.program_id(0)

    def store(chunk, pair, k, part):
        dense_ref[step * PAIR_BLOCK + pair, :, k * LANES : (k + 1) * LANES] = part

    densify_step(axes, first, where_ref, rows_ref, cols_ref, values_ref, pick_ref, store)

    @pl.when(step == pl.num_programs(0) - 1)
    def apply():
        apply_blocks(dense_ref[...].reshape(out_ref.shape[0], -1), blocks, out_ref)


def apply_blocks(dense, blocks, out_ref):
    total = None
    depth = blocks[0].shape[0]
    for k, block in enumerate(blocks):
        part = jnp.dot(
            dense[:, k * depth : (k + 1) * depth], block[...], preferred_element_type=jnp.float32
        )
        total = part if total is None else total + part
    out_ref[...] = total


def apply_kernel(dense_ref, *rest):
    apply_blocks(dense_ref[0], rest[:-1], rest[-1])


def params():
    return pltpu.CompilerParams(vmem_limit_bytes=VMEM_LIMIT)


def densify(axes, first, where, tile_row, tile_col, values, blocks=None):
    rows_axis, cols_axis, chunk_tiles, chunks = axes
    slots, width = values.shape
    pairs = width // LANES
    source_rows = cols_axis * chunk_tiles * TILE
    cells = chunks * chunk_tiles * cols_axis * chunk_tiles
    piece = chunk_tiles * TILE
    in_specs = [
        pl.BlockSpec(memory_space=pltpu.SMEM),
        pl.BlockSpec((1, slots), lambda p: (0, 0)),
        pl.BlockSpec((1, slots), lambda p: (0, 0)),
        pl.BlockSpec((slots, PAIR_BLOCK * LANES), lambda p: (0, p)),
    ]
    pick = pltpu.VMEM((cells, slots), jnp.bfloat16)
    flops = 2 * cells * slots * width
    if blocks is None:
        return pl.pallas_call(
            functools.partial(densify_kernel, axes, first),
            grid=(pairs // PAIR_BLOCK,),
            in_specs=in_specs,
            out_specs=pl.BlockSpec(
                (chunks, PAIR_BLOCK, 2 * SUB, source_rows), lambda p: (0, p, 0, 0)
            ),
            out_shape=jax.ShapeDtypeStruct((chunks, pairs, 2 * SUB, source_rows), jnp.bfloat16),
            scratch_shapes=[pick],
            compiler_params=params(),
            cost_estimate=pl.CostEstimate(
                flops=2 * flops, bytes_accessed=4 * slots * width, transcendentals=0
            ),
            name="densify",
        )(where, tile_row, tile_col, values).reshape(chunks, piece, source_rows)
    feat_width = blocks[0].shape[1]
    return pl.pallas_call(
        functools.partial(densify_apply_kernel, axes, first),
        grid=(pairs // PAIR_BLOCK,),
        in_specs=in_specs
        + [pl.BlockSpec(block.shape, lambda p: (0, 0)) for block in blocks],
        out_specs=pl.BlockSpec((piece, feat_width), lambda p: (0, 0)),
        out_shape=jax.ShapeDtypeStruct((piece, feat_width), jnp.float32),
        scratch_shapes=[pick, pltpu.VMEM((pairs, 2 * SUB, source_rows), jnp.bfloat16)],
        compiler_params=params(),
        cost_estimate=pl.CostEstimate(
            flops=2 * flops, bytes_accessed=4 * slots * width, transcendentals=0
        ),
        name="densify_apply",
    )(where, tile_row, tile_col, values, *blocks)


def apply(dense, position, blocks):
    unused, piece, source_rows = dense.shape
    feat_width = blocks[0].shape[1]
    return pl.pallas_call(
        apply_kernel,
        grid=(1,),
        in_specs=[pl.BlockSpec((1, piece, source_rows), lambda p: (position, 0, 0))]
        + [pl.BlockSpec(block.shape, lambda p: (0, 0)) for block in blocks],
        out_specs=pl.BlockSpec((piece, feat_width), lambda p: (0, 0)),
        out_shape=jax.ShapeDtypeStruct((piece, feat_width), jnp.float32),
        compiler_params=params(),
        cost_estimate=pl.CostEstimate(
            flops=4 * piece * source_rows * feat_width,
            bytes_accessed=2 * piece * source_rows,
            transcendentals=0,
        ),
        name="apply",
    )(dense, *blocks)


def gather_blocks(features, cols_axis, after):
    swap = [(k, k ^ 1) for k in range(cols_axis)]
    shift = [(k, (k + 2) % cols_axis) for k in range(cols_axis)]
    held = [features]
    for hop in range(1, cols_axis // 2):
        held.append(lax.ppermute(held[-1], "col", shift))
    blocks = [features, lax.ppermute(features, "col", swap)]
    for block in held[1:]:
        block, after = lax.optimization_barrier((block, after))
        blocks += [block, lax.ppermute(block, "col", swap)]
    return blocks, after


def finish_kernel(chunk_tiles, own_ref, right_ref, left_ref, weight_ref, bias_ref, out_ref):
    total = own_ref[...] + right_ref[...].astype(jnp.float32) + left_ref[...].astype(jnp.float32)
    hidden = total.astype(jnp.bfloat16)
    mixed = jnp.dot(hidden, weight_ref[...], preferred_element_type=jnp.float32) + bias_ref[...]
    mixed = jnp.maximum(mixed, 0.0)
    mixed = mixed.reshape(TILE, chunk_tiles, mixed.shape[1])
    for k in range(chunk_tiles):
        out_ref[k * TILE : (k + 1) * TILE, :] = mixed[:, k, :].astype(jnp.bfloat16)


def finish(own, from_right, from_left, weight, bias, chunk_tiles):
    return pl.pallas_call(
        functools.partial(finish_kernel, chunk_tiles),
        out_shape=jax.ShapeDtypeStruct(own.shape, jnp.bfloat16),
        in_specs=[pl.BlockSpec(memory_space=pltpu.VMEM)] * 5,
        out_specs=pl.BlockSpec(memory_space=pltpu.VMEM),
        compiler_params=params(),
        name="finish",
    )(own, from_right, from_left, weight, bias)


def on_device(features, tile_values, tile_rows, tile_cols, counts, weight, bias):
    piece, feat_width = features.shape[1:]
    rows_axis, cols_axis = lax.axis_size("row"), lax.axis_size("col")
    chunk_tiles = piece // TILE
    slots = tile_values.shape[2]
    z, me = lax.axis_index("row"), lax.axis_index("col")
    where = jnp.stack([counts.reshape(()), z, me])
    values = tile_values.reshape(slots, TILE * TILE)
    tile_row = tile_rows.reshape(1, slots)
    tile_col = tile_cols.reshape(1, slots)
    head = 1
    axes = (rows_axis, cols_axis, chunk_tiles)
    dense = densify(axes + (head,), 0, where, tile_row, tile_col, values)
    blocks, dense = gather_blocks(features.reshape(piece, feat_width), cols_axis, dense)
    partial_values = {}

    def partial_of(position):
        if position not in partial_values:
            if position < head:
                partial_values[position] = apply(dense, position, blocks)
            else:
                partial_values[position] = densify(
                    axes + (1,), position, where, tile_row, tile_col, values, blocks
                )
        return partial_values[position]

    from_left = from_right = None
    for step in range(rows_axis - 1):
        gap = rows_axis - 1 - step
        ahead = jnp.maximum(z - gap, 0) + jnp.maximum(rows_axis - 1 - z - gap, 0)
        behind = ahead + jnp.where(gap <= rows_axis - 1 - z, 1, 0)
        places = range(rows_axis)
        up = sorted({max(d - gap, 0) + max(rows_axis - 1 - d - gap, 0) for d in places if d <= step})
        down = sorted(
            {
                max(d - gap, 0) + max(rows_axis - 1 - d - gap, 0) + (gap <= rows_axis - 1 - d)
                for d in places
                if d >= gap
            }
        )

        def choose(position, options):
            value = partial_of(options[0])
            for option in options[1:]:
                value = jnp.where(position == option, partial_of(option), value)
            return value

        to_up, to_down = choose(ahead, up), choose(behind, down)
        if step:
            to_up = to_up + from_left.astype(jnp.float32)
            to_down = to_down + from_right.astype(jnp.float32)
        from_left = lax.ppermute(
            to_up.astype(jnp.bfloat16), "row", [(d, d + 1) for d in range(rows_axis - 1) if d <= step]
        )
        from_right = lax.ppermute(
            to_down.astype(jnp.bfloat16), "row", [(d, d - 1) for d in range(1, rows_axis) if d >= gap]
        )
    own = partial_of(rows_axis - 1)
    out = finish(own, from_right, from_left, weight, bias.reshape(1, feat_width), chunk_tiles)
    return out.reshape(1, piece, feat_width)


def solution(mesh):
    in_specs = (
        P(("groups", "row"), "col", None),
        P(("groups", "row"), "col", None, None),
        P(("groups", "row"), "col", None),
        P(("groups", "row"), "col", None),
        P(("groups", "row"), "col"),
        P(),
        P(),
    )
    out_specs = P(("groups", "col"), "row", None)
    return jax.shard_map(
        on_device, mesh=mesh, in_specs=in_specs, out_specs=out_specs, check_vma=False
    )
```

```python
import functools

import jax
import jax.numpy as jnp
from jax import lax
from jax.experimental import pallas as pl
from jax.experimental.pallas import tpu as pltpu
from jax.sharding import PartitionSpec as P

TILE = 64
LANES = 128
SUB = 8
STREAMS = 2
VMEM_LIMIT = 24 * 1024 * 1024


def cell_ids(where_ref, rows, cols, first, rows_axis, cols_axis, chunk_tiles):
    live, z, me = where_ref[0], where_ref[1], where_ref[2]
    chunk = rows // chunk_tiles
    local = rows - chunk * chunk_tiles
    order = chunk - z - 1
    order = jnp.where(order < 0, order + rows_axis, order)
    block = cols // chunk_tiles
    col_local = cols - block * chunk_tiles
    hop = me // 2 - block // 2
    hop = jnp.where(hop < 0, hop + cols_axis // 2, hop)
    near = 2 * hop + jnp.abs(block % 2 - me % 2)
    source = near * chunk_tiles + col_local
    cell = ((order - first) * (cols_axis * chunk_tiles) + source) * chunk_tiles + local
    slot = lax.broadcasted_iota(jnp.int32, rows.shape, 1)
    return jnp.where(slot < live, cell, -1)


def densify_step(axes, first, where_ref, rows_ref, cols_ref, value_refs, pick_ref, store):
    rows_axis, cols_axis, chunk_tiles, chunks = axes
    cells, slots = pick_ref.shape

    @pl.when(pl.program_id(0) == 0)
    def build():
        cell = cell_ids(
            where_ref, rows_ref[...], cols_ref[...], first, rows_axis, cols_axis, chunk_tiles
        )
        index = lax.broadcasted_iota(jnp.int32, (cells, slots), 0)
        pick_ref[...] = jnp.where(index == cell, 1.0, 0.0).astype(pick_ref.dtype)

    part_cells = 256
    halves = part_cells // (2 * SUB)
    parts_per_chunk = cells // chunks // part_cells
    low = lax.broadcasted_iota(jnp.int32, (halves, SUB, LANES), 2) < TILE
    for operand, values_ref in enumerate(value_refs):
        for part in range(cells // part_cells):
            summed = jnp.dot(
                pick_ref[part * part_cells : (part + 1) * part_cells, :],
                values_ref[...],
                preferred_element_type=jnp.float32,
            )
            for pair in range(2):
                block = summed[:, pair * LANES : (pair + 1) * LANES]
                block = block.reshape(halves, 2, SUB, LANES)
                left, right = block[:, 0], block[:, 1]
                even = jnp.where(low, left, pltpu.roll(right, TILE, 2))
                odd = jnp.where(low, pltpu.roll(left, TILE, 2), right)
                both = jnp.concatenate([even, odd], axis=1).astype(jnp.bfloat16)
                chunk, column = part // parts_per_chunk, part % parts_per_chunk * halves
                for k in range(halves):
                    store(chunk, 2 * operand + pair, column + k, both[k])


def densify_kernel(axes, first, where_ref, rows_ref, cols_ref, *rest):
    value_refs, (out_ref, pick_ref) = rest[:-2], rest[-2:]

    def store(chunk, pair, k, part):
        out_ref[chunk, pair, :, k * LANES : (k + 1) * LANES] = part

    densify_step(axes, first, where_ref, rows_ref, cols_ref, value_refs, pick_ref, store)


def densify_apply_kernel(axes, first, where_ref, rows_ref, cols_ref, *rest):
    value_refs = rest[:STREAMS]
    blocks, (out_ref, pick_ref, dense_ref) = rest[STREAMS:-3], rest[-3:]
    step = pl.program_id(0)

    def store(chunk, pair, k, part):
        dense_ref[step * 2 * STREAMS + pair, :, k * LANES : (k + 1) * LANES] = part

    densify_step(axes, first, where_ref, rows_ref, cols_ref, value_refs, pick_ref, store)

    @pl.when(step == pl.num_programs(0) - 1)
    def apply():
        out_ref[...] = apply_blocks(dense_ref[...].reshape(out_ref.shape[0], -1), blocks)


def apply_blocks(dense, blocks):
    total = None
    depth = blocks[0].shape[0]
    for k, block in enumerate(blocks):
        part = jnp.dot(
            dense[:, k * depth : (k + 1) * depth], block[...], preferred_element_type=jnp.float32
        )
        total = part if total is None else total + part
    return total


def apply_kernel(parts, *refs):
    out_ref = refs[-1]
    rows = out_ref.shape[0] // parts
    for k in range(parts):
        total = apply_blocks(refs[k][0].reshape(rows, -1), refs[parts:-1])
        out_ref[k * rows : (k + 1) * rows, :] = total.astype(out_ref.dtype)


def params():
    return pltpu.CompilerParams(vmem_limit_bytes=VMEM_LIMIT)


def densify(axes, first, lanes, where, tile_row, tile_col, values, blocks=None):
    rows_axis, cols_axis, chunk_tiles, chunks = axes
    slots = values.shape[0]
    pairs = (lanes[1] - lanes[0]) // LANES
    offset = lanes[0] // (2 * LANES)
    source_rows = cols_axis * chunk_tiles * TILE
    cells = chunks * chunk_tiles * cols_axis * chunk_tiles
    piece = chunk_tiles * TILE
    in_specs = [
        pl.BlockSpec(memory_space=pltpu.SMEM),
        pl.BlockSpec((1, slots), lambda p: (0, 0)),
        pl.BlockSpec((1, slots), lambda p: (0, 0)),
    ] + [
        pl.BlockSpec((slots, 2 * LANES), lambda p, k=k: (0, offset + p * STREAMS + k))
        for k in range(STREAMS)
    ]
    operands = (where, tile_row, tile_col) + (values,) * STREAMS
    pick = pltpu.VMEM((cells, slots), jnp.bfloat16)
    cost = pl.CostEstimate(
        flops=4 * cells * slots * pairs * LANES,
        bytes_accessed=4 * slots * pairs * LANES,
        transcendentals=0,
    )
    grid = (pairs // (2 * STREAMS),)
    if blocks is None:
        return pl.pallas_call(
            functools.partial(densify_kernel, axes, first),
            grid=grid,
            in_specs=in_specs,
            out_specs=pl.BlockSpec(
                (chunks, 2 * STREAMS, 2 * SUB, source_rows), lambda p: (0, p, 0, 0)
            ),
            out_shape=jax.ShapeDtypeStruct((chunks, pairs, 2 * SUB, source_rows), jnp.bfloat16),
            scratch_shapes=[pick],
            compiler_params=params(),
            cost_estimate=cost,
            name="densify",
        )(*operands)
    feat_width = blocks[0].shape[1]
    return pl.pallas_call(
        functools.partial(densify_apply_kernel, axes, first),
        grid=grid,
        in_specs=in_specs
        + [pl.BlockSpec(block.shape, lambda p: (0, 0)) for block in blocks],
        out_specs=pl.BlockSpec((piece, feat_width), lambda p: (0, 0)),
        out_shape=jax.ShapeDtypeStruct((piece, feat_width), jnp.float32),
        scratch_shapes=[pick, pltpu.VMEM((pairs, 2 * SUB, source_rows), jnp.bfloat16)],
        compiler_params=params(),
        cost_estimate=cost,
        name="densify_apply",
    )(*operands, *blocks)


def apply(dense, position, blocks):
    source_rows = dense[0].shape[3]
    piece = len(dense) * dense[0].shape[1] * dense[0].shape[2]
    feat_width = blocks[0].shape[1]
    return pl.pallas_call(
        functools.partial(apply_kernel, len(dense)),
        grid=(1,),
        in_specs=[
            pl.BlockSpec((1,) + part.shape[1:], lambda p: (position, 0, 0, 0)) for part in dense
        ]
        + [pl.BlockSpec(block.shape, lambda p: (0, 0)) for block in blocks],
        out_specs=pl.BlockSpec((piece, feat_width), lambda p: (0, 0)),
        out_shape=jax.ShapeDtypeStruct((piece, feat_width), jnp.bfloat16),
        compiler_params=params(),
        cost_estimate=pl.CostEstimate(
            flops=4 * piece * source_rows * feat_width,
            bytes_accessed=2 * piece * source_rows,
            transcendentals=0,
        ),
        name="apply",
    )(*dense, *blocks)


def gather_blocks(features, cols_axis, first):
    swap = [(k, k ^ 1) for k in range(cols_axis)]
    shift = [(k, (k + 2) % cols_axis) for k in range(cols_axis)]
    held = [features]
    for hop in range(1, cols_axis // 2):
        held.append(lax.ppermute(held[-1], "col", shift))
    blocks = [features, lax.ppermute(features, "col", swap)]
    for block in held[1:]:
        block, first = lax.optimization_barrier((block, first))
        blocks += [block, lax.ppermute(block, "col", swap)]
    return blocks, first


def finish_kernel(chunk_tiles, own_ref, *refs):
    weight_ref, bias_ref, out_ref = refs[-3:]
    total = own_ref[...]
    for ref in refs[:-3]:
        total = total + ref[...].astype(jnp.float32)
    hidden = total.astype(jnp.bfloat16)
    mixed = jnp.dot(hidden, weight_ref[...], preferred_element_type=jnp.float32) + bias_ref[...]
    mixed = jnp.maximum(mixed, 0.0)
    mixed = mixed.reshape(TILE, chunk_tiles, mixed.shape[1])
    for k in range(chunk_tiles):
        out_ref[k * TILE : (k + 1) * TILE, :] = mixed[:, k, :].astype(jnp.bfloat16)


def finish(own, received, weight, bias, chunk_tiles):
    return pl.pallas_call(
        functools.partial(finish_kernel, chunk_tiles),
        out_shape=jax.ShapeDtypeStruct(own.shape, jnp.bfloat16),
        in_specs=[pl.BlockSpec(memory_space=pltpu.VMEM)] * (3 + len(received)),
        out_specs=pl.BlockSpec(memory_space=pltpu.VMEM),
        compiler_params=params(),
        name="finish",
    )(own, *received, weight, bias)


def on_device(features, tile_values, tile_rows, tile_cols, counts, weight, bias):
    piece, feat_width = features.shape[1:]
    rows_axis, cols_axis = lax.axis_size("row"), lax.axis_size("col")
    chunk_tiles = piece // TILE
    slots = tile_values.shape[2]
    z, me = lax.axis_index("row"), lax.axis_index("col")
    where = jnp.stack([counts.reshape(()), z, me])
    width = TILE * TILE
    tiles = (where, tile_rows.reshape(1, slots), tile_cols.reshape(1, slots))
    tiles += (tile_values.reshape(slots, width),)
    axes = (rows_axis, cols_axis, chunk_tiles)

    group = min(3, rows_axis - 1)
    first = densify(axes + (group,), 0, (0, width // 2), *tiles)
    blocks, first = gather_blocks(features.reshape(piece, feat_width), cols_axis, first)
    received = []
    for position in range(rows_axis - 1):
        if position % group == 0:
            chunks = min(group, rows_axis - 1 - position)
            if position:
                first = densify(axes + (chunks,), position, (0, width // 2), *tiles)
            second = densify(axes + (chunks,), position, (width // 2, width), *tiles)
        part = apply((first, second), position % group, blocks)
        shift = position + 1
        to = [(d, (d + shift) % rows_axis) for d in range(rows_axis)]
        received.append(lax.ppermute(part, "row", to))
    own = densify(axes + (1,), rows_axis - 1, (0, width), *tiles, blocks)
    out = finish(own, received, weight, bias.reshape(1, feat_width), chunk_tiles)
    return out.reshape(1, piece, feat_width)


def solution(mesh):
    in_specs = (
        P(("groups", "row"), "col", None),
        P(("groups", "row"), "col", None, None),
        P(("groups", "row"), "col", None),
        P(("groups", "row"), "col", None),
        P(("groups", "row"), "col"),
        P(),
        P(),
    )
    out_specs = P(("groups", "col"), "row", None)
    return jax.shard_map(
        on_device, mesh=mesh, in_specs=in_specs, out_specs=out_specs, check_vma=False
    )
```

```python
import functools

import jax
import jax.numpy as jnp
from jax import lax
from jax.experimental import pallas as pl
from jax.experimental.pallas import tpu as pltpu
from jax.sharding import PartitionSpec as P

TILE = 64
LANES = 128
SUB = 8
VMEM_LIMIT = 44 * 1024 * 1024


def send_order(chunk, z, rows_axis):
    if rows_axis == 4:
        return 3 - (chunk ^ z)
    order = chunk - z - 1
    return jnp.where(order < 0, order + rows_axis, order)


def cell_ids(counts, rows, cols, z, me, rows_axis, cols_axis, chunk_tiles):
    chunk = rows // chunk_tiles
    local = rows - chunk * chunk_tiles
    order = send_order(chunk, z, rows_axis)
    block = cols // chunk_tiles
    col_local = cols - block * chunk_tiles
    hop = me // 2 - block // 2
    hop = jnp.where(hop < 0, hop + cols_axis // 2, hop)
    near = 2 * hop + jnp.abs(block % 2 - me % 2)
    cell = ((order * cols_axis + near) * chunk_tiles + col_local) * chunk_tiles + local
    slot = lax.broadcasted_iota(jnp.int32, rows.shape, 1)
    return jnp.where(slot < counts, cell, -1)


def densify_lanes(axes, first, lane, refs, scratch, dense_ref):
    cols_axis, chunk_tiles, chunks = axes
    cell_ref, values_hbm = refs
    values_ref, pick_ref, value_sems = scratch
    cells, slots = pick_ref.shape
    steps = values_ref.shape[0]

    def value_copy(step):
        return pltpu.make_async_copy(
            values_hbm.at[:, pl.ds(lane + step * 2 * LANES, 2 * LANES)],
            values_ref.at[step],
            value_sems.at[step],
        )

    for step in range(steps):
        value_copy(step).start()
    cell = cell_ref[...] - first * (cells // chunks)
    index = lax.broadcasted_iota(jnp.int32, (cells, slots), 0)
    pick_ref[...] = jnp.where(index == cell, 1.0, 0.0).astype(pick_ref.dtype)

    part_cells = 256
    halves = part_cells // (2 * SUB)
    parts_per_chunk = cells // chunks // part_cells
    low = lax.broadcasted_iota(jnp.int32, (halves, SUB, LANES), 2) < TILE

    def body(step, carry):
        value_copy(step).wait()
        for part in range(cells // part_cells):
            summed = jnp.dot(
                pick_ref[part * part_cells : (part + 1) * part_cells, :],
                values_ref[step],
                preferred_element_type=jnp.float32,
            )
            for pair in range(2):
                block = summed[:, pair * LANES : (pair + 1) * LANES]
                block = block.reshape(halves, 2, SUB, LANES)
                left, right = block[:, 0], block[:, 1]
                even = jnp.where(low, left, pltpu.roll(right, TILE, 2))
                odd = jnp.where(low, pltpu.roll(left, TILE, 2), right)
                both = jnp.concatenate([even, odd], axis=1).astype(jnp.bfloat16)
                chunk, column = part // parts_per_chunk, part % parts_per_chunk * halves
                for k in range(halves):
                    lanes = pl.ds((column + k) * LANES, LANES)
                    dense_ref[chunk, 2 * step + pair, :, lanes] = both[k]
        return carry

    lax.fori_loop(0, steps, body, 0)


def densify_kernel(axes, first, lane, *refs):
    densify_lanes(axes, first, lane, refs[:2], refs[3:], refs[2])


def densify_apply_kernel(axes, first, lane, *refs):
    out_ref, dense_ref = refs[-5:-3]
    densify_lanes(axes, first, lane, refs[:2], refs[-3:], dense_ref)
    out_ref[...] = apply_blocks(dense_ref[0].reshape(out_ref.shape[0], -1), refs[2:-5])


def apply_blocks(dense, blocks):
    total = None
    depth = blocks[0].shape[0]
    for k, block in enumerate(blocks):
        part = jnp.dot(
            dense[:, k * depth : (k + 1) * depth], block[...], preferred_element_type=jnp.float32
        )
        total = part if total is None else total + part
    return total


def apply_kernel(parts, position, *refs):
    out_ref = refs[-1]
    rows = out_ref.shape[0] // parts
    for k in range(parts):
        total = apply_blocks(refs[k][position].reshape(rows, -1), refs[parts:-1])
        out_ref[k * rows : (k + 1) * rows, :] = total.astype(out_ref.dtype)


def params():
    return pltpu.CompilerParams(vmem_limit_bytes=VMEM_LIMIT)


IN_VMEM = pl.BlockSpec(memory_space=pltpu.VMEM)
IN_HBM = pl.BlockSpec(memory_space=pltpu.HBM)


def densify(axes, first, lanes, cell, values, blocks=None):
    cols_axis, chunk_tiles, chunks = axes
    slots = values.shape[0]
    width = lanes[1] - lanes[0]
    pairs = width // LANES
    steps = pairs // 2
    source_rows = cols_axis * chunk_tiles * TILE
    cells = chunks * chunk_tiles * cols_axis * chunk_tiles
    piece = chunk_tiles * TILE
    dense_shape = (chunks, pairs, 2 * SUB, source_rows)
    in_specs = [IN_VMEM, IN_HBM]
    scratch = [
        pltpu.VMEM((steps, slots, 2 * LANES), jnp.bfloat16),
        pltpu.VMEM((cells, slots), jnp.bfloat16),
        pltpu.SemaphoreType.DMA((steps,)),
    ]
    cost = pl.CostEstimate(
        flops=4 * cells * slots * width, bytes_accessed=4 * slots * width, transcendentals=0
    )
    operands = (cell, values)
    if blocks is None:
        return pl.pallas_call(
            functools.partial(densify_kernel, axes, first, lanes[0]),
            in_specs=in_specs,
            out_specs=IN_VMEM,
            out_shape=jax.ShapeDtypeStruct(dense_shape, jnp.bfloat16),
            scratch_shapes=scratch,
            compiler_params=params(),
            cost_estimate=cost,
            name="densify",
        )(*operands)
    return pl.pallas_call(
        functools.partial(densify_apply_kernel, axes, first, lanes[0]),
        in_specs=in_specs + [IN_VMEM] * len(blocks),
        out_specs=IN_VMEM,
        out_shape=jax.ShapeDtypeStruct((piece, blocks[0].shape[1]), jnp.float32),
        scratch_shapes=[pltpu.VMEM(dense_shape, jnp.bfloat16)] + scratch,
        compiler_params=params(),
        cost_estimate=cost,
        name="densify_apply",
    )(*operands, *blocks)


def apply(dense, position, blocks):
    source_rows = dense[0].shape[3]
    piece = len(dense) * dense[0].shape[1] * dense[0].shape[2]
    feat_width = blocks[0].shape[1]
    return pl.pallas_call(
        functools.partial(apply_kernel, len(dense), position),
        in_specs=[IN_VMEM] * (len(dense) + len(blocks)),
        out_specs=IN_VMEM,
        out_shape=jax.ShapeDtypeStruct((piece, feat_width), jnp.bfloat16),
        compiler_params=params(),
        cost_estimate=pl.CostEstimate(
            flops=4 * piece * source_rows * feat_width,
            bytes_accessed=2 * piece * source_rows,
            transcendentals=0,
        ),
        name="apply",
    )(*dense, *blocks)


def gather_blocks(features, cols_axis, first):
    swap = [(k, k ^ 1) for k in range(cols_axis)]
    shift = [(k, (k + 2) % cols_axis) for k in range(cols_axis)]
    held = [features]
    for hop in range(1, cols_axis // 2):
        held.append(lax.ppermute(held[-1], "col", shift))
    blocks = [features, lax.ppermute(features, "col", swap)]
    for block in held[1:]:
        block, first = lax.optimization_barrier((block, first))
        blocks += [block, lax.ppermute(block, "col", swap)]
    return blocks, first


def finish_kernel(chunk_tiles, own_ref, *refs):
    weight_ref, bias_ref, out_ref = refs[-3:]
    total = own_ref[...]
    for ref in refs[:-3]:
        total = total + ref[...].astype(jnp.float32)
    hidden = total.astype(jnp.bfloat16)
    mixed = jnp.dot(hidden, weight_ref[...], preferred_element_type=jnp.float32) + bias_ref[...]
    mixed = jnp.maximum(mixed, 0.0)
    mixed = mixed.reshape(TILE, chunk_tiles, mixed.shape[1])
    for k in range(chunk_tiles):
        out_ref[k * TILE : (k + 1) * TILE, :] = mixed[:, k, :].astype(jnp.bfloat16)


def finish(own, received, weight, bias, chunk_tiles):
    return pl.pallas_call(
        functools.partial(finish_kernel, chunk_tiles),
        out_shape=jax.ShapeDtypeStruct(own.shape, jnp.bfloat16),
        in_specs=[pl.BlockSpec(memory_space=pltpu.VMEM)] * (3 + len(received)),
        out_specs=pl.BlockSpec(memory_space=pltpu.VMEM),
        compiler_params=params(),
        name="finish",
    )(own, *received, weight, bias)


def on_device(features, tile_values, tile_rows, tile_cols, counts, weight, bias):
    piece, feat_width = features.shape[1:]
    rows_axis, cols_axis = lax.axis_size("row"), lax.axis_size("col")
    chunk_tiles = piece // TILE
    slots = tile_values.shape[2]
    width = TILE * TILE
    cell = cell_ids(
        counts,
        tile_rows.reshape(1, slots),
        tile_cols.reshape(1, slots),
        lax.axis_index("row"),
        lax.axis_index("col"),
        rows_axis,
        cols_axis,
        chunk_tiles,
    )
    tiles = (cell, tile_values.reshape(slots, width))
    axes = (cols_axis, chunk_tiles)

    group = min(3, rows_axis - 1)
    first = densify(axes + (group,), 0, (0, width // 2), *tiles)
    blocks, first = gather_blocks(features.reshape(piece, feat_width), cols_axis, first)
    parts = []
    received = []
    for position in range(rows_axis - 1):
        if position % group == 0:
            chunks = min(group, rows_axis - 1 - position)
            if position:
                first = densify(axes + (chunks,), position, (0, width // 2), *tiles)
            second = densify(axes + (chunks,), position, (width // 2, width), *tiles)
        parts.append(apply((first, second), position % group, blocks))
        if rows_axis != 4:
            shift = position + 1
            to = [(d, (d + shift) % rows_axis) for d in range(rows_axis)]
            received.append(lax.ppermute(parts[-1], "row", to))
    if rows_axis == 4:
        passed = lax.ppermute(parts[0], "row", [(0, 1), (3, 2)])
        received.append(lax.ppermute(parts[0], "row", [(1, 2), (2, 1)]))
        received.append(lax.ppermute(parts[1], "row", [(0, 2), (3, 1)]))
        joined = parts[1].astype(jnp.float32) + passed.astype(jnp.float32)
        joined, last = lax.optimization_barrier((joined.astype(jnp.bfloat16), parts[2]))
        received.append(lax.ppermute(joined, "row", [(1, 3), (2, 0)]))
        received.append(lax.ppermute(last, "row", [(0, 1), (1, 0), (2, 3), (3, 2)]))
    own = densify(axes + (1,), rows_axis - 1, (0, width), *tiles, blocks)
    out = finish(own, received, weight, bias.reshape(1, feat_width), chunk_tiles)
    return out.reshape(1, piece, feat_width)


def solution(mesh):
    in_specs = (
        P(("groups", "row"), "col", None),
        P(("groups", "row"), "col", None, None),
        P(("groups", "row"), "col", None),
        P(("groups", "row"), "col", None),
        P(("groups", "row"), "col"),
        P(),
        P(),
    )
    out_specs = P(("groups", "col"), "row", None)
    return jax.shard_map(
        on_device, mesh=mesh, in_specs=in_specs, out_specs=out_specs, check_vma=False
    )
```

```python
import functools

import jax
import jax.numpy as jnp
from jax import lax
from jax.experimental import pallas as pl
from jax.experimental.pallas import tpu as pltpu
from jax.sharding import PartitionSpec as P

TILE = 64
LANES = 128
SUB = 8
VMEM_LIMIT = 44 * 1024 * 1024
OWN_VMEM_LIMIT = 50 * 1024 * 1024


def send_order(chunk, z, rows_axis):
    if rows_axis == 4:
        apart = chunk ^ z
        return jnp.where((z == 0) | (z == 3), 3 - apart, (apart + 3) & 3)
    order = chunk - z - 1
    return jnp.where(order < 0, order + rows_axis, order)


def cell_ids(counts, rows, cols, z, me, rows_axis, cols_axis, chunk_tiles):
    chunk = rows // chunk_tiles
    local = rows - chunk * chunk_tiles
    order = send_order(chunk, z, rows_axis)
    block = cols // chunk_tiles
    col_local = cols - block * chunk_tiles
    hop = me // 2 - block // 2
    hop = jnp.where(hop < 0, hop + cols_axis // 2, hop)
    near = 2 * hop + jnp.abs(block % 2 - me % 2)
    cell = ((order * cols_axis + near) * chunk_tiles + col_local) * chunk_tiles + local
    slot = lax.broadcasted_iota(jnp.int32, rows.shape, 1)
    return jnp.where(slot < counts, cell, -1)


def densify_lanes(axes, first, lane, form, refs, scratch, dense_ref):
    cols_axis, chunk_tiles, chunks = axes
    cell_ref, values_hbm = refs
    values_ref, pick_ref, value_sems = scratch
    cells, slots = pick_ref.shape
    steps = values_ref.shape[0]

    def value_copy(step):
        return pltpu.make_async_copy(
            values_hbm.at[:, pl.ds(lane + step * 2 * LANES, 2 * LANES)],
            values_ref.at[step],
            value_sems.at[step],
        )

    for step in range(steps):
        value_copy(step).start()
    cell = cell_ref[...] - first * (cells // chunks)
    index = lax.broadcasted_iota(jnp.int32, (cells, slots), 0)
    pick_ref[...] = jnp.where(index == cell, 1.0, 0.0).astype(pick_ref.dtype)

    part_cells, unroll = form
    part_cells = min(part_cells, cells)
    per_chunk = cells // chunks
    halves = 256 // (2 * SUB)
    low = lax.broadcasted_iota(jnp.int32, (halves, SUB, LANES), 2) < TILE

    def body(turn, carry):
        for step in [turn * unroll + k for k in range(unroll)]:
            value_copy(step).wait()
            for part in range(0, cells, part_cells):
                summed = jnp.dot(
                    pick_ref[part : part + part_cells, :],
                    values_ref[step],
                    preferred_element_type=jnp.float32,
                )
                for top in range(0, part_cells, 256):
                    chunk, column = divmod(part + top, per_chunk)
                    for pair in range(2):
                        block = summed[top : top + 256, pair * LANES : (pair + 1) * LANES]
                        block = block.reshape(halves, 2, SUB, LANES)
                        left, right = block[:, 0], block[:, 1]
                        even = jnp.where(low, left, pltpu.roll(right, TILE, 2))
                        odd = jnp.where(low, pltpu.roll(left, TILE, 2), right)
                        both = jnp.concatenate([even, odd], axis=1).astype(jnp.bfloat16)
                        for k in range(halves):
                            lanes = pl.ds((column // (2 * SUB) + k) * LANES, LANES)
                            dense_ref[chunk, 2 * step + pair, :, lanes] = both[k]
        return carry

    lax.fori_loop(0, steps // unroll, body, 0)


def densify_kernel(axes, first, lane, form, *refs):
    densify_lanes(axes, first, lane, form, refs[:2], refs[3:], refs[2])


def densify_apply_kernel(axes, first, lane, form, *refs):
    out_ref, dense_ref = refs[-5:-3]
    densify_lanes(axes, first, lane, form, refs[:2], refs[-3:], dense_ref)
    out_ref[...] = apply_blocks(dense_ref[0].reshape(out_ref.shape[0], -1), refs[2:-5])


def apply_blocks(dense, blocks):
    total = None
    depth = blocks[0].shape[0]
    for k, block in enumerate(blocks):
        part = jnp.dot(
            dense[:, k * depth : (k + 1) * depth], block[...], preferred_element_type=jnp.float32
        )
        total = part if total is None else total + part
    return total


def apply_kernel(parts, position, *refs):
    out_ref = refs[-1]
    rows = out_ref.shape[0] // parts
    for k in range(parts):
        total = apply_blocks(refs[k][position].reshape(rows, -1), refs[parts:-1])
        out_ref[k * rows : (k + 1) * rows, :] = total.astype(out_ref.dtype)


def params(limit=VMEM_LIMIT):
    return pltpu.CompilerParams(vmem_limit_bytes=limit)


IN_VMEM = pl.BlockSpec(memory_space=pltpu.VMEM)
IN_HBM = pl.BlockSpec(memory_space=pltpu.HBM)


def densify(axes, first, lanes, form, cell, values, blocks=None):
    cols_axis, chunk_tiles, chunks = axes
    slots = values.shape[0]
    width = lanes[1] - lanes[0]
    pairs = width // LANES
    steps = pairs // 2
    source_rows = cols_axis * chunk_tiles * TILE
    cells = chunks * chunk_tiles * cols_axis * chunk_tiles
    piece = chunk_tiles * TILE
    dense_shape = (chunks, pairs, 2 * SUB, source_rows)
    in_specs = [IN_VMEM, IN_HBM]
    scratch = [
        pltpu.VMEM((steps, slots, 2 * LANES), jnp.bfloat16),
        pltpu.VMEM((cells, slots), jnp.bfloat16),
        pltpu.SemaphoreType.DMA((steps,)),
    ]
    cost = pl.CostEstimate(
        flops=4 * cells * slots * width, bytes_accessed=4 * slots * width, transcendentals=0
    )
    operands = (cell, values)
    if blocks is None:
        return pl.pallas_call(
            functools.partial(densify_kernel, axes, first, lanes[0], form),
            in_specs=in_specs,
            out_specs=IN_VMEM,
            out_shape=jax.ShapeDtypeStruct(dense_shape, jnp.bfloat16),
            scratch_shapes=scratch,
            compiler_params=params(),
            cost_estimate=cost,
            name="densify",
        )(*operands)
    return pl.pallas_call(
        functools.partial(densify_apply_kernel, axes, first, lanes[0], form),
        in_specs=in_specs + [IN_VMEM] * len(blocks),
        out_specs=IN_VMEM,
        out_shape=jax.ShapeDtypeStruct((piece, blocks[0].shape[1]), jnp.float32),
        scratch_shapes=[pltpu.VMEM(dense_shape, jnp.bfloat16)] + scratch,
        compiler_params=params(OWN_VMEM_LIMIT),
        cost_estimate=cost,
        name="densify_apply",
    )(*operands, *blocks)


def apply(dense, position, blocks):
    source_rows = dense[0].shape[3]
    piece = len(dense) * dense[0].shape[1] * dense[0].shape[2]
    feat_width = blocks[0].shape[1]
    return pl.pallas_call(
        functools.partial(apply_kernel, len(dense), position),
        in_specs=[IN_VMEM] * (len(dense) + len(blocks)),
        out_specs=IN_VMEM,
        out_shape=jax.ShapeDtypeStruct((piece, feat_width), jnp.bfloat16),
        compiler_params=params(),
        cost_estimate=pl.CostEstimate(
            flops=4 * piece * source_rows * feat_width,
            bytes_accessed=2 * piece * source_rows,
            transcendentals=0,
        ),
        name="apply",
    )(*dense, *blocks)


def gather_blocks(features, cols_axis, first):
    swap = [(k, k ^ 1) for k in range(cols_axis)]
    shift = [(k, (k + 2) % cols_axis) for k in range(cols_axis)]
    held = [features]
    for hop in range(1, cols_axis // 2):
        held.append(lax.ppermute(held[-1], "col", shift))
    blocks = [features, lax.ppermute(features, "col", swap)]
    for block in held[1:]:
        block, first = lax.optimization_barrier((block, first))
        blocks += [block, lax.ppermute(block, "col", swap)]
    return blocks, first


def finish_kernel(rows_axis, chunk_tiles, own_ref, *refs):
    weight_ref, bias_ref, out_ref = refs[-3:]
    terms = [ref[...].astype(jnp.float32) for ref in refs[:-3]]
    total = own_ref[...]
    if rows_axis == 4:
        z = lax.axis_index("row")
        inner = (z == 1) | (z == 2)
        terms = [terms[0], jnp.where(inner, terms[2] + terms[3], terms[1])]
    for term in terms:
        total = total + term
    hidden = total.astype(jnp.bfloat16)
    mixed = jnp.dot(hidden, weight_ref[...], preferred_element_type=jnp.float32) + bias_ref[...]
    mixed = jnp.maximum(mixed, 0.0)
    mixed = mixed.reshape(TILE, chunk_tiles, mixed.shape[1])
    for k in range(chunk_tiles):
        out_ref[k * TILE : (k + 1) * TILE, :] = mixed[:, k, :].astype(jnp.bfloat16)


def finish(own, received, weight, bias, rows_axis, chunk_tiles):
    return pl.pallas_call(
        functools.partial(finish_kernel, rows_axis, chunk_tiles),
        out_shape=jax.ShapeDtypeStruct(own.shape, jnp.bfloat16),
        in_specs=[pl.BlockSpec(memory_space=pltpu.VMEM)] * (3 + len(received)),
        out_specs=pl.BlockSpec(memory_space=pltpu.VMEM),
        compiler_params=params(),
        name="finish",
    )(own, *received, weight, bias)


def on_device(features, tile_values, tile_rows, tile_cols, counts, weight, bias):
    piece, feat_width = features.shape[1:]
    rows_axis, cols_axis = lax.axis_size("row"), lax.axis_size("col")
    chunk_tiles = piece // TILE
    slots = tile_values.shape[2]
    width = TILE * TILE
    z = lax.axis_index("row")
    cell = cell_ids(
        counts,
        tile_rows.reshape(1, slots),
        tile_cols.reshape(1, slots),
        z,
        lax.axis_index("col"),
        rows_axis,
        cols_axis,
        chunk_tiles,
    )
    tiles = (cell, tile_values.reshape(slots, width))
    axes = (cols_axis, chunk_tiles)

    group = min(3, rows_axis - 1)
    first = densify(axes + (group,), 0, (0, width // 2), (768, 2), *tiles)
    blocks, first = gather_blocks(features.reshape(piece, feat_width), cols_axis, first)
    parts = []
    received = []
    for position in range(rows_axis - 1):
        if position % group == 0:
            chunks = min(group, rows_axis - 1 - position)
            if position:
                first = densify(axes + (chunks,), position, (0, width // 2), (768, 2), *tiles)
            second = densify(axes + (chunks,), position, (width // 2, width), (256, 2), *tiles)
        parts.append(apply((first, second), position % group, blocks))
        if rows_axis != 4:
            shift = position + 1
            to = [(d, (d + shift) % rows_axis) for d in range(rows_axis)]
            received.append(lax.ppermute(parts[-1], "row", to))
    if rows_axis == 4:
        near = [(0, 1), (1, 0), (2, 3), (3, 2)]
        inner = (z == 1) | (z == 2)
        passed = lax.ppermute(parts[0], "row", near)
        crossed = lax.ppermute(parts[2], "row", [(1, 2), (2, 1)])
        joined = parts[1].astype(jnp.float32)
        joined = joined + jnp.where(inner, passed.astype(jnp.float32), 0.0)
        joined, last = lax.optimization_barrier((joined.astype(jnp.bfloat16), parts[2]))
        far = lax.ppermute(joined, "row", [(0, 2), (1, 3), (2, 0), (3, 1)])
        last = lax.ppermute(last, "row", near)
        received = [far, passed, crossed, last]
    own = densify(axes + (1,), rows_axis - 1, (0, width), (256, 4), *tiles, blocks)
    bias = bias.reshape(1, feat_width)
    out = finish(own, received, weight, bias, rows_axis, chunk_tiles)
    return out.reshape(1, piece, feat_width)


def solution(mesh):
    in_specs = (
        P(("groups", "row"), "col", None),
        P(("groups", "row"), "col", None, None),
        P(("groups", "row"), "col", None),
        P(("groups", "row"), "col", None),
        P(("groups", "row"), "col"),
        P(),
        P(),
    )
    out_specs = P(("groups", "col"), "row", None)
    return jax.shard_map(
        on_device, mesh=mesh, in_specs=in_specs, out_specs=out_specs, check_vma=False
    )
```

```python
import functools

import jax
import jax.numpy as jnp
from jax import lax
from jax.experimental import pallas as pl
from jax.experimental.pallas import tpu as pltpu
from jax.sharding import PartitionSpec as P

TILE = 64
LANES = 128
SUB = 8
VMEM_LIMIT = 44 * 1024 * 1024


def send_order(chunk, z, rows_axis):
    if rows_axis == 4:
        apart = chunk ^ z
        return jnp.where((z == 0) | (z == 3), 3 - apart, (apart + 3) & 3)
    order = chunk - z - 1
    return jnp.where(order < 0, order + rows_axis, order)


def cell_ids(counts, rows, cols, z, me, rows_axis, cols_axis, chunk_tiles):
    chunk = rows // chunk_tiles
    local = rows - chunk * chunk_tiles
    order = send_order(chunk, z, rows_axis)
    block = cols // chunk_tiles
    col_local = cols - block * chunk_tiles
    hop = me // 2 - block // 2
    hop = jnp.where(hop < 0, hop + cols_axis // 2, hop)
    near = 2 * hop + jnp.abs(block % 2 - me % 2)
    cell = ((order * cols_axis + near) * chunk_tiles + col_local) * chunk_tiles + local
    slot = lax.broadcasted_iota(jnp.int32, rows.shape, 1)
    return jnp.where(slot < counts, cell, -1)


def densify_lanes(axes, first, form, cell_ref, values_ref, pick_ref, dense_ref, copies):
    cols_axis, chunk_tiles, chunks = axes
    cells, slots = pick_ref.shape
    steps = values_ref.shape[1] // (2 * LANES)
    for begin, copy in copies:
        copy.start()
    cell = cell_ref[...] - first * (cells // chunks)
    index = lax.broadcasted_iota(jnp.int32, (cells, slots), 0)
    pick_ref[...] = jnp.where(index == cell, 1.0, 0.0).astype(pick_ref.dtype)

    part_cells, unroll = form
    part_cells = min(part_cells, cells)
    per_chunk = cells // chunks
    halves = 256 // (2 * SUB)
    low = lax.broadcasted_iota(jnp.int32, (halves, SUB, LANES), 2) < TILE

    def body(turn, carry):
        for begin, copy in copies:
            pl.when(turn * unroll == begin)(copy.wait)
        for step in [turn * unroll + k for k in range(unroll)]:
            lane = pl.multiple_of(step * 2 * LANES, 2 * LANES)
            for part in range(0, cells, part_cells):
                summed = jnp.dot(
                    pick_ref[part : part + part_cells, :],
                    values_ref[:, pl.ds(lane, 2 * LANES)],
                    preferred_element_type=jnp.float32,
                )
                for top in range(0, part_cells, 256):
                    chunk, column = divmod(part + top, per_chunk)
                    for pair in range(2):
                        block = summed[top : top + 256, pair * LANES : (pair + 1) * LANES]
                        block = block.reshape(halves, 2, SUB, LANES)
                        left, right = block[:, 0], block[:, 1]
                        even = jnp.where(low, left, pltpu.roll(right, TILE, 2))
                        odd = jnp.where(low, pltpu.roll(left, TILE, 2), right)
                        both = jnp.concatenate([even, odd], axis=1).astype(jnp.bfloat16)
                        for k in range(halves):
                            lanes = pl.ds((column // (2 * SUB) + k) * LANES, LANES)
                            dense_ref[chunk, 2 * step + pair, :, lanes] = both[k]
        return carry

    lax.fori_loop(0, steps // unroll, body, 0)


def densify_kernel(axes, first, lane, form, cell_ref, values_hbm, out_ref, *scratch):
    values_ref, pick_ref, sems = scratch
    copies = []
    width = values_ref.shape[1]
    cuts = [0, width // 4, width // 2, width]
    for k in range(3):
        copy = pltpu.make_async_copy(
            values_hbm.at[:, pl.ds(lane + cuts[k], cuts[k + 1] - cuts[k])],
            values_ref.at[:, pl.ds(cuts[k], cuts[k + 1] - cuts[k])],
            sems.at[k],
        )
        copies.append((cuts[k] // (2 * LANES), copy))
    densify_lanes(axes, first, form, cell_ref, values_ref, pick_ref, out_ref, copies)


def densify_apply_kernel(axes, first, form, cell_ref, values_ref, *refs):
    out_ref, dense_ref, pick_ref = refs[-3:]
    densify_lanes(axes, first, form, cell_ref, values_ref, pick_ref, dense_ref, [])
    out_ref[...] = apply_blocks(dense_ref[0].reshape(out_ref.shape[0], -1), refs[:-3])


def apply_blocks(dense, blocks):
    total = None
    depth = blocks[0].shape[0]
    for k, block in enumerate(blocks):
        part = jnp.dot(
            dense[:, k * depth : (k + 1) * depth], block[...], preferred_element_type=jnp.float32
        )
        total = part if total is None else total + part
    return total


def apply_kernel(parts, position, *refs):
    out_ref = refs[-1]
    rows = out_ref.shape[0] // parts
    for k in range(parts):
        total = apply_blocks(refs[k][position].reshape(rows, -1), refs[parts:-1])
        out_ref[k * rows : (k + 1) * rows, :] = total.astype(out_ref.dtype)


def params():
    return pltpu.CompilerParams(vmem_limit_bytes=VMEM_LIMIT)


IN_VMEM = pl.BlockSpec(memory_space=pltpu.VMEM)
IN_HBM = pl.BlockSpec(memory_space=pltpu.HBM)


def densify(axes, first, lanes, form, cell, values, blocks=None):
    cols_axis, chunk_tiles, chunks = axes
    slots = values.shape[0]
    width = lanes[1] - lanes[0]
    pairs = width // LANES
    source_rows = cols_axis * chunk_tiles * TILE
    cells = chunks * chunk_tiles * cols_axis * chunk_tiles
    piece = chunk_tiles * TILE
    dense_shape = (chunks, pairs, 2 * SUB, source_rows)
    pick = pltpu.VMEM((cells, slots), jnp.bfloat16)
    cost = pl.CostEstimate(
        flops=4 * cells * slots * width, bytes_accessed=4 * slots * width, transcendentals=0
    )
    operands = (cell, values)
    if blocks is None:
        return pl.pallas_call(
            functools.partial(densify_kernel, axes, first, lanes[0], form),
            in_specs=[IN_VMEM, IN_HBM],
            out_specs=IN_VMEM,
            out_shape=jax.ShapeDtypeStruct(dense_shape, jnp.bfloat16),
            scratch_shapes=[
                pltpu.VMEM((slots, width), jnp.bfloat16),
                pick,
                pltpu.SemaphoreType.DMA((3,)),
            ],
            compiler_params=params(),
            cost_estimate=cost,
            name="densify",
        )(*operands)
    return pl.pallas_call(
        functools.partial(densify_apply_kernel, axes, first, form),
        in_specs=[IN_VMEM] * (2 + len(blocks)),
        out_specs=IN_VMEM,
        out_shape=jax.ShapeDtypeStruct((piece, blocks[0].shape[1]), jnp.float32),
        scratch_shapes=[pltpu.VMEM(dense_shape, jnp.bfloat16), pick],
        compiler_params=params(),
        cost_estimate=cost,
        name="densify_apply",
    )(*operands, *blocks)


def apply(dense, position, blocks):
    source_rows = dense[0].shape[3]
    piece = len(dense) * dense[0].shape[1] * dense[0].shape[2]
    feat_width = blocks[0].shape[1]
    return pl.pallas_call(
        functools.partial(apply_kernel, len(dense), position),
        in_specs=[IN_VMEM] * (len(dense) + len(blocks)),
        out_specs=IN_VMEM,
        out_shape=jax.ShapeDtypeStruct((piece, feat_width), jnp.bfloat16),
        compiler_params=params(),
        cost_estimate=pl.CostEstimate(
            flops=4 * piece * source_rows * feat_width,
            bytes_accessed=2 * piece * source_rows,
            transcendentals=0,
        ),
        name="apply",
    )(*dense, *blocks)


def gather_blocks(features, cols_axis, first):
    swap = [(k, k ^ 1) for k in range(cols_axis)]
    shift = [(k, (k + 2) % cols_axis) for k in range(cols_axis)]
    held = [features]
    for hop in range(1, cols_axis // 2):
        held.append(lax.ppermute(held[-1], "col", shift))
    blocks = [features, lax.ppermute(features, "col", swap)]
    for block in held[1:]:
        block, first = lax.optimization_barrier((block, first))
        blocks += [block, lax.ppermute(block, "col", swap)]
    return blocks, first


def finish_kernel(rows_axis, chunk_tiles, own_ref, *refs):
    weight_ref, bias_ref, out_ref = refs[-3:]
    terms = [ref[...].astype(jnp.float32) for ref in refs[:-3]]
    total = own_ref[...]
    if rows_axis == 4:
        z = lax.axis_index("row")
        inner = (z == 1) | (z == 2)
        terms = [terms[0], jnp.where(inner, terms[2] + terms[3], terms[1])]
    for term in terms:
        total = total + term
    hidden = total.astype(jnp.bfloat16)
    mixed = jnp.dot(hidden, weight_ref[...], preferred_element_type=jnp.float32) + bias_ref[...]
    mixed = jnp.maximum(mixed, 0.0)
    mixed = mixed.reshape(TILE, chunk_tiles, mixed.shape[1])
    for k in range(chunk_tiles):
        out_ref[k * TILE : (k + 1) * TILE, :] = mixed[:, k, :].astype(jnp.bfloat16)


def finish(own, received, weight, bias, rows_axis, chunk_tiles):
    return pl.pallas_call(
        functools.partial(finish_kernel, rows_axis, chunk_tiles),
        out_shape=jax.ShapeDtypeStruct(own.shape, jnp.bfloat16),
        in_specs=[pl.BlockSpec(memory_space=pltpu.VMEM)] * (3 + len(received)),
        out_specs=pl.BlockSpec(memory_space=pltpu.VMEM),
        compiler_params=params(),
        name="finish",
    )(own, *received, weight, bias)


def on_device(features, tile_values, tile_rows, tile_cols, counts, weight, bias):
    piece, feat_width = features.shape[1:]
    rows_axis, cols_axis = lax.axis_size("row"), lax.axis_size("col")
    chunk_tiles = piece // TILE
    slots = tile_values.shape[2]
    width = TILE * TILE
    z = lax.axis_index("row")
    cell = cell_ids(
        counts,
        tile_rows.reshape(1, slots),
        tile_cols.reshape(1, slots),
        z,
        lax.axis_index("col"),
        rows_axis,
        cols_axis,
        chunk_tiles,
    )
    tiles = (cell, tile_values.reshape(slots, width))
    axes = (cols_axis, chunk_tiles)

    group = min(3, rows_axis - 1)
    first = densify(axes + (group,), 0, (0, width // 2), (256, 1), *tiles)
    blocks, first = gather_blocks(features.reshape(piece, feat_width), cols_axis, first)
    parts = []
    received = []
    for position in range(rows_axis - 1):
        if position % group == 0:
            chunks = min(group, rows_axis - 1 - position)
            if position:
                first = densify(axes + (chunks,), position, (0, width // 2), (256, 1), *tiles)
            second = densify(axes + (chunks,), position, (width // 2, width), (256, 1), *tiles)
        parts.append(apply((first, second), position % group, blocks))
        if rows_axis != 4:
            shift = position + 1
            to = [(d, (d + shift) % rows_axis) for d in range(rows_axis)]
            received.append(lax.ppermute(parts[-1], "row", to))
    if rows_axis == 4:
        near = [(0, 1), (1, 0), (2, 3), (3, 2)]
        inner = (z == 1) | (z == 2)
        passed = lax.ppermute(parts[0], "row", near)
        crossed = lax.ppermute(parts[2], "row", [(1, 2), (2, 1)])
        joined = parts[1].astype(jnp.float32)
        joined = joined + jnp.where(inner, passed.astype(jnp.float32), 0.0)
        joined, last = lax.optimization_barrier((joined.astype(jnp.bfloat16), parts[2]))
        far = lax.ppermute(joined, "row", [(0, 2), (1, 3), (2, 0), (3, 1)])
        last = lax.ppermute(last, "row", near)
        received = [far, passed, crossed, last]
    own = densify(axes + (1,), rows_axis - 1, (0, width), (256, 2), *tiles, blocks)
    bias = bias.reshape(1, feat_width)
    out = finish(own, received, weight, bias, rows_axis, chunk_tiles)
    return out.reshape(1, piece, feat_width)


def solution(mesh):
    in_specs = (
        P(("groups", "row"), "col", None),
        P(("groups", "row"), "col", None, None),
        P(("groups", "row"), "col", None),
        P(("groups", "row"), "col", None),
        P(("groups", "row"), "col"),
        P(),
        P(),
    )
    out_specs = P(("groups", "col"), "row", None)
    return jax.shard_map(
        on_device, mesh=mesh, in_specs=in_specs, out_specs=out_specs, check_vma=False
    )
```

```python
import functools

import jax
import jax.numpy as jnp
from jax import lax
from jax.experimental import pallas as pl
from jax.experimental.pallas import tpu as pltpu
from jax.sharding import PartitionSpec as P

TILE = 64
LANES = 128
SUB = 8
VMEM_LIMIT = 42 * 1024 * 1024


def send_order(chunk, z, rows_axis):
    if rows_axis == 4:
        apart = chunk ^ z
        return jnp.where((z == 0) | (z == 3), 3 - apart, (apart + 3) & 3)
    order = chunk - z - 1
    return jnp.where(order < 0, order + rows_axis, order)


def cell_ids(counts, rows, cols, z, me, rows_axis, cols_axis, chunk_tiles):
    chunk = rows // chunk_tiles
    local = rows - chunk * chunk_tiles
    order = send_order(chunk, z, rows_axis)
    block = cols // chunk_tiles
    col_local = cols - block * chunk_tiles
    hop = me // 2 - block // 2
    hop = jnp.where(hop < 0, hop + cols_axis // 2, hop)
    near = 2 * hop + jnp.abs(block % 2 - me % 2)
    cell = ((order * cols_axis + near) * chunk_tiles + col_local) * chunk_tiles + local
    slot = lax.broadcasted_iota(jnp.int32, rows.shape, 1)
    return jnp.where(slot < counts, cell, -1)


def densify_lanes(
    axes, first, form, cell_ref, values_ref, pick_ref, dense_ref, copies=(), held=()
):
    cols_axis, chunk_tiles, chunks = axes
    cells, slots = pick_ref.shape
    steps = values_ref.shape[1] // (2 * LANES)
    for begin, copy in copies:
        copy.start()
    cell = cell_ref[...] - first * (cells // chunks)
    index = lax.broadcasted_iota(jnp.int32, (cells, slots), 0)
    pick_ref[...] = jnp.where(index == cell, 1.0, 0.0).astype(pick_ref.dtype)

    part_cells = min(form, cells)
    per_chunk = cells // chunks
    halves = part_cells // (2 * SUB)
    low = lax.broadcasted_iota(jnp.int32, (halves, SUB, LANES), 2) < TILE

    def product(step, part):
        lane = pl.multiple_of(step * 2 * LANES, 2 * LANES)
        return jnp.dot(
            pick_ref[part : part + part_cells, :],
            values_ref[:, pl.ds(lane, 2 * LANES)],
            preferred_element_type=jnp.float32,
        )

    def place(step, part, summed):
        chunk, column = divmod(part, per_chunk)
        for pair in range(2):
            block = summed[:, pair * LANES : (pair + 1) * LANES]
            block = block.reshape(halves, 2, SUB, LANES)
            left, right = block[:, 0], block[:, 1]
            even = jnp.where(low, left, pltpu.roll(right, TILE, 2))
            odd = jnp.where(low, pltpu.roll(left, TILE, 2), right)
            both = jnp.concatenate([even, odd], axis=1).astype(jnp.bfloat16)
            for k in range(halves):
                lanes = pl.ds((column // (2 * SUB) + k) * LANES, LANES)
                dense_ref[chunk, 2 * step + pair, :, lanes] = both[k]

    def await_copies(step):
        for begin, copy in copies:
            pl.when(step == begin)(copy.wait)

    parts = range(0, cells, part_cells)
    if not held:

        def body(step, carry):
            await_copies(step)
            for part in parts:
                place(step, part, product(step, part))
            return carry

        lax.fori_loop(0, steps, body, 0)
        return

    even_ref, odd_ref = held

    def body(turn, carry):
        step = 2 * turn
        await_copies(step)
        before = jnp.maximum(step - 1, 0)
        for part in parts:
            even_ref[part : part + part_cells, :] = product(step, part)
            place(before, part, odd_ref[part : part + part_cells, :])
        for part in parts:
            odd_ref[part : part + part_cells, :] = product(step + 1, part)
            place(step, part, even_ref[part : part + part_cells, :])
        return carry

    lax.fori_loop(0, steps // 2, body, 0)
    for part in parts:
        place(steps - 1, part, odd_ref[part : part + part_cells, :])


def densify_kernel(axes, first, lane, form, cell_ref, values_hbm, out_ref, *scratch):
    values_ref, pick_ref, sems, *held = scratch
    copies = []
    width = values_ref.shape[1]
    cuts = [0, width // 4, width // 2, width]
    for k in range(3):
        copy = pltpu.make_async_copy(
            values_hbm.at[:, pl.ds(lane + cuts[k], cuts[k + 1] - cuts[k])],
            values_ref.at[:, pl.ds(cuts[k], cuts[k + 1] - cuts[k])],
            sems.at[k],
        )
        copies.append((cuts[k] // (2 * LANES), copy))
    densify_lanes(axes, first, form, cell_ref, values_ref, pick_ref, out_ref, copies, held)


def densify_apply_kernel(axes, first, form, cell_ref, values_ref, *refs):
    out_ref, dense_ref, pick_ref = refs[-3:]
    densify_lanes(axes, first, form, cell_ref, values_ref, pick_ref, dense_ref)
    out_ref[...] = apply_blocks(dense_ref[0].reshape(out_ref.shape[0], -1), refs[:-3])


def apply_blocks(dense, blocks):
    total = None
    depth = blocks[0].shape[0]
    for k, block in enumerate(blocks):
        part = jnp.dot(
            dense[:, k * depth : (k + 1) * depth], block[...], preferred_element_type=jnp.float32
        )
        total = part if total is None else total + part
    return total


def apply_kernel(parts, position, *refs):
    out_ref = refs[-1]
    rows = out_ref.shape[0] // parts
    for k in range(parts):
        total = apply_blocks(refs[k][position].reshape(rows, -1), refs[parts:-1])
        out_ref[k * rows : (k + 1) * rows, :] = total.astype(out_ref.dtype)


def params():
    return pltpu.CompilerParams(vmem_limit_bytes=VMEM_LIMIT)


IN_VMEM = pl.BlockSpec(memory_space=pltpu.VMEM)
IN_HBM = pl.BlockSpec(memory_space=pltpu.HBM)


def densify(axes, first, lanes, form, held, cell, values, blocks=None):
    cols_axis, chunk_tiles, chunks = axes
    slots = values.shape[0]
    width = lanes[1] - lanes[0]
    pairs = width // LANES
    source_rows = cols_axis * chunk_tiles * TILE
    cells = chunks * chunk_tiles * cols_axis * chunk_tiles
    piece = chunk_tiles * TILE
    dense_shape = (chunks, pairs, 2 * SUB, source_rows)
    pick = pltpu.VMEM((cells, slots), jnp.bfloat16)
    cost = pl.CostEstimate(
        flops=4 * cells * slots * width, bytes_accessed=4 * slots * width, transcendentals=0
    )
    operands = (cell, values)
    if blocks is None:
        return pl.pallas_call(
            functools.partial(densify_kernel, axes, first, lanes[0], form),
            in_specs=[IN_VMEM, IN_HBM],
            out_specs=IN_VMEM,
            out_shape=jax.ShapeDtypeStruct(dense_shape, jnp.bfloat16),
            scratch_shapes=[
                pltpu.VMEM((slots, width), jnp.bfloat16),
                pick,
                pltpu.SemaphoreType.DMA((3,)),
            ]
            + [pltpu.VMEM((cells, 2 * LANES), jnp.float32)] * held,
            compiler_params=params(),
            cost_estimate=cost,
            name="densify",
        )(*operands)
    return pl.pallas_call(
        functools.partial(densify_apply_kernel, axes, first, form),
        in_specs=[IN_VMEM] * (2 + len(blocks)),
        out_specs=IN_VMEM,
        out_shape=jax.ShapeDtypeStruct((piece, blocks[0].shape[1]), jnp.float32),
        scratch_shapes=[pltpu.VMEM(dense_shape, jnp.bfloat16), pick],
        compiler_params=params(),
        cost_estimate=cost,
        name="densify_apply",
    )(*operands, *blocks)


def apply(dense, position, blocks):
    source_rows = dense[0].shape[3]
    piece = len(dense) * dense[0].shape[1] * dense[0].shape[2]
    feat_width = blocks[0].shape[1]
    return pl.pallas_call(
        functools.partial(apply_kernel, len(dense), position),
        in_specs=[IN_VMEM] * (len(dense) + len(blocks)),
        out_specs=IN_VMEM,
        out_shape=jax.ShapeDtypeStruct((piece, feat_width), jnp.bfloat16),
        compiler_params=params(),
        cost_estimate=pl.CostEstimate(
            flops=4 * piece * source_rows * feat_width,
            bytes_accessed=2 * piece * source_rows,
            transcendentals=0,
        ),
        name="apply",
    )(*dense, *blocks)


def gather_blocks(features, cols_axis, first):
    swap = [(k, k ^ 1) for k in range(cols_axis)]
    shift = [(k, (k + 2) % cols_axis) for k in range(cols_axis)]
    held = [features]
    for hop in range(1, cols_axis // 2):
        held.append(lax.ppermute(held[-1], "col", shift))
    blocks = [features, lax.ppermute(features, "col", swap)]
    for block in held[1:]:
        block, first = lax.optimization_barrier((block, first))
        blocks += [block, lax.ppermute(block, "col", swap)]
    return blocks, first


def finish_kernel(rows_axis, chunk_tiles, own_ref, *refs):
    weight_ref, bias_ref, out_ref = refs[-3:]
    terms = [ref[...].astype(jnp.float32) for ref in refs[:-3]]
    total = own_ref[...]
    if rows_axis == 4:
        z = lax.axis_index("row")
        inner = (z == 1) | (z == 2)
        terms = [terms[0], jnp.where(inner, terms[2] + terms[3], terms[1])]
    for term in terms:
        total = total + term
    hidden = total.astype(jnp.bfloat16)
    mixed = jnp.dot(hidden, weight_ref[...], preferred_element_type=jnp.float32) + bias_ref[...]
    mixed = jnp.maximum(mixed, 0.0)
    mixed = mixed.reshape(TILE, chunk_tiles, mixed.shape[1])
    for k in range(chunk_tiles):
        out_ref[k * TILE : (k + 1) * TILE, :] = mixed[:, k, :].astype(jnp.bfloat16)


def finish(own, received, weight, bias, rows_axis, chunk_tiles):
    return pl.pallas_call(
        functools.partial(finish_kernel, rows_axis, chunk_tiles),
        out_shape=jax.ShapeDtypeStruct(own.shape, jnp.bfloat16),
        in_specs=[pl.BlockSpec(memory_space=pltpu.VMEM)] * (3 + len(received)),
        out_specs=pl.BlockSpec(memory_space=pltpu.VMEM),
        compiler_params=params(),
        name="finish",
    )(own, *received, weight, bias)


def on_device(features, tile_values, tile_rows, tile_cols, counts, weight, bias):
    piece, feat_width = features.shape[1:]
    rows_axis, cols_axis = lax.axis_size("row"), lax.axis_size("col")
    chunk_tiles = piece // TILE
    slots = tile_values.shape[2]
    width = TILE * TILE
    z = lax.axis_index("row")
    cell = cell_ids(
        counts,
        tile_rows.reshape(1, slots),
        tile_cols.reshape(1, slots),
        z,
        lax.axis_index("col"),
        rows_axis,
        cols_axis,
        chunk_tiles,
    )
    tiles = (cell, tile_values.reshape(slots, width))
    axes = (cols_axis, chunk_tiles)

    group = min(3, rows_axis - 1)
    first = densify(axes + (group,), 0, (0, width // 2), 256, 2, *tiles)
    blocks, first = gather_blocks(features.reshape(piece, feat_width), cols_axis, first)
    parts = []
    received = []
    for position in range(rows_axis - 1):
        if position % group == 0:
            chunks = min(group, rows_axis - 1 - position)
            if position:
                first = densify(axes + (chunks,), position, (0, width // 2), 256, 2, *tiles)
            second = densify(axes + (chunks,), position, (width // 2, width), 128, 0, *tiles)
        parts.append(apply((first, second), position % group, blocks))
        if rows_axis != 4:
            shift = position + 1
            to = [(d, (d + shift) % rows_axis) for d in range(rows_axis)]
            received.append(lax.ppermute(parts[-1], "row", to))
    if rows_axis == 4:
        near = [(0, 1), (1, 0), (2, 3), (3, 2)]
        inner = (z == 1) | (z == 2)
        passed = lax.ppermute(parts[0], "row", near)
        crossed = lax.ppermute(parts[2], "row", [(1, 2), (2, 1)])
        joined = parts[1].astype(jnp.float32)
        joined = joined + jnp.where(inner, passed.astype(jnp.float32), 0.0)
        joined, last = lax.optimization_barrier((joined.astype(jnp.bfloat16), parts[2]))
        far = lax.ppermute(joined, "row", [(0, 2), (1, 3), (2, 0), (3, 1)])
        last = lax.ppermute(last, "row", near)
        received = [far, passed, crossed, last]
    own = densify(axes + (1,), rows_axis - 1, (0, width), 256, 0, *tiles, blocks)
    bias = bias.reshape(1, feat_width)
    out = finish(own, received, weight, bias, rows_axis, chunk_tiles)
    return out.reshape(1, piece, feat_width)


def solution(mesh):
    in_specs = (
        P(("groups", "row"), "col", None),
        P(("groups", "row"), "col", None, None),
        P(("groups", "row"), "col", None),
        P(("groups", "row"), "col", None),
        P(("groups", "row"), "col"),
        P(),
        P(),
    )
    out_specs = P(("groups", "col"), "row", None)
    return jax.shard_map(
        on_device, mesh=mesh, in_specs=in_specs, out_specs=out_specs, check_vma=False
    )
```

```python
import functools

import jax
import jax.numpy as jnp
from jax import lax
from jax.experimental import pallas as pl
from jax.experimental.pallas import tpu as pltpu
from jax.sharding import PartitionSpec as P

TILE = 64
LANES = 128
SUB = 8
VMEM_LIMIT = 34 * 1024 * 1024


def send_order(chunk, z, rows_axis):
    if rows_axis == 4:
        apart = chunk ^ z
        return jnp.where((z == 0) | (z == 3), 3 - apart, (apart + 3) & 3)
    order = chunk - z - 1
    return jnp.where(order < 0, order + rows_axis, order)


def cell_ids(counts, rows, cols, z, me, rows_axis, cols_axis, chunk_tiles):
    chunk = rows // chunk_tiles
    local = rows - chunk * chunk_tiles
    order = send_order(chunk, z, rows_axis)
    block = cols // chunk_tiles
    col_local = cols - block * chunk_tiles
    hop = me // 2 - block // 2
    hop = jnp.where(hop < 0, hop + cols_axis // 2, hop)
    near = 2 * hop + jnp.abs(block % 2 - me % 2)
    cell = ((order * cols_axis + near) * chunk_tiles + col_local) * chunk_tiles + local
    slot = lax.broadcasted_iota(jnp.int32, rows.shape, 1)
    return jnp.where(slot < counts, cell, -1)


def densify_lanes(
    axes, first, cell_ref, values_ref, pick_ref, dense_ref, copies, held
):
    cols_axis, chunk_tiles, chunks = axes
    cells, slots = pick_ref.shape
    steps = values_ref.shape[1] // (2 * LANES)
    for begin, copy in copies:
        copy.start()
    cell = cell_ref[...] - first * (cells // chunks)
    index = lax.broadcasted_iota(jnp.int32, (cells, slots), 0)
    pick_ref[...] = jnp.where(index == cell, 1.0, 0.0).astype(pick_ref.dtype)

    part_cells = 256
    per_chunk = cells // chunks
    halves = part_cells // (2 * SUB)
    low = lax.broadcasted_iota(jnp.int32, (halves, SUB, LANES), 2) < TILE

    def product(step, part):
        lane = pl.multiple_of(step * 2 * LANES, 2 * LANES)
        return jnp.dot(
            pick_ref[part : part + part_cells, :],
            values_ref[:, pl.ds(lane, 2 * LANES)],
            preferred_element_type=jnp.float32,
        )

    def place(step, part, summed):
        chunk, column = divmod(part, per_chunk)
        for pair in range(2):
            block = summed[:, pair * LANES : (pair + 1) * LANES]
            block = block.reshape(halves, 2, SUB, LANES)
            left, right = block[:, 0], block[:, 1]
            even = jnp.where(low, left, pltpu.roll(right, TILE, 2))
            odd = jnp.where(low, pltpu.roll(left, TILE, 2), right)
            both = jnp.concatenate([even, odd], axis=1).astype(jnp.bfloat16)
            for k in range(halves):
                lanes = pl.ds((column // (2 * SUB) + k) * LANES, LANES)
                dense_ref[chunk, 2 * step + pair, :, lanes] = both[k]

    def await_copies(step):
        for begin, copy in copies:
            pl.when(step == begin)(copy.wait)

    parts = range(0, cells, part_cells)
    even_ref, odd_ref = held

    def body(turn, carry):
        step = 2 * turn
        await_copies(step)
        before = jnp.maximum(step - 1, 0)
        for part in parts:
            even_ref[part : part + part_cells, :] = product(step, part)
            place(before, part, odd_ref[part : part + part_cells, :])
        for part in parts:
            odd_ref[part : part + part_cells, :] = product(step + 1, part)
            place(step, part, even_ref[part : part + part_cells, :])
        return carry

    lax.fori_loop(0, steps // 2, body, 0)
    for part in parts:
        place(steps - 1, part, odd_ref[part : part + part_cells, :])


def load_kernel(axes, first, cell_ref, values_hbm, out_ref, values_ref, pick_ref, sems, *held):
    pieces = sems.shape[0]
    width = values_ref.shape[1] // pieces
    copies = []
    for k in range(pieces):
        lanes = pl.ds(k * width, width)
        copy = pltpu.make_async_copy(values_hbm.at[:, lanes], values_ref.at[:, lanes], sems.at[k])
        copies.append((k * width // (2 * LANES), copy))
    densify_lanes(axes, first, cell_ref, values_ref, pick_ref, out_ref, copies, held)


def densify_kernel(axes, first, cell_ref, values_ref, out_ref, pick_ref, *held):
    densify_lanes(axes, first, cell_ref, values_ref, pick_ref, out_ref, (), held)


def densify_apply_kernel(axes, first, cell_ref, values_ref, *refs):
    blocks, (out_ref, dense_ref, pick_ref, *held) = refs[:-5], refs[-5:]
    densify_lanes(axes, first, cell_ref, values_ref, pick_ref, dense_ref, (), held)
    total = apply_blocks(dense_ref[0].reshape(out_ref.shape[0], -1), blocks)
    out_ref[...] = total.astype(out_ref.dtype)


def apply_blocks(dense, blocks):
    total = None
    depth = blocks[0].shape[0]
    for k, block in enumerate(blocks):
        part = jnp.dot(
            dense[:, k * depth : (k + 1) * depth], block[...], preferred_element_type=jnp.float32
        )
        total = part if total is None else total + part
    return total


def apply_kernel(dense_ref, *refs):
    out_ref = refs[-1]
    total = apply_blocks(dense_ref[0].reshape(out_ref.shape[0], -1), refs[:-1])
    out_ref[...] = total.astype(out_ref.dtype)


IN_VMEM = pl.BlockSpec(memory_space=pltpu.VMEM)
IN_HBM = pl.BlockSpec(memory_space=pltpu.HBM)


def call(kernel, name, out_shape, operands, flops, scratch=(), in_specs=None):
    return pl.pallas_call(
        kernel,
        in_specs=in_specs or [IN_VMEM] * len(operands),
        out_specs=jax.tree.map(lambda leaf: IN_VMEM, out_shape),
        out_shape=out_shape,
        scratch_shapes=list(scratch),
        compiler_params=pltpu.CompilerParams(vmem_limit_bytes=VMEM_LIMIT),
        cost_estimate=pl.CostEstimate(
            flops=2 * flops,
            bytes_accessed=sum(x.size * x.dtype.itemsize for x in operands),
            transcendentals=0,
        ),
        name=name,
    )(*operands)


def densify(axes, position, cell, values, how, blocks=(), dtype=None):
    cols_axis, chunk_tiles, chunks = axes
    slots, width = values.shape
    source_rows = cols_axis * chunk_tiles * TILE
    cells = chunk_tiles * cols_axis * chunk_tiles
    piece = chunk_tiles * TILE
    dense_shape = (1, width // LANES, 2 * SUB, source_rows)
    dense = jax.ShapeDtypeStruct(dense_shape, jnp.bfloat16)
    flops = 2 * cells * slots * width
    pick = pltpu.VMEM((cells, slots), jnp.bfloat16)
    held = [pltpu.VMEM((cells, 2 * LANES), jnp.float32)] * 2
    if how == "load":
        return call(
            functools.partial(load_kernel, axes, position),
            "load_densify",
            (dense, jax.ShapeDtypeStruct(values.shape, values.dtype)),
            (cell, values),
            flops,
            [pick, pltpu.SemaphoreType.DMA((8,))] + held,
            [IN_VMEM, IN_HBM],
        )
    if how == "densify":
        kernel = functools.partial(densify_kernel, axes, position)
        return call(kernel, "densify", dense, (cell, values), flops, [pick] + held)
    return call(
        functools.partial(densify_apply_kernel, axes, position),
        "densify_apply",
        jax.ShapeDtypeStruct((piece, blocks[0].shape[1]), dtype),
        (cell, values, *blocks),
        flops,
        [pltpu.VMEM(dense_shape, jnp.bfloat16), pick] + held,
    )


def apply(dense, blocks):
    piece = dense.shape[1] * dense.shape[2]
    feat_width = blocks[0].shape[1]
    out = jax.ShapeDtypeStruct((piece, feat_width), jnp.bfloat16)
    flops = 2 * piece * dense.shape[3] * feat_width
    return call(apply_kernel, "apply", out, (dense, *blocks), flops)


def gather_blocks(features, cols_axis, first):
    swap = [(k, k ^ 1) for k in range(cols_axis)]
    shift = [(k, (k + 2) % cols_axis) for k in range(cols_axis)]
    held = [features]
    for hop in range(1, cols_axis // 2):
        held.append(lax.ppermute(held[-1], "col", shift))
    blocks = [features, lax.ppermute(features, "col", swap)]
    for block in held[1:]:
        block, first = lax.optimization_barrier((block, first))
        blocks += [block, lax.ppermute(block, "col", swap)]
    return blocks, first


def finish_kernel(rows_axis, chunk_tiles, own_ref, *refs):
    weight_ref, bias_ref, out_ref = refs[-3:]
    terms = [ref[...].astype(jnp.float32) for ref in refs[:-3]]
    total = own_ref[...]
    if rows_axis == 4:
        z = lax.axis_index("row")
        inner = (z == 1) | (z == 2)
        terms = [terms[0], jnp.where(inner, terms[2] + terms[3], terms[1])]
    for term in terms:
        total = total + term
    hidden = total.astype(jnp.bfloat16)
    mixed = jnp.dot(hidden, weight_ref[...], preferred_element_type=jnp.float32) + bias_ref[...]
    mixed = jnp.maximum(mixed, 0.0)
    mixed = mixed.reshape(TILE, chunk_tiles, mixed.shape[1])
    for k in range(chunk_tiles):
        out_ref[k * TILE : (k + 1) * TILE, :] = mixed[:, k, :].astype(jnp.bfloat16)


def finish(own, received, weight, bias, rows_axis, chunk_tiles):
    kernel = functools.partial(finish_kernel, rows_axis, chunk_tiles)
    out = jax.ShapeDtypeStruct(own.shape, jnp.bfloat16)
    flops = 2 * own.shape[0] * weight.size
    return call(kernel, "finish", out, (own, *received, weight, bias), flops)


def on_device(features, tile_values, tile_rows, tile_cols, counts, weight, bias):
    piece, feat_width = features.shape[1:]
    rows_axis, cols_axis = lax.axis_size("row"), lax.axis_size("col")
    chunk_tiles = piece // TILE
    slots = tile_values.shape[2]
    width = TILE * TILE
    z = lax.axis_index("row")
    cell = cell_ids(
        counts,
        tile_rows.reshape(1, slots),
        tile_cols.reshape(1, slots),
        z,
        lax.axis_index("col"),
        rows_axis,
        cols_axis,
        chunk_tiles,
    )
    values = tile_values.reshape(slots, width)
    axes = (cols_axis, chunk_tiles, 1)

    dense, values = densify(axes, 0, cell, values, "load")
    blocks, dense = gather_blocks(features.reshape(piece, feat_width), cols_axis, dense)
    if rows_axis == 4:
        near = [(0, 1), (1, 0), (2, 3), (3, 2)]
        inner = (z == 1) | (z == 2)
        last = densify(axes, 2, cell, values, "densify")
        passed = lax.ppermute(apply(dense, blocks), "row", near)
        last = apply(last, blocks)
        crossed = lax.ppermute(last, "row", [(1, 2), (2, 1)])
        values, crossing = lax.optimization_barrier((values, last))
        joined = densify(axes, 1, cell, values, "apply", blocks, jnp.float32)
        joined = joined + jnp.where(inner, passed.astype(jnp.float32), 0.0)
        joined, last = lax.optimization_barrier((joined.astype(jnp.bfloat16), last))
        far = lax.ppermute(joined, "row", [(0, 2), (1, 3), (2, 0), (3, 1)])
        last = lax.ppermute(last, "row", near)
        received = [far, passed, crossed, last]
    else:
        received = []
        for position in range(rows_axis - 1):
            if position:
                part = densify(axes, position, cell, values, "apply", blocks, jnp.bfloat16)
            else:
                part = apply(dense, blocks)
            to = [(d, (d + position + 1) % rows_axis) for d in range(rows_axis)]
            received.append(lax.ppermute(part, "row", to))
    own = densify(axes, rows_axis - 1, cell, values, "apply", blocks, jnp.float32)
    bias = bias.reshape(1, feat_width)
    out = finish(own, received, weight, bias, rows_axis, chunk_tiles)
    return out.reshape(1, piece, feat_width)


def solution(mesh):
    in_specs = (
        P(("groups", "row"), "col", None),
        P(("groups", "row"), "col", None, None),
        P(("groups", "row"), "col", None),
        P(("groups", "row"), "col", None),
        P(("groups", "row"), "col"),
        P(),
        P(),
    )
    out_specs = P(("groups", "col"), "row", None)
    return jax.shard_map(
        on_device, mesh=mesh, in_specs=in_specs, out_specs=out_specs, check_vma=False
    )
```

```python
import functools

import jax
import jax.numpy as jnp
from jax import lax
from jax.experimental import pallas as pl
from jax.experimental.pallas import tpu as pltpu
from jax.sharding import PartitionSpec as P

TILE = 64
LANES = 128
SUB = 8
VMEM_LIMIT = 24 * 1024 * 1024
LOAD_VMEM_LIMIT = 48 * 1024 * 1024


def send_order(chunk, z, rows_axis):
    if rows_axis == 4:
        return 3 - (chunk ^ z)
    order = chunk - z - 1
    return jnp.where(order < 0, order + rows_axis, order)


def cell_ids(counts, rows, cols, z, me, rows_axis, cols_axis, chunk_tiles):
    chunk = rows // chunk_tiles
    local = rows - chunk * chunk_tiles
    order = send_order(chunk, z, rows_axis)
    block = cols // chunk_tiles
    col_local = cols - block * chunk_tiles
    hop = me // 2 - block // 2
    hop = jnp.where(hop < 0, hop + cols_axis // 2, hop)
    near = 2 * hop + jnp.abs(block % 2 - me % 2)
    cell = ((order * cols_axis + near) * chunk_tiles + col_local) * chunk_tiles + local
    slot = lax.broadcasted_iota(jnp.int32, rows.shape, 1)
    return jnp.where(slot < counts, cell, -1)


def densify_lanes(
    axes, first, cell_ref, values_ref, pick_ref, dense_ref, copies, held
):
    cols_axis, chunk_tiles, chunks = axes
    cells, slots = pick_ref.shape
    steps = values_ref.shape[1] // (2 * LANES)
    for begin, copy in copies:
        copy.start()
    cell = cell_ref[...] - first * (cells // chunks)
    index = lax.broadcasted_iota(jnp.int32, (cells, slots), 0)
    pick_ref[...] = jnp.where(index == cell, 1.0, 0.0).astype(pick_ref.dtype)

    part_cells = 256
    per_chunk = cells // chunks
    halves = part_cells // (2 * SUB)
    low = lax.broadcasted_iota(jnp.int32, (halves, SUB, LANES), 2) < TILE

    def product(step, part):
        lane = pl.multiple_of(step * 2 * LANES, 2 * LANES)
        return jnp.dot(
            pick_ref[part : part + part_cells, :],
            values_ref[:, pl.ds(lane, 2 * LANES)],
            preferred_element_type=jnp.float32,
        )

    def place(step, part, summed):
        chunk, column = divmod(part, per_chunk)
        for pair in range(2):
            block = summed[:, pair * LANES : (pair + 1) * LANES]
            block = block.reshape(halves, 2, SUB, LANES)
            left, right = block[:, 0], block[:, 1]
            even = jnp.where(low, left, pltpu.roll(right, TILE, 2))
            odd = jnp.where(low, pltpu.roll(left, TILE, 2), right)
            both = jnp.concatenate([even, odd], axis=1).astype(jnp.bfloat16)
            for k in range(halves):
                lanes = pl.ds((column // (2 * SUB) + k) * LANES, LANES)
                dense_ref[chunk, 2 * step + pair, :, lanes] = both[k]

    def await_copies(step):
        for begin, copy in copies:
            pl.when(step == begin)(copy.wait)

    parts = range(0, cells, part_cells)
    even_ref, odd_ref = held

    def body(turn, carry):
        step = 2 * turn
        await_copies(step)
        before = jnp.maximum(step - 1, 0)
        for part in parts:
            even_ref[part : part + part_cells, :] = product(step, part)
            place(before, part, odd_ref[part : part + part_cells, :])
        for part in parts:
            odd_ref[part : part + part_cells, :] = product(step + 1, part)
            place(step, part, even_ref[part : part + part_cells, :])
        return carry

    lax.fori_loop(0, steps // 2, body, 0)
    for part in parts:
        place(steps - 1, part, odd_ref[part : part + part_cells, :])


def load_kernel(axes, first, cell_ref, values_hbm, out_ref, values_ref, pick_ref, sems, *held):
    width = values_ref.shape[1]
    cuts = [0, width // 8, width // 4, width // 2, width * 3 // 4, width]
    copies = []
    for k in range(len(cuts) - 1):
        lanes = pl.ds(cuts[k], cuts[k + 1] - cuts[k])
        copy = pltpu.make_async_copy(values_hbm.at[:, lanes], values_ref.at[:, lanes], sems.at[k])
        copies.append((cuts[k] // (2 * LANES), copy))
    densify_lanes(axes, first, cell_ref, values_ref, pick_ref, out_ref, copies, held)


def densify_kernel(axes, first, cell_ref, values_ref, out_ref, pick_ref, *held):
    densify_lanes(axes, first, cell_ref, values_ref, pick_ref, out_ref, (), held)


def densify_apply_kernel(axes, first, cell_ref, values_ref, *refs):
    blocks, (out_ref, dense_ref, pick_ref, *held) = refs[:-5], refs[-5:]
    densify_lanes(axes, first, cell_ref, values_ref, pick_ref, dense_ref, (), held)
    total = apply_blocks(dense_ref[0].reshape(out_ref.shape[0], -1), blocks)
    out_ref[...] = total.astype(out_ref.dtype)


def apply_blocks(dense, blocks):
    total = None
    depth = blocks[0].shape[0]
    for k, block in enumerate(blocks):
        part = jnp.dot(
            dense[:, k * depth : (k + 1) * depth], block[...], preferred_element_type=jnp.float32
        )
        total = part if total is None else total + part
    return total


def apply_kernel(dense_ref, *refs):
    out_ref = refs[-1]
    total = apply_blocks(dense_ref[0].reshape(out_ref.shape[0], -1), refs[:-1])
    out_ref[...] = total.astype(out_ref.dtype)


IN_VMEM = pl.BlockSpec(memory_space=pltpu.VMEM)
IN_HBM = pl.BlockSpec(memory_space=pltpu.HBM)


def call(kernel, name, out_shape, operands, flops, scratch=(), in_specs=None, limit=VMEM_LIMIT):
    return pl.pallas_call(
        kernel,
        in_specs=in_specs or [IN_VMEM] * len(operands),
        out_specs=jax.tree.map(lambda leaf: IN_VMEM, out_shape),
        out_shape=out_shape,
        scratch_shapes=list(scratch),
        compiler_params=pltpu.CompilerParams(vmem_limit_bytes=limit),
        cost_estimate=pl.CostEstimate(
            flops=flops // 64,
            bytes_accessed=sum(x.size for x in operands) // 64,
            transcendentals=0,
        ),
        name=name,
    )(*operands)


def densify(axes, position, cell, values, how, blocks=(), dtype=None):
    cols_axis, chunk_tiles, chunks = axes
    slots, width = values.shape
    source_rows = cols_axis * chunk_tiles * TILE
    cells = chunk_tiles * cols_axis * chunk_tiles
    piece = chunk_tiles * TILE
    dense_shape = (1, width // LANES, 2 * SUB, source_rows)
    dense = jax.ShapeDtypeStruct(dense_shape, jnp.bfloat16)
    flops = 2 * cells * slots * width
    pick = pltpu.VMEM((cells, slots), jnp.bfloat16)
    held = [pltpu.VMEM((cells, 2 * LANES), jnp.float32)] * 2
    if how == "load":
        return call(
            functools.partial(load_kernel, axes, position),
            "load_densify",
            dense,
            (cell, values),
            flops,
            [pltpu.VMEM(values.shape, values.dtype), pick, pltpu.SemaphoreType.DMA((5,))] + held,
            [IN_VMEM, IN_HBM],
            LOAD_VMEM_LIMIT,
        )
    if how == "densify":
        kernel = functools.partial(densify_kernel, axes, position)
        return call(kernel, "densify", dense, (cell, values), flops, [pick] + held)
    return call(
        functools.partial(densify_apply_kernel, axes, position),
        "densify_apply",
        jax.ShapeDtypeStruct((piece, blocks[0].shape[1]), dtype),
        (cell, values, *blocks),
        flops,
        [pltpu.VMEM(dense_shape, jnp.bfloat16), pick] + held,
    )


def apply(dense, blocks, dtype=jnp.bfloat16):
    piece = dense.shape[1] * dense.shape[2]
    feat_width = blocks[0].shape[1]
    out = jax.ShapeDtypeStruct((piece, feat_width), dtype)
    flops = 2 * piece * dense.shape[3] * feat_width
    return call(apply_kernel, "apply", out, (dense, *blocks), flops)


def gather_blocks(features, cols_axis, first):
    swap = [(k, k ^ 1) for k in range(cols_axis)]
    shift = [(k, (k + 2) % cols_axis) for k in range(cols_axis)]
    held = [features]
    for hop in range(1, cols_axis // 2):
        held.append(lax.ppermute(held[-1], "col", shift))
    blocks = [features, lax.ppermute(features, "col", swap)]
    for block in held[1:]:
        block, first = lax.optimization_barrier((block, first))
        blocks += [block, lax.ppermute(block, "col", swap)]
    return blocks, first


def finish_kernel(chunk_tiles, own_ref, *refs):
    weight_ref, bias_ref, out_ref = refs[-3:]
    total = own_ref[...]
    for ref in refs[:-3]:
        total = total + ref[...].astype(jnp.float32)
    hidden = total.astype(jnp.bfloat16)
    mixed = jnp.dot(hidden, weight_ref[...], preferred_element_type=jnp.float32) + bias_ref[...]
    mixed = jnp.maximum(mixed, 0.0)
    mixed = mixed.reshape(TILE, chunk_tiles, mixed.shape[1])
    for k in range(chunk_tiles):
        out_ref[k * TILE : (k + 1) * TILE, :] = mixed[:, k, :].astype(jnp.bfloat16)


def finish(own, received, weight, bias, chunk_tiles):
    kernel = functools.partial(finish_kernel, chunk_tiles)
    out = jax.ShapeDtypeStruct(own.shape, jnp.bfloat16)
    flops = 2 * own.shape[0] * weight.size
    return call(kernel, "finish", out, (own, *received, weight, bias), flops)


def on_device(features, tile_values, tile_rows, tile_cols, counts, weight, bias):
    piece, feat_width = features.shape[1:]
    rows_axis, cols_axis = lax.axis_size("row"), lax.axis_size("col")
    chunk_tiles = piece // TILE
    slots = tile_values.shape[2]
    width = TILE * TILE
    z = lax.axis_index("row")
    cell = cell_ids(
        counts,
        tile_rows.reshape(1, slots),
        tile_cols.reshape(1, slots),
        z,
        lax.axis_index("col"),
        rows_axis,
        cols_axis,
        chunk_tiles,
    )
    values = tile_values.reshape(slots, width)
    axes = (cols_axis, chunk_tiles, 1)

    dense = densify(axes, 0, cell, values, "load")
    blocks, dense = gather_blocks(features.reshape(piece, feat_width), cols_axis, dense)
    if rows_axis == 4:
        near = [(0, 1), (1, 0), (2, 3), (3, 2)]
        inner = (z == 1) | (z == 2)
        second = densify(axes, 1, cell, values, "densify")
        dense, second = lax.optimization_barrier((dense, second))
        part = apply(dense, blocks)
        passed = lax.ppermute(part, "row", near)
        crossed = lax.ppermute(part, "row", [(1, 2), (2, 1)])
        joined = apply(second, blocks, jnp.float32)
        part = densify(axes, 2, cell, values, "apply", blocks, jnp.bfloat16)
        joined, part = lax.optimization_barrier((joined, part))
        joined = joined + jnp.where(inner, passed.astype(jnp.float32), 0.0)
        joined, cell = lax.optimization_barrier((joined.astype(jnp.bfloat16), cell))
        far = lax.ppermute(joined, "row", [(0, 2), (1, 3), (2, 0), (3, 1)])
        received = [far, crossed, lax.ppermute(part, "row", near)]
    else:
        received = []
        for position in range(rows_axis - 1):
            if position:
                part = densify(axes, position, cell, values, "apply", blocks, jnp.bfloat16)
            else:
                part = apply(dense, blocks)
            to = [(d, (d + position + 1) % rows_axis) for d in range(rows_axis)]
            received.append(lax.ppermute(part, "row", to))
    own = densify(axes, rows_axis - 1, cell, values, "apply", blocks, jnp.float32)
    bias = bias.reshape(1, feat_width)
    out = finish(own, received, weight, bias, chunk_tiles)
    return out.reshape(1, piece, feat_width)


def solution(mesh):
    in_specs = (
        P(("groups", "row"), "col", None),
        P(("groups", "row"), "col", None, None),
        P(("groups", "row"), "col", None),
        P(("groups", "row"), "col", None),
        P(("groups", "row"), "col"),
        P(),
        P(),
    )
    out_specs = P(("groups", "col"), "row", None)
    return jax.shard_map(
        on_device, mesh=mesh, in_specs=in_specs, out_specs=out_specs, check_vma=False
    )
```

```python
import functools

import jax
import jax.numpy as jnp
from jax import lax
from jax.experimental import pallas as pl
from jax.experimental.pallas import tpu as pltpu
from jax.sharding import PartitionSpec as P

TILE = 64
LANES = 128
SUB = 8
VMEM_LIMIT = 24 * 1024 * 1024
LOAD_VMEM_LIMIT = 46 * 1024 * 1024


def send_order(chunk, z, rows_axis):
    if rows_axis == 4:
        return 3 - (chunk ^ z)
    order = chunk - z - 1
    return jnp.where(order < 0, order + rows_axis, order)


def cell_ids(counts, rows, cols, z, me, rows_axis, cols_axis, chunk_tiles):
    chunk = rows // chunk_tiles
    local = rows - chunk * chunk_tiles
    order = send_order(chunk, z, rows_axis)
    block = cols // chunk_tiles
    col_local = cols - block * chunk_tiles
    hop = me // 2 - block // 2
    hop = jnp.where(hop < 0, hop + cols_axis // 2, hop)
    near = 2 * hop + jnp.abs(block % 2 - me % 2)
    cell = ((order * cols_axis + near) * chunk_tiles + col_local) * chunk_tiles + local
    slot = lax.broadcasted_iota(jnp.int32, rows.shape, 1)
    return jnp.where(slot < counts, cell, -1)


def densify_lanes(
    axes, first, cell_ref, values_ref, pick_ref, dense_ref, copies, held
):
    cols_axis, chunk_tiles, chunks = axes
    cells, slots = pick_ref.shape
    steps = values_ref.shape[1] // (2 * LANES)
    for begin, copy in copies:
        copy.start()
    cell = cell_ref[...] - first * (cells // chunks)
    index = lax.broadcasted_iota(jnp.int32, (cells, slots), 0)
    pick_ref[...] = jnp.where(index == cell, 1.0, 0.0).astype(pick_ref.dtype)

    part_cells = 256
    per_chunk = cells // chunks
    halves = part_cells // (2 * SUB)
    low = lax.broadcasted_iota(jnp.int32, (halves, SUB, LANES), 2) < TILE

    def product(step, part):
        lane = pl.multiple_of(step * 2 * LANES, 2 * LANES)
        return jnp.dot(
            pick_ref[part : part + part_cells, :],
            values_ref[:, pl.ds(lane, 2 * LANES)],
            preferred_element_type=jnp.float32,
        )

    def place(step, part, summed):
        chunk, column = divmod(part, per_chunk)
        for pair in range(2):
            block = summed[:, pair * LANES : (pair + 1) * LANES]
            block = block.reshape(halves, 2, SUB, LANES)
            left, right = block[:, 0], block[:, 1]
            even = jnp.where(low, left, pltpu.roll(right, TILE, 2))
            odd = jnp.where(low, pltpu.roll(left, TILE, 2), right)
            both = jnp.concatenate([even, odd], axis=1).astype(jnp.bfloat16)
            for k in range(halves):
                lanes = pl.ds((column // (2 * SUB) + k) * LANES, LANES)
                dense_ref[chunk, 2 * step + pair, :, lanes] = both[k]

    def await_copies(step):
        for begin, copy in copies:
            pl.when(step == begin)(copy.wait)

    parts = range(0, cells, part_cells)
    even_ref, odd_ref = held

    def body(turn, carry):
        step = 2 * turn
        await_copies(step)
        before = jnp.maximum(step - 1, 0)
        for part in parts:
            even_ref[part : part + part_cells, :] = product(step, part)
            place(before, part, odd_ref[part : part + part_cells, :])
        for part in parts:
            odd_ref[part : part + part_cells, :] = product(step + 1, part)
            place(step, part, even_ref[part : part + part_cells, :])
        return carry

    lax.fori_loop(0, steps // 2, body, 0)
    for part in parts:
        place(steps - 1, part, odd_ref[part : part + part_cells, :])


def load_kernel(axes, first, cell_ref, values_hbm, out_ref, values_ref, pick_ref, sems, *held):
    width = values_ref.shape[1]
    cuts = [0, width // 8, width // 4, width // 2, width * 3 // 4, width]
    copies = []
    for k in range(len(cuts) - 1):
        lanes = pl.ds(cuts[k], cuts[k + 1] - cuts[k])
        copy = pltpu.make_async_copy(values_hbm.at[:, lanes], values_ref.at[:, lanes], sems.at[k])
        copies.append((cuts[k] // (2 * LANES), copy))
    densify_lanes(axes, first, cell_ref, values_ref, pick_ref, out_ref, copies, held)


def densify_kernel(axes, first, cell_ref, values_ref, out_ref, pick_ref, *held):
    densify_lanes(axes, first, cell_ref, values_ref, pick_ref, out_ref, (), held)


def densify_apply_kernel(axes, first, cell_ref, values_ref, *refs):
    blocks, (out_ref, dense_ref, pick_ref, *held) = refs[:-5], refs[-5:]
    densify_lanes(axes, first, cell_ref, values_ref, pick_ref, dense_ref, (), held)
    total = apply_blocks(dense_ref[0].reshape(out_ref.shape[0], -1), blocks)
    out_ref[...] = total.astype(out_ref.dtype)


def apply_blocks(dense, blocks):
    total = None
    depth = blocks[0].shape[0]
    for k, block in enumerate(blocks):
        part = jnp.dot(
            dense[:, k * depth : (k + 1) * depth], block[...], preferred_element_type=jnp.float32
        )
        total = part if total is None else total + part
    return total


def apply_kernel(dense_ref, *refs):
    out_ref = refs[-1]
    total = apply_blocks(dense_ref[0].reshape(out_ref.shape[0], -1), refs[:-1])
    out_ref[...] = total.astype(out_ref.dtype)


IN_VMEM = pl.BlockSpec(memory_space=pltpu.VMEM)
IN_HBM = pl.BlockSpec(memory_space=pltpu.HBM)


def call(kernel, name, out_shape, operands, flops, scratch=(), in_specs=None, limit=VMEM_LIMIT):
    return pl.pallas_call(
        kernel,
        in_specs=in_specs or [IN_VMEM] * len(operands),
        out_specs=jax.tree.map(lambda leaf: IN_VMEM, out_shape),
        out_shape=out_shape,
        scratch_shapes=list(scratch),
        compiler_params=pltpu.CompilerParams(vmem_limit_bytes=limit),
        cost_estimate=pl.CostEstimate(
            flops=2 * flops,
            bytes_accessed=sum(x.size * x.dtype.itemsize for x in operands),
            transcendentals=0,
        ),
        name=name,
    )(*operands)


def densify(axes, position, cell, values, how, blocks=(), dtype=None):
    cols_axis, chunk_tiles, chunks = axes
    slots, width = values.shape
    source_rows = cols_axis * chunk_tiles * TILE
    cells = chunk_tiles * cols_axis * chunk_tiles
    piece = chunk_tiles * TILE
    dense_shape = (1, width // LANES, 2 * SUB, source_rows)
    dense = jax.ShapeDtypeStruct(dense_shape, jnp.bfloat16)
    flops = 2 * cells * slots * width
    pick = pltpu.VMEM((cells, slots), jnp.bfloat16)
    held = [pltpu.VMEM((cells, 2 * LANES), jnp.float32)] * 2
    if how == "load":
        return call(
            functools.partial(load_kernel, axes, position),
            "load_densify",
            dense,
            (cell, values),
            flops,
            [pltpu.VMEM(values.shape, values.dtype), pick, pltpu.SemaphoreType.DMA((5,))] + held,
            [IN_VMEM, IN_HBM],
            LOAD_VMEM_LIMIT,
        )
    if how == "densify":
        kernel = functools.partial(densify_kernel, axes, position)
        return call(kernel, "densify", dense, (cell, values), flops, [pick] + held)
    return call(
        functools.partial(densify_apply_kernel, axes, position),
        "densify_apply",
        jax.ShapeDtypeStruct((piece, blocks[0].shape[1]), dtype),
        (cell, values, *blocks),
        flops,
        [pltpu.VMEM(dense_shape, jnp.bfloat16), pick] + held,
    )


def apply(dense, blocks, dtype=jnp.bfloat16):
    piece = dense.shape[1] * dense.shape[2]
    feat_width = blocks[0].shape[1]
    out = jax.ShapeDtypeStruct((piece, feat_width), dtype)
    flops = 2 * piece * dense.shape[3] * feat_width
    return call(apply_kernel, "apply", out, (dense, *blocks), flops)


def gather_blocks(features, cols_axis, first):
    swap = [(k, k ^ 1) for k in range(cols_axis)]
    shift = [(k, (k + 2) % cols_axis) for k in range(cols_axis)]
    held = [features]
    for hop in range(1, cols_axis // 2):
        held.append(lax.ppermute(held[-1], "col", shift))
    blocks = [features, lax.ppermute(features, "col", swap)]
    for block in held[1:]:
        block, first = lax.optimization_barrier((block, first))
        blocks += [block, lax.ppermute(block, "col", swap)]
    return blocks, first


def finish_kernel(chunk_tiles, own_ref, *refs):
    weight_ref, bias_ref, out_ref = refs[-3:]
    total = own_ref[...]
    for ref in refs[:-3]:
        total = total + ref[...].astype(jnp.float32)
    hidden = total.astype(jnp.bfloat16)
    mixed = jnp.dot(hidden, weight_ref[...], preferred_element_type=jnp.float32) + bias_ref[...]
    mixed = jnp.maximum(mixed, 0.0)
    mixed = mixed.reshape(TILE, chunk_tiles, mixed.shape[1])
    for k in range(chunk_tiles):
        out_ref[k * TILE : (k + 1) * TILE, :] = mixed[:, k, :].astype(jnp.bfloat16)


def finish(own, received, weight, bias, chunk_tiles):
    kernel = functools.partial(finish_kernel, chunk_tiles)
    out = jax.ShapeDtypeStruct(own.shape, jnp.bfloat16)
    flops = 2 * own.shape[0] * weight.size
    return call(kernel, "finish", out, (own, *received, weight, bias), flops)


def on_device(features, tile_values, tile_rows, tile_cols, counts, weight, bias):
    piece, feat_width = features.shape[1:]
    rows_axis, cols_axis = lax.axis_size("row"), lax.axis_size("col")
    chunk_tiles = piece // TILE
    slots = tile_values.shape[2]
    width = TILE * TILE
    z = lax.axis_index("row")
    cell = cell_ids(
        counts,
        tile_rows.reshape(1, slots),
        tile_cols.reshape(1, slots),
        z,
        lax.axis_index("col"),
        rows_axis,
        cols_axis,
        chunk_tiles,
    )
    values = tile_values.reshape(slots, width)
    axes = (cols_axis, chunk_tiles, 1)

    dense = densify(axes, 0, cell, values, "load")
    blocks, dense = gather_blocks(features.reshape(piece, feat_width), cols_axis, dense)
    if rows_axis == 4:
        near = [(0, 1), (1, 0), (2, 3), (3, 2)]
        inner = (z == 1) | (z == 2)
        second = densify(axes, 1, cell, values, "densify")
        dense, second = lax.optimization_barrier((dense, second))
        part = apply(dense, blocks)
        passed = lax.ppermute(part, "row", near)
        crossed = lax.ppermute(part, "row", [(1, 2), (2, 1)])
        joined = apply(second, blocks, jnp.float32)
        part = densify(axes, 2, cell, values, "apply", blocks, jnp.bfloat16)
        joined, part = lax.optimization_barrier((joined, part))
        joined = joined + jnp.where(inner, passed.astype(jnp.float32), 0.0)
        joined, cell = lax.optimization_barrier((joined.astype(jnp.bfloat16), cell))
        far = lax.ppermute(joined, "row", [(0, 2), (1, 3), (2, 0), (3, 1)])
        received = [far, crossed, lax.ppermute(part, "row", near)]
    else:
        received = []
        for position in range(rows_axis - 1):
            if position:
                part = densify(axes, position, cell, values, "apply", blocks, jnp.bfloat16)
            else:
                part = apply(dense, blocks)
            to = [(d, (d + position + 1) % rows_axis) for d in range(rows_axis)]
            received.append(lax.ppermute(part, "row", to))
    own = densify(axes, rows_axis - 1, cell, values, "apply", blocks, jnp.float32)
    bias = bias.reshape(1, feat_width)
    out = finish(own, received, weight, bias, chunk_tiles)
    return out.reshape(1, piece, feat_width)


def solution(mesh):
    in_specs = (
        P(("groups", "row"), "col", None),
        P(("groups", "row"), "col", None, None),
        P(("groups", "row"), "col", None),
        P(("groups", "row"), "col", None),
        P(("groups", "row"), "col"),
        P(),
        P(),
    )
    out_specs = P(("groups", "col"), "row", None)
    return jax.shard_map(
        on_device, mesh=mesh, in_specs=in_specs, out_specs=out_specs, check_vma=False
    )
```

```python
import functools

import jax
import jax.numpy as jnp
from jax import lax
from jax.experimental import pallas as pl
from jax.experimental.pallas import tpu as pltpu
from jax.sharding import PartitionSpec as P

TILE = 64
LANES = 128
SUB = 8
VMEM_LIMIT = 24 * 1024 * 1024
LOAD_VMEM_LIMIT = 46 * 1024 * 1024


def send_order(chunk, z, rows_axis):
    if rows_axis == 4:
        return 3 - (chunk ^ z)
    order = chunk - z - 1
    return jnp.where(order < 0, order + rows_axis, order)


def cell_ids(counts, rows, cols, z, me, rows_axis, cols_axis, chunk_tiles):
    chunk = rows // chunk_tiles
    local = rows - chunk * chunk_tiles
    order = send_order(chunk, z, rows_axis)
    block = cols // chunk_tiles
    col_local = cols - block * chunk_tiles
    hop = me // 2 - block // 2
    hop = jnp.where(hop < 0, hop + cols_axis // 2, hop)
    near = 2 * hop + jnp.abs(block % 2 - me % 2)
    cell = ((order * cols_axis + near) * chunk_tiles + col_local) * chunk_tiles + local
    slot = lax.broadcasted_iota(jnp.int32, rows.shape, 1)
    return jnp.where(slot < counts, cell, -1)


def densify_lanes(
    axes, first, cell_ref, values_ref, pick_ref, dense_ref, copies, held
):
    cols_axis, chunk_tiles, chunks = axes
    cells, slots = pick_ref.shape
    steps = values_ref.shape[1] // (2 * LANES)
    for begin, copy in copies:
        copy.start()
    cell = cell_ref[...] - first * (cells // chunks)
    index = lax.broadcasted_iota(jnp.int32, (cells, slots), 0)
    pick_ref[...] = jnp.where(index == cell, 1.0, 0.0).astype(pick_ref.dtype)

    part_cells = 256
    per_chunk = cells // chunks
    halves = part_cells // (2 * SUB)
    low = lax.broadcasted_iota(jnp.int32, (halves, SUB, LANES), 2) < TILE

    def product(step, part):
        lane = pl.multiple_of(step * 2 * LANES, 2 * LANES)
        return jnp.dot(
            pick_ref[part : part + part_cells, :],
            values_ref[:, pl.ds(lane, 2 * LANES)],
            preferred_element_type=jnp.float32,
        )

    def place(step, part, summed):
        chunk, column = divmod(part, per_chunk)
        for pair in range(2):
            block = summed[:, pair * LANES : (pair + 1) * LANES]
            block = block.reshape(halves, 2, SUB, LANES)
            left, right = block[:, 0], block[:, 1]
            even = jnp.where(low, left, pltpu.roll(right, TILE, 2))
            odd = jnp.where(low, pltpu.roll(left, TILE, 2), right)
            both = jnp.concatenate([even, odd], axis=1).astype(jnp.bfloat16)
            for k in range(halves):
                lanes = pl.ds((column // (2 * SUB) + k) * LANES, LANES)
                dense_ref[chunk, 2 * step + pair, :, lanes] = both[k]

    def await_copies(step):
        for begin, copy in copies:
            pl.when(step == begin)(copy.wait)

    parts = range(0, cells, part_cells)
    even_ref, odd_ref = held

    def body(turn, carry):
        step = 2 * turn
        await_copies(step)
        before = jnp.maximum(step - 1, 0)
        for part in parts:
            even_ref[part : part + part_cells, :] = product(step, part)
            place(before, part, odd_ref[part : part + part_cells, :])
        for part in parts:
            odd_ref[part : part + part_cells, :] = product(step + 1, part)
            place(step, part, even_ref[part : part + part_cells, :])
        return carry

    lax.fori_loop(0, steps // 2, body, 0)
    for part in parts:
        place(steps - 1, part, odd_ref[part : part + part_cells, :])


def load_kernel(axes, first, cell_ref, values_hbm, out_ref, values_ref, pick_ref, sems, *held):
    width = values_ref.shape[1]
    cuts = [0, width // 8, width // 4, width // 2, width * 3 // 4, width]
    copies = []
    for k in range(len(cuts) - 1):
        lanes = pl.ds(cuts[k], cuts[k + 1] - cuts[k])
        copy = pltpu.make_async_copy(values_hbm.at[:, lanes], values_ref.at[:, lanes], sems.at[k])
        copies.append((cuts[k] // (2 * LANES), copy))
    densify_lanes(axes, first, cell_ref, values_ref, pick_ref, out_ref, copies, held)


def densify_apply_kernel(axes, first, cell_ref, values_ref, *refs):
    blocks, (out_ref, dense_ref, pick_ref, *held) = refs[:-5], refs[-5:]
    densify_lanes(axes, first, cell_ref, values_ref, pick_ref, dense_ref, (), held)
    total = apply_blocks(dense_ref[0].reshape(out_ref.shape[0], -1), blocks)
    out_ref[...] = total.astype(out_ref.dtype)


def apply_blocks(dense, blocks):
    total = None
    depth = blocks[0].shape[0]
    for k, block in enumerate(blocks):
        part = jnp.dot(
            dense[:, k * depth : (k + 1) * depth], block[...], preferred_element_type=jnp.float32
        )
        total = part if total is None else total + part
    return total


def apply_kernel(place, dense_ref, *refs):
    out_ref = refs[-1]
    total = apply_blocks(dense_ref[place].reshape(out_ref.shape[0], -1), refs[:-1])
    out_ref[...] = total.astype(out_ref.dtype)


IN_VMEM = pl.BlockSpec(memory_space=pltpu.VMEM)
IN_HBM = pl.BlockSpec(memory_space=pltpu.HBM)


def call(kernel, name, out_shape, operands, flops, scratch=(), in_specs=None, limit=VMEM_LIMIT):
    return pl.pallas_call(
        kernel,
        in_specs=in_specs or [IN_VMEM] * len(operands),
        out_specs=jax.tree.map(lambda leaf: IN_VMEM, out_shape),
        out_shape=out_shape,
        scratch_shapes=list(scratch),
        compiler_params=pltpu.CompilerParams(vmem_limit_bytes=limit),
        cost_estimate=pl.CostEstimate(
            flops=flops // 4,
            bytes_accessed=sum(x.size * x.dtype.itemsize for x in operands),
            transcendentals=0,
        ),
        name=name,
    )(*operands)


def densify(axes, position, cell, values, how, blocks=(), dtype=None):
    cols_axis, chunk_tiles, chunks = axes
    slots, width = values.shape
    source_rows = cols_axis * chunk_tiles * TILE
    cells = chunks * chunk_tiles * cols_axis * chunk_tiles
    piece = chunk_tiles * TILE
    dense_shape = (chunks, width // LANES, 2 * SUB, source_rows)
    dense = jax.ShapeDtypeStruct(dense_shape, jnp.bfloat16)
    flops = 2 * cells * slots * width
    pick = pltpu.VMEM((cells, slots), jnp.bfloat16)
    held = [pltpu.VMEM((cells, 2 * LANES), jnp.float32)] * 2
    if how == "load":
        return call(
            functools.partial(load_kernel, axes, position),
            "load_densify",
            dense,
            (cell, values),
            flops,
            [pltpu.VMEM(values.shape, values.dtype), pick, pltpu.SemaphoreType.DMA((5,))] + held,
            [IN_VMEM, IN_HBM],
            LOAD_VMEM_LIMIT,
        )
    return call(
        functools.partial(densify_apply_kernel, axes, position),
        "densify_apply",
        jax.ShapeDtypeStruct((piece, blocks[0].shape[1]), dtype),
        (cell, values, *blocks),
        flops,
        [pltpu.VMEM(dense_shape, jnp.bfloat16), pick] + held,
    )


def apply(dense, place, blocks, dtype=jnp.bfloat16):
    piece = dense.shape[1] * dense.shape[2]
    feat_width = blocks[0].shape[1]
    out = jax.ShapeDtypeStruct((piece, feat_width), dtype)
    flops = 2 * piece * dense.shape[3] * feat_width
    return call(functools.partial(apply_kernel, place), "apply", out, (dense, *blocks), flops)


def gather_blocks(features, cols_axis, first):
    swap = [(k, k ^ 1) for k in range(cols_axis)]
    shift = [(k, (k + 2) % cols_axis) for k in range(cols_axis)]
    held = [features]
    for hop in range(1, cols_axis // 2):
        held.append(lax.ppermute(held[-1], "col", shift))
    blocks = [features, lax.ppermute(features, "col", swap)]
    for block in held[1:]:
        block, first = lax.optimization_barrier((block, first))
        blocks += [block, lax.ppermute(block, "col", swap)]
    return blocks, first


def finish_kernel(chunk_tiles, own_ref, *refs):
    weight_ref, bias_ref, out_ref = refs[-3:]
    total = own_ref[...]
    for ref in refs[:-3]:
        total = total + ref[...].astype(jnp.float32)
    hidden = total.astype(jnp.bfloat16)
    mixed = jnp.dot(hidden, weight_ref[...], preferred_element_type=jnp.float32) + bias_ref[...]
    mixed = jnp.maximum(mixed, 0.0)
    mixed = mixed.reshape(TILE, chunk_tiles, mixed.shape[1])
    for k in range(chunk_tiles):
        out_ref[k * TILE : (k + 1) * TILE, :] = mixed[:, k, :].astype(jnp.bfloat16)


def finish(own, received, weight, bias, chunk_tiles):
    kernel = functools.partial(finish_kernel, chunk_tiles)
    out = jax.ShapeDtypeStruct(own.shape, jnp.bfloat16)
    flops = 2 * own.shape[0] * weight.size
    return call(kernel, "finish", out, (own, *received, weight, bias), flops)


def on_device(features, tile_values, tile_rows, tile_cols, counts, weight, bias):
    piece, feat_width = features.shape[1:]
    rows_axis, cols_axis = lax.axis_size("row"), lax.axis_size("col")
    chunk_tiles = piece // TILE
    slots = tile_values.shape[2]
    width = TILE * TILE
    z = lax.axis_index("row")
    cell = cell_ids(
        counts,
        tile_rows.reshape(1, slots),
        tile_cols.reshape(1, slots),
        z,
        lax.axis_index("col"),
        rows_axis,
        cols_axis,
        chunk_tiles,
    )
    values = tile_values.reshape(slots, width)
    axes = (cols_axis, chunk_tiles, 1)

    head = min(2, rows_axis - 1)
    dense = densify((cols_axis, chunk_tiles, head), 0, cell, values, "load")
    blocks, dense = gather_blocks(features.reshape(piece, feat_width), cols_axis, dense)
    if rows_axis == 4:
        near = [(0, 1), (1, 0), (2, 3), (3, 2)]
        inner = (z == 1) | (z == 2)
        part = apply(dense, 0, blocks)
        passed = lax.ppermute(part, "row", near)
        crossed = lax.ppermute(part, "row", [(1, 2), (2, 1)])
        joined = apply(dense, 1, blocks, jnp.float32)
        part = densify(axes, 2, cell, values, "apply", blocks, jnp.bfloat16)
        joined, part = lax.optimization_barrier((joined, part))
        joined = joined + jnp.where(inner, passed.astype(jnp.float32), 0.0)
        joined, cell = lax.optimization_barrier((joined.astype(jnp.bfloat16), cell))
        far = lax.ppermute(joined, "row", [(0, 2), (1, 3), (2, 0), (3, 1)])
        received = [far, crossed, lax.ppermute(part, "row", near)]
    else:
        received = []
        for position in range(rows_axis - 1):
            if position < head:
                part = apply(dense, position, blocks)
            else:
                part = densify(axes, position, cell, values, "apply", blocks, jnp.bfloat16)
            to = [(d, (d + position + 1) % rows_axis) for d in range(rows_axis)]
            received.append(lax.ppermute(part, "row", to))
    own = densify(axes, rows_axis - 1, cell, values, "apply", blocks, jnp.float32)
    bias = bias.reshape(1, feat_width)
    out = finish(own, received, weight, bias, chunk_tiles)
    return out.reshape(1, piece, feat_width)


def solution(mesh):
    in_specs = (
        P(("groups", "row"), "col", None),
        P(("groups", "row"), "col", None, None),
        P(("groups", "row"), "col", None),
        P(("groups", "row"), "col", None),
        P(("groups", "row"), "col"),
        P(),
        P(),
    )
    out_specs = P(("groups", "col"), "row", None)
    return jax.shard_map(
        on_device, mesh=mesh, in_specs=in_specs, out_specs=out_specs, check_vma=False
    )
```

```python
import functools

import jax
import jax.numpy as jnp
from jax import lax
from jax.experimental import pallas as pl
from jax.experimental.pallas import tpu as pltpu
from jax.sharding import PartitionSpec as P

TILE = 64
LANES = 128
SUB = 8
VMEM_LIMIT = 24 * 1024 * 1024
LOAD_VMEM_LIMIT = 46 * 1024 * 1024


def send_order(chunk, z, rows_axis):
    if rows_axis == 4:
        return 3 - (chunk ^ z)
    order = chunk - z - 1
    return jnp.where(order < 0, order + rows_axis, order)


def cell_ids(counts, rows, cols, z, me, rows_axis, cols_axis, chunk_tiles):
    chunk = rows // chunk_tiles
    local = rows - chunk * chunk_tiles
    order = send_order(chunk, z, rows_axis)
    block = cols // chunk_tiles
    col_local = cols - block * chunk_tiles
    hop = me // 2 - block // 2
    hop = jnp.where(hop < 0, hop + cols_axis // 2, hop)
    near = 2 * hop + jnp.abs(block % 2 - me % 2)
    cell = ((order * cols_axis + near) * chunk_tiles + col_local) * chunk_tiles + local
    slot = lax.broadcasted_iota(jnp.int32, rows.shape, 1)
    return jnp.where(slot < counts, cell, -1)


def densify_lanes(
    axes, first, cell_ref, values_ref, pick_ref, dense_ref, copies, held
):
    cols_axis, chunk_tiles, chunks = axes
    cells, slots = pick_ref.shape
    steps = values_ref.shape[1] // (2 * LANES)
    for begin, copy in copies:
        copy.start()
    cell = cell_ref[...] - first * (cells // chunks)
    index = lax.broadcasted_iota(jnp.int32, (cells, slots), 0)
    pick_ref[...] = jnp.where(index == cell, 1.0, 0.0).astype(pick_ref.dtype)

    part_cells = 256
    per_chunk = cells // chunks
    halves = part_cells // (2 * SUB)
    low = lax.broadcasted_iota(jnp.int32, (halves, SUB, LANES), 2) < TILE

    def product(step, part):
        lane = pl.multiple_of(step * 2 * LANES, 2 * LANES)
        return jnp.dot(
            pick_ref[part : part + part_cells, :],
            values_ref[:, pl.ds(lane, 2 * LANES)],
            preferred_element_type=jnp.float32,
        )

    def place(step, part, summed):
        chunk, column = divmod(part, per_chunk)
        for pair in range(2):
            block = summed[:, pair * LANES : (pair + 1) * LANES]
            block = block.reshape(halves, 2, SUB, LANES)
            left, right = block[:, 0], block[:, 1]
            even = jnp.where(low, left, pltpu.roll(right, TILE, 2))
            odd = jnp.where(low, pltpu.roll(left, TILE, 2), right)
            both = jnp.concatenate([even, odd], axis=1).astype(jnp.bfloat16)
            for k in range(halves):
                lanes = pl.ds((column // (2 * SUB) + k) * LANES, LANES)
                dense_ref[chunk, 2 * step + pair, :, lanes] = both[k]

    def await_copies(step):
        for begin, copy in copies:
            pl.when(step == begin)(copy.wait)

    parts = range(0, cells, part_cells)
    even_ref, odd_ref = held

    def body(turn, carry):
        step = 2 * turn
        await_copies(step)
        before = jnp.maximum(step - 1, 0)
        for part in parts:
            even_ref[part : part + part_cells, :] = product(step, part)
            place(before, part, odd_ref[part : part + part_cells, :])
        for part in parts:
            odd_ref[part : part + part_cells, :] = product(step + 1, part)
            place(step, part, even_ref[part : part + part_cells, :])
        return carry

    lax.fori_loop(0, steps // 2, body, 0)
    for part in parts:
        place(steps - 1, part, odd_ref[part : part + part_cells, :])


def load_kernel(axes, first, cell_ref, values_hbm, out_ref, values_ref, pick_ref, sems, *held):
    width = values_ref.shape[1]
    cuts = [0, width // 8, width // 4, width // 2, width * 3 // 4, width]
    copies = []
    for k in range(len(cuts) - 1):
        lanes = pl.ds(cuts[k], cuts[k + 1] - cuts[k])
        copy = pltpu.make_async_copy(values_hbm.at[:, lanes], values_ref.at[:, lanes], sems.at[k])
        copies.append((cuts[k] // (2 * LANES), copy))
    densify_lanes(axes, first, cell_ref, values_ref, pick_ref, out_ref, copies, held)


def densify_apply_kernel(axes, first, cell_ref, values_ref, *refs):
    blocks, (out_ref, dense_ref, pick_ref, *held) = refs[:-5], refs[-5:]
    densify_lanes(axes, first, cell_ref, values_ref, pick_ref, dense_ref, (), held)
    total = apply_blocks(dense_ref[0].reshape(out_ref.shape[0], -1), blocks)
    out_ref[...] = total.astype(out_ref.dtype)


def apply_blocks(dense, blocks):
    total = None
    depth = blocks[0].shape[0]
    for k, block in enumerate(blocks):
        part = jnp.dot(
            dense[:, k * depth : (k + 1) * depth], block[...], preferred_element_type=jnp.float32
        )
        total = part if total is None else total + part
    return total


def apply_kernel(chunks, dense_ref, values_ref, *refs):
    for place, out_ref in enumerate(refs[-chunks:]):
        total = apply_blocks(dense_ref[place].reshape(out_ref.shape[0], -1), refs[:-chunks])
        out_ref[...] = total.astype(out_ref.dtype)


IN_VMEM = pl.BlockSpec(memory_space=pltpu.VMEM)
IN_HBM = pl.BlockSpec(memory_space=pltpu.HBM)


def call(kernel, name, out_shape, operands, flops, scratch=(), in_specs=None, limit=VMEM_LIMIT):
    return pl.pallas_call(
        kernel,
        in_specs=in_specs or [IN_VMEM] * len(operands),
        out_specs=jax.tree.map(lambda leaf: IN_VMEM, out_shape),
        out_shape=out_shape,
        scratch_shapes=list(scratch),
        compiler_params=pltpu.CompilerParams(vmem_limit_bytes=limit),
        cost_estimate=pl.CostEstimate(
            flops=flops // 4,
            bytes_accessed=sum(x.size * x.dtype.itemsize for x in operands),
            transcendentals=0,
        ),
        name=name,
    )(*operands)


def densify(axes, position, cell, values, how, blocks=(), dtype=None):
    cols_axis, chunk_tiles, chunks = axes
    slots, width = values.shape
    source_rows = cols_axis * chunk_tiles * TILE
    cells = chunks * chunk_tiles * cols_axis * chunk_tiles
    piece = chunk_tiles * TILE
    dense_shape = (chunks, width // LANES, 2 * SUB, source_rows)
    dense = jax.ShapeDtypeStruct(dense_shape, jnp.bfloat16)
    flops = 2 * cells * slots * width
    pick = pltpu.VMEM((cells, slots), jnp.bfloat16)
    held = [pltpu.VMEM((cells, 2 * LANES), jnp.float32)] * 2
    if how == "load":
        return call(
            functools.partial(load_kernel, axes, position),
            "load_densify",
            dense,
            (cell, values),
            flops,
            [pltpu.VMEM(values.shape, values.dtype), pick, pltpu.SemaphoreType.DMA((5,))] + held,
            [IN_VMEM, IN_HBM],
            LOAD_VMEM_LIMIT,
        )
    return call(
        functools.partial(densify_apply_kernel, axes, position),
        "densify_apply",
        jax.ShapeDtypeStruct((piece, blocks[0].shape[1]), dtype),
        (cell, values, *blocks),
        flops,
        [pltpu.VMEM(dense_shape, jnp.bfloat16), pick] + held,
    )


def apply(dense, values, blocks, dtypes):
    piece = dense.shape[1] * dense.shape[2]
    feat_width = blocks[0].shape[1]
    outs = tuple(jax.ShapeDtypeStruct((piece, feat_width), dtype) for dtype in dtypes)
    flops = 2 * len(outs) * piece * dense.shape[3] * feat_width
    kernel = functools.partial(apply_kernel, len(outs))
    return call(kernel, "apply", outs, (dense, values, *blocks), flops)


def gather_blocks(features, cols_axis, first):
    swap = [(k, k ^ 1) for k in range(cols_axis)]
    shift = [(k, (k + 2) % cols_axis) for k in range(cols_axis)]
    held = [features]
    for hop in range(1, cols_axis // 2):
        held.append(lax.ppermute(held[-1], "col", shift))
    blocks = [features, lax.ppermute(features, "col", swap)]
    for block in held[1:]:
        block, first = lax.optimization_barrier((block, first))
        blocks += [block, lax.ppermute(block, "col", swap)]
    return blocks, first


def finish_kernel(chunk_tiles, own_ref, *refs):
    weight_ref, bias_ref, out_ref = refs[-3:]
    total = own_ref[...]
    for ref in refs[:-3]:
        total = total + ref[...].astype(jnp.float32)
    hidden = total.astype(jnp.bfloat16)
    mixed = jnp.dot(hidden, weight_ref[...], preferred_element_type=jnp.float32) + bias_ref[...]
    mixed = jnp.maximum(mixed, 0.0)
    mixed = mixed.reshape(TILE, chunk_tiles, mixed.shape[1])
    for k in range(chunk_tiles):
        out_ref[k * TILE : (k + 1) * TILE, :] = mixed[:, k, :].astype(jnp.bfloat16)


def finish(own, received, weight, bias, chunk_tiles):
    kernel = functools.partial(finish_kernel, chunk_tiles)
    out = jax.ShapeDtypeStruct(own.shape, jnp.bfloat16)
    flops = 2 * own.shape[0] * weight.size
    return call(kernel, "finish", out, (own, *received, weight, bias), flops)


def on_device(features, tile_values, tile_rows, tile_cols, counts, weight, bias):
    piece, feat_width = features.shape[1:]
    rows_axis, cols_axis = lax.axis_size("row"), lax.axis_size("col")
    chunk_tiles = piece // TILE
    slots = tile_values.shape[2]
    width = TILE * TILE
    z = lax.axis_index("row")
    cell = cell_ids(
        counts,
        tile_rows.reshape(1, slots),
        tile_cols.reshape(1, slots),
        z,
        lax.axis_index("col"),
        rows_axis,
        cols_axis,
        chunk_tiles,
    )
    values = tile_values.reshape(slots, width)
    axes = (cols_axis, chunk_tiles, 1)

    head = min(2, rows_axis - 1)
    dense = densify((cols_axis, chunk_tiles, head), 0, cell, values, "load")
    blocks, dense = gather_blocks(features.reshape(piece, feat_width), cols_axis, dense)
    if rows_axis == 4:
        near = [(0, 1), (1, 0), (2, 3), (3, 2)]
        inner = (z == 1) | (z == 2)
        part, joined = apply(dense, values, blocks, (jnp.bfloat16, jnp.float32))
        passed = lax.ppermute(part, "row", near)
        crossed = lax.ppermute(part, "row", [(1, 2), (2, 1)])
        part = densify(axes, 2, cell, values, "apply", blocks, jnp.bfloat16)
        joined, part = lax.optimization_barrier((joined, part))
        joined = joined + jnp.where(inner, passed.astype(jnp.float32), 0.0)
        joined, cell = lax.optimization_barrier((joined.astype(jnp.bfloat16), cell))
        far = lax.ppermute(joined, "row", [(0, 2), (1, 3), (2, 0), (3, 1)])
        received = [far, crossed, lax.ppermute(part, "row", near)]
    else:
        received = []
        parts = list(apply(dense, values, blocks, (jnp.bfloat16,) * head))
        for position in range(rows_axis - 1):
            if position < head:
                part = parts[position]
            else:
                part = densify(axes, position, cell, values, "apply", blocks, jnp.bfloat16)
            to = [(d, (d + position + 1) % rows_axis) for d in range(rows_axis)]
            received.append(lax.ppermute(part, "row", to))
    own = densify(axes, rows_axis - 1, cell, values, "apply", blocks, jnp.float32)
    bias = bias.reshape(1, feat_width)
    out = finish(own, received, weight, bias, chunk_tiles)
    return out.reshape(1, piece, feat_width)


def solution(mesh):
    in_specs = (
        P(("groups", "row"), "col", None),
        P(("groups", "row"), "col", None, None),
        P(("groups", "row"), "col", None),
        P(("groups", "row"), "col", None),
        P(("groups", "row"), "col"),
        P(),
        P(),
    )
    out_specs = P(("groups", "col"), "row", None)
    return jax.shard_map(
        on_device, mesh=mesh, in_specs=in_specs, out_specs=out_specs, check_vma=False
    )
```

```python
import functools

import jax
import jax.numpy as jnp
from jax import lax
from jax.experimental import pallas as pl
from jax.experimental.pallas import tpu as pltpu
from jax.sharding import PartitionSpec as P

TILE = 64
LANES = 128
SUB = 8
VMEM_LIMIT = 24 * 1024 * 1024
LOAD_VMEM_LIMIT = 46 * 1024 * 1024


def send_order(chunk, z, rows_axis):
    if rows_axis == 4:
        return 3 - (chunk ^ z)
    order = chunk - z - 1
    return jnp.where(order < 0, order + rows_axis, order)


def cell_ids(counts, rows, cols, z, me, rows_axis, cols_axis, chunk_tiles):
    chunk = rows // chunk_tiles
    local = rows - chunk * chunk_tiles
    order = send_order(chunk, z, rows_axis)
    block = cols // chunk_tiles
    col_local = cols - block * chunk_tiles
    hop = me // 2 - block // 2
    hop = jnp.where(hop < 0, hop + cols_axis // 2, hop)
    near = 2 * hop + jnp.abs(block % 2 - me % 2)
    cell = ((order * cols_axis + near) * chunk_tiles + col_local) * chunk_tiles + local
    slot = lax.broadcasted_iota(jnp.int32, rows.shape, 1)
    return jnp.where(slot < counts, cell, -1)


def densify_lanes(
    axes, first, cell_ref, values_ref, pick_ref, dense_ref, copies, held
):
    cols_axis, chunk_tiles, chunks = axes
    cells, slots = pick_ref.shape
    steps = values_ref.shape[1] // (2 * LANES)
    for begin, copy in copies:
        copy.start()
    cell = cell_ref[...] - first * (cells // chunks)
    index = lax.broadcasted_iota(jnp.int32, (cells, slots), 0)
    pick_ref[...] = jnp.where(index == cell, 1.0, 0.0).astype(pick_ref.dtype)

    part_cells = 256
    per_chunk = cells // chunks
    halves = part_cells // (2 * SUB)
    low = lax.broadcasted_iota(jnp.int32, (halves, SUB, LANES), 2) < TILE

    def product(step, part):
        lane = pl.multiple_of(step * 2 * LANES, 2 * LANES)
        return jnp.dot(
            pick_ref[part : part + part_cells, :],
            values_ref[:, pl.ds(lane, 2 * LANES)],
            preferred_element_type=jnp.float32,
        )

    def place(step, part, summed):
        chunk, column = divmod(part, per_chunk)
        for pair in range(2):
            block = summed[:, pair * LANES : (pair + 1) * LANES]
            block = block.reshape(halves, 2, SUB, LANES)
            left, right = block[:, 0], block[:, 1]
            even = jnp.where(low, left, pltpu.roll(right, TILE, 2))
            odd = jnp.where(low, pltpu.roll(left, TILE, 2), right)
            both = jnp.concatenate([even, odd], axis=1).astype(jnp.bfloat16)
            for k in range(halves):
                lanes = pl.ds((column // (2 * SUB) + k) * LANES, LANES)
                dense_ref[chunk, 2 * step + pair, :, lanes] = both[k]

    def await_copies(step):
        for begin, copy in copies:
            pl.when(step == begin)(copy.wait)

    parts = range(0, cells, part_cells)
    even_ref, odd_ref = held

    def body(turn, carry):
        step = 2 * turn
        await_copies(step)
        before = jnp.maximum(step - 1, 0)
        for part in parts:
            even_ref[part : part + part_cells, :] = product(step, part)
            place(before, part, odd_ref[part : part + part_cells, :])
        for part in parts:
            odd_ref[part : part + part_cells, :] = product(step + 1, part)
            place(step, part, even_ref[part : part + part_cells, :])
        return carry

    lax.fori_loop(0, steps // 2, body, 0)
    for part in parts:
        place(steps - 1, part, odd_ref[part : part + part_cells, :])


def load_kernel(axes, first, cell_ref, values_hbm, out_ref, values_ref, pick_ref, sems, *held):
    width = values_ref.shape[1]
    cuts = [0, width // 8, width // 4, width // 2, width * 3 // 4, width]
    copies = []
    for k in range(len(cuts) - 1):
        lanes = pl.ds(cuts[k], cuts[k + 1] - cuts[k])
        copy = pltpu.make_async_copy(values_hbm.at[:, lanes], values_ref.at[:, lanes], sems.at[k])
        copies.append((cuts[k] // (2 * LANES), copy))
    densify_lanes(axes, first, cell_ref, values_ref, pick_ref, out_ref, copies, held)


def densify_apply_kernel(axes, first, cell_ref, values_ref, *refs):
    blocks, (out_ref, dense_ref, pick_ref, *held) = refs[:-5], refs[-5:]
    densify_lanes(axes, first, cell_ref, values_ref, pick_ref, dense_ref, (), held)
    total = apply_blocks(dense_ref[0].reshape(out_ref.shape[0], -1), blocks)
    out_ref[...] = total.astype(out_ref.dtype)


def apply_blocks(dense, blocks):
    total = None
    depth = blocks[0].shape[0]
    for k, block in enumerate(blocks):
        part = jnp.dot(
            dense[:, k * depth : (k + 1) * depth], block[...], preferred_element_type=jnp.float32
        )
        total = part if total is None else total + part
    return total


def apply_kernel(chunks, dense_ref, values_ref, *refs):
    for place, out_ref in enumerate(refs[-chunks:]):
        total = apply_blocks(dense_ref[place].reshape(out_ref.shape[0], -1), refs[:-chunks])
        out_ref[...] = total.astype(out_ref.dtype)


IN_VMEM = pl.BlockSpec(memory_space=pltpu.VMEM)
IN_HBM = pl.BlockSpec(memory_space=pltpu.HBM)


def call(kernel, name, out_shape, operands, flops, scratch=(), in_specs=None, limit=VMEM_LIMIT, weigh=2):
    return pl.pallas_call(
        kernel,
        in_specs=in_specs or [IN_VMEM] * len(operands),
        out_specs=jax.tree.map(lambda leaf: IN_VMEM, out_shape),
        out_shape=out_shape,
        scratch_shapes=list(scratch),
        compiler_params=pltpu.CompilerParams(vmem_limit_bytes=limit),
        cost_estimate=pl.CostEstimate(
            flops=weigh * flops,
            bytes_accessed=sum(x.size * x.dtype.itemsize for x in operands),
            transcendentals=0,
        ),
        name=name,
    )(*operands)


def densify(axes, position, cell, values, how, blocks=(), dtype=None):
    cols_axis, chunk_tiles, chunks = axes
    slots, width = values.shape
    source_rows = cols_axis * chunk_tiles * TILE
    cells = chunks * chunk_tiles * cols_axis * chunk_tiles
    piece = chunk_tiles * TILE
    dense_shape = (chunks, width // LANES, 2 * SUB, source_rows)
    dense = jax.ShapeDtypeStruct(dense_shape, jnp.bfloat16)
    flops = 2 * cells * slots * width
    pick = pltpu.VMEM((cells, slots), jnp.bfloat16)
    held = [pltpu.VMEM((cells, 2 * LANES), jnp.float32)] * 2
    if how == "load":
        return call(
            functools.partial(load_kernel, axes, position),
            "load_densify",
            dense,
            (cell, values),
            flops,
            [pltpu.VMEM(values.shape, values.dtype), pick, pltpu.SemaphoreType.DMA((5,))] + held,
            [IN_VMEM, IN_HBM],
            LOAD_VMEM_LIMIT,
        )
    return call(
        functools.partial(densify_apply_kernel, axes, position),
        "densify_apply",
        jax.ShapeDtypeStruct((piece, blocks[0].shape[1]), dtype),
        (cell, values, *blocks),
        flops,
        [pltpu.VMEM(dense_shape, jnp.bfloat16), pick] + held,
        weigh=1,
    )


def apply(dense, values, blocks, dtypes):
    piece = dense.shape[1] * dense.shape[2]
    feat_width = blocks[0].shape[1]
    outs = tuple(jax.ShapeDtypeStruct((piece, feat_width), dtype) for dtype in dtypes)
    flops = 2 * len(outs) * piece * dense.shape[3] * feat_width
    kernel = functools.partial(apply_kernel, len(outs))
    return call(kernel, "apply", outs, (dense, values, *blocks), flops)


def gather_blocks(features, cols_axis, first):
    swap = [(k, k ^ 1) for k in range(cols_axis)]
    shift = [(k, (k + 2) % cols_axis) for k in range(cols_axis)]
    held = [features]
    for hop in range(1, cols_axis // 2):
        held.append(lax.ppermute(held[-1], "col", shift))
    blocks = [features, lax.ppermute(features, "col", swap)]
    for block in held[1:]:
        block, first = lax.optimization_barrier((block, first))
        blocks += [block, lax.ppermute(block, "col", swap)]
    return blocks, first


def finish_kernel(chunk_tiles, own_ref, *refs):
    weight_ref, bias_ref, out_ref = refs[-3:]
    total = own_ref[...]
    for ref in refs[:-3]:
        total = total + ref[...].astype(jnp.float32)
    hidden = total.astype(jnp.bfloat16)
    mixed = jnp.dot(hidden, weight_ref[...], preferred_element_type=jnp.float32) + bias_ref[...]
    mixed = jnp.maximum(mixed, 0.0)
    mixed = mixed.reshape(TILE, chunk_tiles, mixed.shape[1])
    for k in range(chunk_tiles):
        out_ref[k * TILE : (k + 1) * TILE, :] = mixed[:, k, :].astype(jnp.bfloat16)


def finish(own, received, weight, bias, chunk_tiles):
    kernel = functools.partial(finish_kernel, chunk_tiles)
    out = jax.ShapeDtypeStruct(own.shape, jnp.bfloat16)
    flops = 2 * own.shape[0] * weight.size
    return call(kernel, "finish", out, (own, *received, weight, bias), flops)


def on_device(features, tile_values, tile_rows, tile_cols, counts, weight, bias):
    piece, feat_width = features.shape[1:]
    rows_axis, cols_axis = lax.axis_size("row"), lax.axis_size("col")
    chunk_tiles = piece // TILE
    slots = tile_values.shape[2]
    width = TILE * TILE
    z = lax.axis_index("row")
    cell = cell_ids(
        counts,
        tile_rows.reshape(1, slots),
        tile_cols.reshape(1, slots),
        z,
        lax.axis_index("col"),
        rows_axis,
        cols_axis,
        chunk_tiles,
    )
    values = tile_values.reshape(slots, width)
    axes = (cols_axis, chunk_tiles, 1)

    head = min(2, rows_axis - 1)
    dense = densify((cols_axis, chunk_tiles, head), 0, cell, values, "load")
    blocks, dense = gather_blocks(features.reshape(piece, feat_width), cols_axis, dense)
    if rows_axis == 4:
        near = [(0, 1), (1, 0), (2, 3), (3, 2)]
        inner = (z == 1) | (z == 2)
        part, joined = apply(dense, values, blocks, (jnp.bfloat16, jnp.float32))
        passed = lax.ppermute(part, "row", near)
        crossed = lax.ppermute(part, "row", [(1, 2), (2, 1)])
        part = densify(axes, 2, cell, values, "apply", blocks, jnp.bfloat16)
        joined, part = lax.optimization_barrier((joined, part))
        joined = joined + jnp.where(inner, passed.astype(jnp.float32), 0.0)
        joined, cell = lax.optimization_barrier((joined.astype(jnp.bfloat16), cell))
        far = lax.ppermute(joined, "row", [(0, 2), (1, 3), (2, 0), (3, 1)])
        received = [far, crossed, lax.ppermute(part, "row", near)]
    else:
        received = []
        parts = list(apply(dense, values, blocks, (jnp.bfloat16,) * head))
        for position in range(rows_axis - 1):
            if position < head:
                part = parts[position]
            else:
                part = densify(axes, position, cell, values, "apply", blocks, jnp.bfloat16)
            to = [(d, (d + position + 1) % rows_axis) for d in range(rows_axis)]
            received.append(lax.ppermute(part, "row", to))
    own = densify(axes, rows_axis - 1, cell, values, "apply", blocks, jnp.float32)
    bias = bias.reshape(1, feat_width)
    out = finish(own, received, weight, bias, chunk_tiles)
    return out.reshape(1, piece, feat_width)


def solution(mesh):
    in_specs = (
        P(("groups", "row"), "col", None),
        P(("groups", "row"), "col", None, None),
        P(("groups", "row"), "col", None),
        P(("groups", "row"), "col", None),
        P(("groups", "row"), "col"),
        P(),
        P(),
    )
    out_specs = P(("groups", "col"), "row", None)
    return jax.shard_map(
        on_device, mesh=mesh, in_specs=in_specs, out_specs=out_specs, check_vma=False
    )
```

```python
import functools

import jax
import jax.numpy as jnp
from jax import lax
from jax.experimental import pallas as pl
from jax.experimental.pallas import tpu as pltpu
from jax.sharding import PartitionSpec as P

TILE = 64
LANES = 128
SUB = 8
VMEM_LIMIT = 24 * 1024 * 1024
FIRST_VMEM_LIMIT = 46 * 1024 * 1024
LATER_VMEM_LIMIT = 50 * 1024 * 1024


def send_order(chunk, z, rows_axis):
    if rows_axis == 4:
        return 3 - (chunk ^ z)
    order = chunk - z - 1
    return jnp.where(order < 0, order + rows_axis, order)


def cell_ids(counts, rows, cols, z, me, rows_axis, cols_axis, chunk_tiles):
    chunk = rows // chunk_tiles
    local = rows - chunk * chunk_tiles
    order = send_order(chunk, z, rows_axis)
    block = cols // chunk_tiles
    col_local = cols - block * chunk_tiles
    hop = me // 2 - block // 2
    hop = jnp.where(hop < 0, hop + cols_axis // 2, hop)
    near = 2 * hop + jnp.abs(block % 2 - me % 2)
    cell = ((order * cols_axis + near) * chunk_tiles + col_local) * chunk_tiles + local
    slot = lax.broadcasted_iota(jnp.int32, rows.shape, 1)
    return jnp.where(slot < counts, cell, -1)


def densify_lanes(
    axes, first, cell_ref, values_ref, pick_ref, dense_ref, copies, held
):
    cols_axis, chunk_tiles, chunks = axes
    cells, slots = pick_ref.shape
    steps = values_ref.shape[1] // (2 * LANES)
    for begin, copy in copies:
        copy.start()
    cell = cell_ref[...] - first * (cells // chunks)
    index = lax.broadcasted_iota(jnp.int32, (cells, slots), 0)
    pick_ref[...] = jnp.where(index == cell, 1.0, 0.0).astype(pick_ref.dtype)

    part_cells = 256
    per_chunk = cells // chunks
    halves = part_cells // (2 * SUB)
    low = lax.broadcasted_iota(jnp.int32, (halves, SUB, LANES), 2) < TILE

    def product(step, part):
        lane = pl.multiple_of(step * 2 * LANES, 2 * LANES)
        return jnp.dot(
            pick_ref[part : part + part_cells, :],
            values_ref[:, pl.ds(lane, 2 * LANES)],
            preferred_element_type=jnp.float32,
        )

    def place(step, part, summed):
        chunk, column = divmod(part, per_chunk)
        for pair in range(2):
            block = summed[:, pair * LANES : (pair + 1) * LANES]
            block = block.reshape(halves, 2, SUB, LANES)
            left, right = block[:, 0], block[:, 1]
            even = jnp.where(low, left, pltpu.roll(right, TILE, 2))
            odd = jnp.where(low, pltpu.roll(left, TILE, 2), right)
            both = jnp.concatenate([even, odd], axis=1).astype(jnp.bfloat16)
            for k in range(halves):
                lanes = pl.ds((column // (2 * SUB) + k) * LANES, LANES)
                dense_ref[chunk, 2 * step + pair, :, lanes] = both[k]

    def await_copies(step):
        for begin, copy in copies:
            pl.when(step == begin)(copy.wait)

    parts = range(0, cells, part_cells)
    even_ref, odd_ref = held

    def body(turn, carry):
        step = 2 * turn
        await_copies(step)
        before = jnp.maximum(step - 1, 0)
        for part in parts:
            even_ref[part : part + part_cells, :] = product(step, part)
            place(before, part, odd_ref[part : part + part_cells, :])
        for part in parts:
            odd_ref[part : part + part_cells, :] = product(step + 1, part)
            place(step, part, even_ref[part : part + part_cells, :])
        return carry

    lax.fori_loop(0, steps // 2, body, 0)
    for part in parts:
        place(steps - 1, part, odd_ref[part : part + part_cells, :])


def value_copies(values_hbm, values_ref, sems):
    width = values_ref.shape[1]
    cuts = [0, width // 8, width // 4, width // 2, width * 3 // 4, width]
    copies = []
    for k in range(len(cuts) - 1):
        lanes = pl.ds(cuts[k], cuts[k + 1] - cuts[k])
        copy = pltpu.make_async_copy(values_hbm.at[:, lanes], values_ref.at[:, lanes], sems.at[k])
        copies.append((cuts[k] // (2 * LANES), copy))
    return copies


def densify_kernel(axes, first, cell_ref, values_hbm, out_ref, values_ref, pick_ref, sems, *held):
    copies = value_copies(values_hbm, values_ref, sems)
    densify_lanes(axes, first, cell_ref, values_ref, pick_ref, out_ref, copies, held)


def densify_apply_kernel(axes, first, cell_ref, values_hbm, *refs):
    blocks, (out_ref, dense_ref, values_ref, pick_ref, sems, *held) = refs[:-7], refs[-7:]
    copies = value_copies(values_hbm, values_ref, sems)
    densify_lanes(axes, first, cell_ref, values_ref, pick_ref, dense_ref, copies, held)
    total = apply_blocks(dense_ref[0].reshape(out_ref.shape[0], -1), blocks)
    out_ref[...] = total.astype(out_ref.dtype)


def apply_blocks(dense, blocks):
    total = None
    depth = blocks[0].shape[0]
    for k, block in enumerate(blocks):
        part = jnp.dot(
            dense[:, k * depth : (k + 1) * depth], block[...], preferred_element_type=jnp.float32
        )
        total = part if total is None else total + part
    return total


def apply_kernel(chunks, dense_ref, *refs):
    for place, out_ref in enumerate(refs[-chunks:]):
        total = apply_blocks(dense_ref[place].reshape(out_ref.shape[0], -1), refs[:-chunks])
        out_ref[...] = total.astype(out_ref.dtype)


IN_VMEM = pl.BlockSpec(memory_space=pltpu.VMEM)
IN_HBM = pl.BlockSpec(memory_space=pltpu.HBM)


def call(kernel, name, out_shape, operands, flops, scratch=(), in_specs=None, limit=VMEM_LIMIT, weigh=2):
    return pl.pallas_call(
        kernel,
        in_specs=in_specs or [IN_VMEM] * len(operands),
        out_specs=jax.tree.map(lambda leaf: IN_VMEM, out_shape),
        out_shape=out_shape,
        scratch_shapes=list(scratch),
        compiler_params=pltpu.CompilerParams(vmem_limit_bytes=limit),
        cost_estimate=pl.CostEstimate(
            flops=weigh * flops,
            bytes_accessed=sum(x.size * x.dtype.itemsize for x in operands),
            transcendentals=0,
        ),
        name=name,
    )(*operands)


def densify(axes, position, cell, values, blocks=(), dtype=None):
    cols_axis, chunk_tiles, chunks = axes
    slots, width = values.shape
    source_rows = cols_axis * chunk_tiles * TILE
    cells = chunks * chunk_tiles * cols_axis * chunk_tiles
    piece = chunk_tiles * TILE
    dense_shape = (chunks, width // LANES, 2 * SUB, source_rows)
    flops = 2 * cells * slots * width
    scratch = [
        pltpu.VMEM(values.shape, values.dtype),
        pltpu.VMEM((cells, slots), jnp.bfloat16),
        pltpu.SemaphoreType.DMA((5,)),
        pltpu.VMEM((cells, 2 * LANES), jnp.float32),
        pltpu.VMEM((cells, 2 * LANES), jnp.float32),
    ]
    in_specs = [IN_VMEM, IN_HBM] + [IN_VMEM] * len(blocks)
    operands = (cell, values, *blocks)
    if not blocks:
        kernel = functools.partial(densify_kernel, axes, position)
        dense = jax.ShapeDtypeStruct(dense_shape, jnp.bfloat16)
        return call(kernel, "densify", dense, operands, flops, scratch, in_specs, FIRST_VMEM_LIMIT)
    kernel = functools.partial(densify_apply_kernel, axes, position)
    scratch = [pltpu.VMEM(dense_shape, jnp.bfloat16)] + scratch
    out = jax.ShapeDtypeStruct((piece, blocks[0].shape[1]), dtype)
    return call(
        kernel, "densify_apply", out, operands, flops, scratch, in_specs, LATER_VMEM_LIMIT, 1
    )


def apply(dense, blocks, dtypes):
    piece = dense.shape[1] * dense.shape[2]
    feat_width = blocks[0].shape[1]
    outs = tuple(jax.ShapeDtypeStruct((piece, feat_width), dtype) for dtype in dtypes)
    flops = 2 * len(outs) * piece * dense.shape[3] * feat_width
    kernel = functools.partial(apply_kernel, len(outs))
    return call(kernel, "apply", outs, (dense, *blocks), flops)


def gather_blocks(features, cols_axis, first):
    swap = [(k, k ^ 1) for k in range(cols_axis)]
    shift = [(k, (k + 2) % cols_axis) for k in range(cols_axis)]
    held = [features]
    for hop in range(1, cols_axis // 2):
        held.append(lax.ppermute(held[-1], "col", shift))
    blocks = [features, lax.ppermute(features, "col", swap)]
    for block in held[1:]:
        block, first = lax.optimization_barrier((block, first))
        blocks += [block, lax.ppermute(block, "col", swap)]
    return blocks, first


def finish_kernel(chunk_tiles, own_ref, *refs):
    weight_ref, bias_ref, out_ref = refs[-3:]
    total = own_ref[...]
    for ref in refs[:-3]:
        total = total + ref[...].astype(jnp.float32)
    hidden = total.astype(jnp.bfloat16)
    mixed = jnp.dot(hidden, weight_ref[...], preferred_element_type=jnp.float32) + bias_ref[...]
    mixed = jnp.maximum(mixed, 0.0)
    mixed = mixed.reshape(TILE, chunk_tiles, mixed.shape[1])
    for k in range(chunk_tiles):
        out_ref[k * TILE : (k + 1) * TILE, :] = mixed[:, k, :].astype(jnp.bfloat16)


def finish(own, received, weight, bias, chunk_tiles):
    kernel = functools.partial(finish_kernel, chunk_tiles)
    out = jax.ShapeDtypeStruct(own.shape, jnp.bfloat16)
    flops = 2 * own.shape[0] * weight.size
    return call(kernel, "finish", out, (own, *received, weight, bias), flops)


def on_device(features, tile_values, tile_rows, tile_cols, counts, weight, bias):
    piece, feat_width = features.shape[1:]
    rows_axis, cols_axis = lax.axis_size("row"), lax.axis_size("col")
    chunk_tiles = piece // TILE
    slots = tile_values.shape[2]
    width = TILE * TILE
    z = lax.axis_index("row")
    cell = cell_ids(
        counts,
        tile_rows.reshape(1, slots),
        tile_cols.reshape(1, slots),
        z,
        lax.axis_index("col"),
        rows_axis,
        cols_axis,
        chunk_tiles,
    )
    values = tile_values.reshape(slots, width)
    axes = (cols_axis, chunk_tiles, 1)

    head = min(2, rows_axis - 1)
    dense = densify((cols_axis, chunk_tiles, head), 0, cell, values)
    blocks, dense = gather_blocks(features.reshape(piece, feat_width), cols_axis, dense)
    if rows_axis == 4:
        near = [(0, 1), (1, 0), (2, 3), (3, 2)]
        inner = (z == 1) | (z == 2)
        part, joined = apply(dense, blocks, (jnp.bfloat16, jnp.float32))
        passed = lax.ppermute(part, "row", near)
        crossed = lax.ppermute(part, "row", [(1, 2), (2, 1)])
        part = densify(axes, 2, cell, values, blocks, jnp.bfloat16)
        joined, part = lax.optimization_barrier((joined, part))
        joined = joined + jnp.where(inner, passed.astype(jnp.float32), 0.0)
        joined, cell = lax.optimization_barrier((joined.astype(jnp.bfloat16), cell))
        far = lax.ppermute(joined, "row", [(0, 2), (1, 3), (2, 0), (3, 1)])
        received = [far, crossed, lax.ppermute(part, "row", near)]
    else:
        received = []
        parts = list(apply(dense, blocks, (jnp.bfloat16,) * head))
        for position in range(rows_axis - 1):
            if position < head:
                part = parts[position]
            else:
                part = densify(axes, position, cell, values, blocks, jnp.bfloat16)
            to = [(d, (d + position + 1) % rows_axis) for d in range(rows_axis)]
            received.append(lax.ppermute(part, "row", to))
    own = densify(axes, rows_axis - 1, cell, values, blocks, jnp.float32)
    bias = bias.reshape(1, feat_width)
    out = finish(own, received, weight, bias, chunk_tiles)
    return out.reshape(1, piece, feat_width)


def solution(mesh):
    in_specs = (
        P(("groups", "row"), "col", None),
        P(("groups", "row"), "col", None, None),
        P(("groups", "row"), "col", None),
        P(("groups", "row"), "col", None),
        P(("groups", "row"), "col"),
        P(),
        P(),
    )
    out_specs = P(("groups", "col"), "row", None)
    return jax.shard_map(
        on_device, mesh=mesh, in_specs=in_specs, out_specs=out_specs, check_vma=False
    )
```

```python
import functools

import jax
import jax.numpy as jnp
from jax import lax
from jax.experimental import pallas as pl
from jax.experimental.pallas import tpu as pltpu
from jax.sharding import PartitionSpec as P

TILE = 64
PRODUCT_ROWS = 512
LANES = 128
SUB = 8
VMEM_LIMIT = 24 * 1024 * 1024
FIRST_VMEM_LIMIT = 46 * 1024 * 1024
LATER_VMEM_LIMIT = 50 * 1024 * 1024


def send_order(chunk, z, rows_axis):
    if rows_axis == 4:
        return 3 - (chunk ^ z)
    order = chunk - z - 1
    return jnp.where(order < 0, order + rows_axis, order)


def cell_ids(counts, rows, cols, z, me, rows_axis, cols_axis, chunk_tiles):
    chunk = rows // chunk_tiles
    local = rows - chunk * chunk_tiles
    order = send_order(chunk, z, rows_axis)
    block = cols // chunk_tiles
    col_local = cols - block * chunk_tiles
    hop = me // 2 - block // 2
    hop = jnp.where(hop < 0, hop + cols_axis // 2, hop)
    near = 2 * hop + jnp.abs(block % 2 - me % 2)
    cell = ((order * cols_axis + near) * chunk_tiles + col_local) * chunk_tiles + local
    slot = lax.broadcasted_iota(jnp.int32, rows.shape, 1)
    return jnp.where(slot < counts, cell, -1)


def densify_lanes(
    axes, first, cell_ref, values_ref, pick_ref, dense_ref, copies, held
):
    cols_axis, chunk_tiles, chunks = axes
    cells, slots = pick_ref.shape
    steps = values_ref.shape[1] // (2 * LANES)
    for begin, copy in copies:
        copy.start()
    cell = cell_ref[...] - first * (cells // chunks)
    index = lax.broadcasted_iota(jnp.int32, (cells, slots), 0)
    pick_ref[...] = jnp.where(index == cell, 1.0, 0.0).astype(pick_ref.dtype)

    part_cells = 256
    product_cells = min(PRODUCT_ROWS, cells)
    per_chunk = cells // chunks
    halves = part_cells // (2 * SUB)
    low = lax.broadcasted_iota(jnp.int32, (halves, SUB, LANES), 2) < TILE

    def product(step, part):
        lane = pl.multiple_of(step * 2 * LANES, 2 * LANES)
        return jnp.dot(
            pick_ref[part : part + product_cells, :],
            values_ref[:, pl.ds(lane, 2 * LANES)],
            preferred_element_type=jnp.float32,
        )

    def place(step, part, summed):
        chunk, column = divmod(part, per_chunk)
        for pair in range(2):
            block = summed[:, pair * LANES : (pair + 1) * LANES]
            block = block.reshape(halves, 2, SUB, LANES)
            left, right = block[:, 0], block[:, 1]
            even = jnp.where(low, left, pltpu.roll(right, TILE, 2))
            odd = jnp.where(low, pltpu.roll(left, TILE, 2), right)
            both = jnp.concatenate([even, odd], axis=1).astype(jnp.bfloat16)
            for k in range(halves):
                lanes = pl.ds((column // (2 * SUB) + k) * LANES, LANES)
                dense_ref[chunk, 2 * step + pair, :, lanes] = both[k]

    def await_copies(step):
        for begin, copy in copies:
            pl.when(step == begin)(copy.wait)

    parts = range(0, cells, part_cells)
    even_ref, odd_ref = held

    def body(turn, carry):
        step = 2 * turn
        await_copies(step)
        before = jnp.maximum(step - 1, 0)
        for part in range(0, cells, product_cells):
            even_ref[part : part + product_cells, :] = product(step, part)
            for piece in range(part, part + product_cells, part_cells):
                place(before, piece, odd_ref[piece : piece + part_cells, :])
        for part in range(0, cells, product_cells):
            odd_ref[part : part + product_cells, :] = product(step + 1, part)
            for piece in range(part, part + product_cells, part_cells):
                place(step, piece, even_ref[piece : piece + part_cells, :])
        return carry

    lax.fori_loop(0, steps // 2, body, 0)
    for part in parts:
        place(steps - 1, part, odd_ref[part : part + part_cells, :])


def value_copies(values_hbm, values_ref, sems, lane=0):
    width = values_ref.shape[1]
    cuts = [0, 512] + list(range(1024, width + 1, 1024))
    copies = []
    for k in range(len(cuts) - 1):
        size = cuts[k + 1] - cuts[k]
        copy = pltpu.make_async_copy(
            values_hbm.at[:, pl.ds(lane + cuts[k], size)],
            values_ref.at[:, pl.ds(cuts[k], size)],
            sems.at[k],
        )
        copies.append((cuts[k] // (2 * LANES), copy))
    return copies


def densify_kernel(
    axes, first, lane, cell_ref, values_hbm, out_ref, values_ref, pick_ref, sems, *held
):
    copies = value_copies(values_hbm, values_ref, sems, lane)
    densify_lanes(axes, first, cell_ref, values_ref, pick_ref, out_ref, copies, held)


def densify_apply_kernel(axes, first, cell_ref, values_hbm, *refs):
    blocks, (out_ref, dense_ref, values_ref, pick_ref, sems, *held) = refs[:-7], refs[-7:]
    copies = value_copies(values_hbm, values_ref, sems)
    densify_lanes(axes, first, cell_ref, values_ref, pick_ref, dense_ref, copies, held)
    total = apply_blocks(dense_ref[0].reshape(out_ref.shape[0], -1), blocks)
    out_ref[...] = total.astype(out_ref.dtype)


def apply_blocks(dense, blocks):
    total = None
    depth = blocks[0].shape[0]
    for k, block in enumerate(blocks):
        part = jnp.dot(
            dense[:, k * depth : (k + 1) * depth], block[...], preferred_element_type=jnp.float32
        )
        total = part if total is None else total + part
    return total


def apply_kernel(parts, chunks, *refs):
    outs, blocks = refs[-chunks:], refs[parts:-chunks]
    for place, out_ref in enumerate(outs):
        row = 0
        for dense_ref in refs[:parts]:
            rows = dense_ref.shape[1] * dense_ref.shape[2]
            total = apply_blocks(dense_ref[place].reshape(rows, -1), blocks)
            out_ref[row : row + rows, :] = total.astype(out_ref.dtype)
            row += rows


IN_VMEM = pl.BlockSpec(memory_space=pltpu.VMEM)
IN_HBM = pl.BlockSpec(memory_space=pltpu.HBM)


def call(kernel, name, out_shape, operands, flops, scratch=(), in_specs=None, limit=VMEM_LIMIT, weigh=2):
    return pl.pallas_call(
        kernel,
        in_specs=in_specs or [IN_VMEM] * len(operands),
        out_specs=jax.tree.map(lambda leaf: IN_VMEM, out_shape),
        out_shape=out_shape,
        scratch_shapes=list(scratch),
        compiler_params=pltpu.CompilerParams(vmem_limit_bytes=limit),
        cost_estimate=pl.CostEstimate(
            flops=weigh * flops,
            bytes_accessed=sum(x.size * x.dtype.itemsize for x in operands),
            transcendentals=0,
        ),
        name=name,
    )(*operands)


def densify(axes, position, cell, values, blocks=(), dtype=None, lanes=None):
    cols_axis, chunk_tiles, chunks = axes
    slots = values.shape[0]
    lane, end = lanes or (0, values.shape[1])
    width = end - lane
    source_rows = cols_axis * chunk_tiles * TILE
    cells = chunks * chunk_tiles * cols_axis * chunk_tiles
    piece = chunk_tiles * TILE
    dense_shape = (chunks, width // LANES, 2 * SUB, source_rows)
    flops = 2 * cells * slots * width
    scratch = [
        pltpu.VMEM((slots, width), values.dtype),
        pltpu.VMEM((cells, slots), jnp.bfloat16),
        pltpu.SemaphoreType.DMA((5,)),
        pltpu.VMEM((cells, 2 * LANES), jnp.float32),
        pltpu.VMEM((cells, 2 * LANES), jnp.float32),
    ]
    in_specs = [IN_VMEM, IN_HBM] + [IN_VMEM] * len(blocks)
    operands = (cell, values, *blocks)
    if not blocks:
        kernel = functools.partial(densify_kernel, axes, position, lane)
        dense = jax.ShapeDtypeStruct(dense_shape, jnp.bfloat16)
        return call(kernel, "densify", dense, operands, flops, scratch, in_specs, FIRST_VMEM_LIMIT)
    kernel = functools.partial(densify_apply_kernel, axes, position)
    scratch = [pltpu.VMEM(dense_shape, jnp.bfloat16)] + scratch
    out = jax.ShapeDtypeStruct((piece, blocks[0].shape[1]), dtype)
    return call(
        kernel, "densify_apply", out, operands, flops, scratch, in_specs, LATER_VMEM_LIMIT, 1
    )


def apply(dense, blocks, dtypes):
    piece = sum(part.shape[1] * part.shape[2] for part in dense)
    feat_width = blocks[0].shape[1]
    outs = tuple(jax.ShapeDtypeStruct((piece, feat_width), dtype) for dtype in dtypes)
    flops = 2 * len(outs) * piece * dense[0].shape[3] * feat_width
    kernel = functools.partial(apply_kernel, len(dense), len(outs))
    return call(kernel, "apply", outs, (*dense, *blocks), flops)


def gather_blocks(features, cols_axis, first):
    swap = [(k, k ^ 1) for k in range(cols_axis)]
    shift = [(k, (k + 2) % cols_axis) for k in range(cols_axis)]
    held = [features]
    for hop in range(1, cols_axis // 2):
        held.append(lax.ppermute(held[-1], "col", shift))
    blocks = [features, lax.ppermute(features, "col", swap)]
    for block in held[1:]:
        block, first = lax.optimization_barrier((block, first))
        blocks += [block, lax.ppermute(block, "col", swap)]
    return blocks, first


def finish_kernel(chunk_tiles, own_ref, *refs):
    weight_ref, bias_ref, out_ref = refs[-3:]
    total = own_ref[...]
    for ref in refs[:-3]:
        total = total + ref[...].astype(jnp.float32)
    hidden = total.astype(jnp.bfloat16)
    mixed = jnp.dot(hidden, weight_ref[...], preferred_element_type=jnp.float32) + bias_ref[...]
    mixed = jnp.maximum(mixed, 0.0)
    mixed = mixed.reshape(TILE, chunk_tiles, mixed.shape[1])
    for k in range(chunk_tiles):
        out_ref[k * TILE : (k + 1) * TILE, :] = mixed[:, k, :].astype(jnp.bfloat16)


def finish(own, received, weight, bias, chunk_tiles):
    kernel = functools.partial(finish_kernel, chunk_tiles)
    out = jax.ShapeDtypeStruct(own.shape, jnp.bfloat16)
    flops = 2 * own.shape[0] * weight.size
    return call(kernel, "finish", out, (own, *received, weight, bias), flops)


def on_device(features, tile_values, tile_rows, tile_cols, counts, weight, bias):
    piece, feat_width = features.shape[1:]
    rows_axis, cols_axis = lax.axis_size("row"), lax.axis_size("col")
    chunk_tiles = piece // TILE
    slots = tile_values.shape[2]
    width = TILE * TILE
    z = lax.axis_index("row")
    cell = cell_ids(
        counts,
        tile_rows.reshape(1, slots),
        tile_cols.reshape(1, slots),
        z,
        lax.axis_index("col"),
        rows_axis,
        cols_axis,
        chunk_tiles,
    )
    values = tile_values.reshape(slots, width)
    axes = (cols_axis, chunk_tiles, 1)

    head = min(2, rows_axis - 1)
    head_axes = (cols_axis, chunk_tiles, head)
    cut = width * 3 // 4
    dense = densify(head_axes, 0, cell, values, lanes=(0, cut))
    blocks, dense = gather_blocks(features.reshape(piece, feat_width), cols_axis, dense)
    dense = (dense, densify(head_axes, 0, cell, values, lanes=(cut, width)))
    if rows_axis == 4:
        near = [(0, 1), (1, 0), (2, 3), (3, 2)]
        inner = (z == 1) | (z == 2)
        part, joined = apply(dense, blocks, (jnp.bfloat16, jnp.float32))
        passed = lax.ppermute(part, "row", near)
        crossed = lax.ppermute(part, "row", [(1, 2), (2, 1)])
        part = densify(axes, 2, cell, values, blocks, jnp.bfloat16)
        joined, part = lax.optimization_barrier((joined, part))
        joined = joined + jnp.where(inner, passed.astype(jnp.float32), 0.0)
        joined, cell = lax.optimization_barrier((joined.astype(jnp.bfloat16), cell))
        far = lax.ppermute(joined, "row", [(0, 2), (1, 3), (2, 0), (3, 1)])
        received = [far, crossed, lax.ppermute(part, "row", near)]
    else:
        received = []
        parts = list(apply(dense, blocks, (jnp.bfloat16,) * head))
        for position in range(rows_axis - 1):
            if position < head:
                part = parts[position]
            else:
                part = densify(axes, position, cell, values, blocks, jnp.bfloat16)
            to = [(d, (d + position + 1) % rows_axis) for d in range(rows_axis)]
            received.append(lax.ppermute(part, "row", to))
    own = densify(axes, rows_axis - 1, cell, values, blocks, jnp.float32)
    bias = bias.reshape(1, feat_width)
    out = finish(own, received, weight, bias, chunk_tiles)
    return out.reshape(1, piece, feat_width)


def solution(mesh):
    in_specs = (
        P(("groups", "row"), "col", None),
        P(("groups", "row"), "col", None, None),
        P(("groups", "row"), "col", None),
        P(("groups", "row"), "col", None),
        P(("groups", "row"), "col"),
        P(),
        P(),
    )
    out_specs = P(("groups", "col"), "row", None)
    return jax.shard_map(
        on_device, mesh=mesh, in_specs=in_specs, out_specs=out_specs, check_vma=False
    )
```

```python
import functools

import jax
import jax.numpy as jnp
from jax import lax
from jax.experimental import pallas as pl
from jax.experimental.pallas import tpu as pltpu
from jax.sharding import PartitionSpec as P

TILE = 64
LANES = 128
SUB = 8
VMEM_LIMIT = 24 * 1024 * 1024
FIRST_VMEM_LIMIT = 46 * 1024 * 1024
LATER_VMEM_LIMIT = 50 * 1024 * 1024


def send_order(chunk, z, rows_axis):
    if rows_axis == 4:
        apart = chunk ^ z
        between = (apart == 1) | (apart == 2)
        return jnp.where(((z == 1) | (z == 2)) & between, apart, 3 - apart)
    order = chunk - z - 1
    return jnp.where(order < 0, order + rows_axis, order)


def cell_ids(counts, rows, cols, z, me, rows_axis, cols_axis, chunk_tiles):
    chunk = rows // chunk_tiles
    local = rows - chunk * chunk_tiles
    order = send_order(chunk, z, rows_axis)
    block = cols // chunk_tiles
    col_local = cols - block * chunk_tiles
    hop = me // 2 - block // 2
    hop = jnp.where(hop < 0, hop + cols_axis // 2, hop)
    near = 2 * hop + jnp.abs(block % 2 - me % 2)
    cell = ((order * cols_axis + near) * chunk_tiles + col_local) * chunk_tiles + local
    slot = lax.broadcasted_iota(jnp.int32, rows.shape, 1)
    return jnp.where(slot < counts, cell, -1)


def densify_lanes(
    axes, first, cell_ref, values_ref, pick_ref, dense_ref, copies, held
):
    cols_axis, chunk_tiles, chunks = axes
    cells, slots = pick_ref.shape
    steps = values_ref.shape[1] // (2 * LANES)
    for begin, copy in copies:
        copy.start()
    cell = cell_ref[...] - first * (cells // chunks)
    index = lax.broadcasted_iota(jnp.int32, (cells, slots), 0)
    pick_ref[...] = jnp.where(index == cell, 1.0, 0.0).astype(pick_ref.dtype)

    part_cells = 256
    per_chunk = cells // chunks
    halves = part_cells // (2 * SUB)
    low = lax.broadcasted_iota(jnp.int32, (halves, SUB, LANES), 2) < TILE

    def product(step, part):
        lane = pl.multiple_of(step * 2 * LANES, 2 * LANES)
        return jnp.dot(
            pick_ref[part : part + part_cells, :],
            values_ref[:, pl.ds(lane, 2 * LANES)],
            preferred_element_type=jnp.float32,
        )

    def place(step, part, summed):
        chunk, column = divmod(part, per_chunk)
        for pair in range(2):
            block = summed[:, pair * LANES : (pair + 1) * LANES]
            block = block.reshape(halves, 2, SUB, LANES)
            left, right = block[:, 0], block[:, 1]
            even = jnp.where(low, left, pltpu.roll(right, TILE, 2))
            odd = jnp.where(low, pltpu.roll(left, TILE, 2), right)
            both = jnp.concatenate([even, odd], axis=1).astype(jnp.bfloat16)
            for k in range(halves):
                lanes = pl.ds((column // (2 * SUB) + k) * LANES, LANES)
                dense_ref[chunk, 2 * step + pair, :, lanes] = both[k]

    def await_copies(step):
        for begin, copy in copies:
            pl.when(step == begin)(copy.wait)

    parts = range(0, cells, part_cells)
    even_ref, odd_ref = held

    def body(turn, carry):
        step = 2 * turn
        await_copies(step)
        before = jnp.maximum(step - 1, 0)
        for part in parts:
            even_ref[part : part + part_cells, :] = product(step, part)
            place(before, part, odd_ref[part : part + part_cells, :])
        for part in parts:
            odd_ref[part : part + part_cells, :] = product(step + 1, part)
            place(step, part, even_ref[part : part + part_cells, :])
        return carry

    lax.fori_loop(0, steps // 2, body, 0)
    for part in parts:
        place(steps - 1, part, odd_ref[part : part + part_cells, :])


def value_copies(values_hbm, values_ref, sems):
    width = values_ref.shape[1]
    cuts = [0, width // 8, width // 4, width // 2, width * 3 // 4, width]
    copies = []
    for k in range(len(cuts) - 1):
        lanes = pl.ds(cuts[k], cuts[k + 1] - cuts[k])
        copy = pltpu.make_async_copy(values_hbm.at[:, lanes], values_ref.at[:, lanes], sems.at[k])
        copies.append((cuts[k] // (2 * LANES), copy))
    return copies


def densify_kernel(axes, first, cell_ref, values_hbm, out_ref, values_ref, pick_ref, sems, *held):
    copies = value_copies(values_hbm, values_ref, sems)
    densify_lanes(axes, first, cell_ref, values_ref, pick_ref, out_ref, copies, held)


def densify_apply_kernel(axes, first, cell_ref, values_hbm, *refs):
    blocks, (out_ref, dense_ref, values_ref, pick_ref, sems, *held) = refs[:-7], refs[-7:]
    copies = value_copies(values_hbm, values_ref, sems)
    densify_lanes(axes, first, cell_ref, values_ref, pick_ref, dense_ref, copies, held)
    total = apply_blocks(dense_ref[0].reshape(out_ref.shape[0], -1), blocks)
    out_ref[...] = total.astype(out_ref.dtype)


def apply_blocks(dense, blocks):
    total = None
    depth = blocks[0].shape[0]
    for k, block in enumerate(blocks):
        part = jnp.dot(
            dense[:, k * depth : (k + 1) * depth], block[...], preferred_element_type=jnp.float32
        )
        total = part if total is None else total + part
    return total


def apply_kernel(chunks, dense_ref, *refs):
    for place, out_ref in enumerate(refs[-chunks:]):
        total = apply_blocks(dense_ref[place].reshape(out_ref.shape[0], -1), refs[:-chunks])
        out_ref[...] = total.astype(out_ref.dtype)


IN_VMEM = pl.BlockSpec(memory_space=pltpu.VMEM)
IN_HBM = pl.BlockSpec(memory_space=pltpu.HBM)


def call(kernel, name, out_shape, operands, flops, scratch=(), in_specs=None, limit=VMEM_LIMIT, weigh=2):
    return pl.pallas_call(
        kernel,
        in_specs=in_specs or [IN_VMEM] * len(operands),
        out_specs=jax.tree.map(lambda leaf: IN_VMEM, out_shape),
        out_shape=out_shape,
        scratch_shapes=list(scratch),
        compiler_params=pltpu.CompilerParams(vmem_limit_bytes=limit),
        cost_estimate=pl.CostEstimate(
            flops=weigh * flops,
            bytes_accessed=sum(x.size * x.dtype.itemsize for x in operands),
            transcendentals=0,
        ),
        name=name,
    )(*operands)


def densify(axes, position, cell, values, blocks=(), dtype=None):
    cols_axis, chunk_tiles, chunks = axes
    slots, width = values.shape
    source_rows = cols_axis * chunk_tiles * TILE
    cells = chunks * chunk_tiles * cols_axis * chunk_tiles
    piece = chunk_tiles * TILE
    dense_shape = (chunks, width // LANES, 2 * SUB, source_rows)
    flops = 2 * cells * slots * width
    scratch = [
        pltpu.VMEM(values.shape, values.dtype),
        pltpu.VMEM((cells, slots), jnp.bfloat16),
        pltpu.SemaphoreType.DMA((5,)),
        pltpu.VMEM((cells, 2 * LANES), jnp.float32),
        pltpu.VMEM((cells, 2 * LANES), jnp.float32),
    ]
    in_specs = [IN_VMEM, IN_HBM] + [IN_VMEM] * len(blocks)
    operands = (cell, values, *blocks)
    if not blocks:
        kernel = functools.partial(densify_kernel, axes, position)
        dense = jax.ShapeDtypeStruct(dense_shape, jnp.bfloat16)
        return call(kernel, "densify", dense, operands, flops, scratch, in_specs, FIRST_VMEM_LIMIT)
    kernel = functools.partial(densify_apply_kernel, axes, position)
    scratch = [pltpu.VMEM(dense_shape, jnp.bfloat16)] + scratch
    out = jax.ShapeDtypeStruct((piece, blocks[0].shape[1]), dtype)
    return call(
        kernel, "densify_apply", out, operands, flops, scratch, in_specs, LATER_VMEM_LIMIT, 1
    )


def apply(dense, blocks, dtypes):
    piece = dense.shape[1] * dense.shape[2]
    feat_width = blocks[0].shape[1]
    outs = tuple(jax.ShapeDtypeStruct((piece, feat_width), dtype) for dtype in dtypes)
    flops = 2 * len(outs) * piece * dense.shape[3] * feat_width
    kernel = functools.partial(apply_kernel, len(outs))
    return call(kernel, "apply", outs, (dense, *blocks), flops)


def gather_blocks(features, cols_axis, first):
    swap = [(k, k ^ 1) for k in range(cols_axis)]
    shift = [(k, (k + 2) % cols_axis) for k in range(cols_axis)]
    held = [features]
    for hop in range(1, cols_axis // 2):
        held.append(lax.ppermute(held[-1], "col", shift))
    blocks = [features, lax.ppermute(features, "col", swap)]
    for block in held[1:]:
        block, first = lax.optimization_barrier((block, first))
        blocks += [block, lax.ppermute(block, "col", swap)]
    return blocks, first


def finish_kernel(chunk_tiles, own_ref, *refs):
    weight_ref, bias_ref, out_ref = refs[-3:]
    total = own_ref[...]
    for ref in refs[:-3]:
        total = total + ref[...].astype(jnp.float32)
    hidden = total.astype(jnp.bfloat16)
    mixed = jnp.dot(hidden, weight_ref[...], preferred_element_type=jnp.float32) + bias_ref[...]
    mixed = jnp.maximum(mixed, 0.0)
    mixed = mixed.reshape(TILE, chunk_tiles, mixed.shape[1])
    for k in range(chunk_tiles):
        out_ref[k * TILE : (k + 1) * TILE, :] = mixed[:, k, :].astype(jnp.bfloat16)


def finish(own, received, weight, bias, chunk_tiles):
    kernel = functools.partial(finish_kernel, chunk_tiles)
    out = jax.ShapeDtypeStruct(own.shape, jnp.bfloat16)
    flops = 2 * own.shape[0] * weight.size
    return call(kernel, "finish", out, (own, *received, weight, bias), flops)


def on_device(features, tile_values, tile_rows, tile_cols, counts, weight, bias):
    piece, feat_width = features.shape[1:]
    rows_axis, cols_axis = lax.axis_size("row"), lax.axis_size("col")
    chunk_tiles = piece // TILE
    slots = tile_values.shape[2]
    width = TILE * TILE
    z = lax.axis_index("row")
    cell = cell_ids(
        counts,
        tile_rows.reshape(1, slots),
        tile_cols.reshape(1, slots),
        z,
        lax.axis_index("col"),
        rows_axis,
        cols_axis,
        chunk_tiles,
    )
    values = tile_values.reshape(slots, width)
    axes = (cols_axis, chunk_tiles, 1)

    head = min(2, rows_axis - 1)
    dense = densify((cols_axis, chunk_tiles, head), 0, cell, values)
    blocks, dense = gather_blocks(features.reshape(piece, feat_width), cols_axis, dense)
    if rows_axis == 4:
        near = [(0, 1), (1, 0), (2, 3), (3, 2)]
        inner = (z == 1) | (z == 2)
        part, second = apply(dense, blocks, (jnp.bfloat16, jnp.bfloat16))
        passed = lax.ppermute(part, "row", near)
        crossed = lax.ppermute(part, "row", [(1, 2), (2, 1)])
        early = lax.ppermute(second, "row", [(0, 2), (3, 1), (1, 0), (2, 3)])
        joined = densify(axes, 2, cell, values, blocks, jnp.float32)
        joined = joined + jnp.where(inner, passed.astype(jnp.float32), 0.0)
        joined, cell = lax.optimization_barrier((joined.astype(jnp.bfloat16), cell))
        late = lax.ppermute(joined, "row", [(0, 1), (3, 2), (1, 3), (2, 0)])
        received = [late, crossed, early]
    else:
        received = []
        parts = list(apply(dense, blocks, (jnp.bfloat16,) * head))
        for position in range(rows_axis - 1):
            if position < head:
                part = parts[position]
            else:
                part = densify(axes, position, cell, values, blocks, jnp.bfloat16)
            to = [(d, (d + position + 1) % rows_axis) for d in range(rows_axis)]
            received.append(lax.ppermute(part, "row", to))
    own = densify(axes, rows_axis - 1, cell, values, blocks, jnp.float32)
    bias = bias.reshape(1, feat_width)
    out = finish(own, received, weight, bias, chunk_tiles)
    return out.reshape(1, piece, feat_width)


def solution(mesh):
    in_specs = (
        P(("groups", "row"), "col", None),
        P(("groups", "row"), "col", None, None),
        P(("groups", "row"), "col", None),
        P(("groups", "row"), "col", None),
        P(("groups", "row"), "col"),
        P(),
        P(),
    )
    out_specs = P(("groups", "col"), "row", None)
    return jax.shard_map(
        on_device, mesh=mesh, in_specs=in_specs, out_specs=out_specs, check_vma=False
    )
```

```python
import functools

import jax
import jax.numpy as jnp
from jax import lax
from jax.experimental import pallas as pl
from jax.experimental.pallas import tpu as pltpu
from jax.sharding import PartitionSpec as P

TILE = 64
LANES = 128
SUB = 8
VMEM_LIMIT = 24 * 1024 * 1024
FIRST_VMEM_LIMIT = 46 * 1024 * 1024
LATER_VMEM_LIMIT = 50 * 1024 * 1024


def send_order(chunk, z, rows_axis):
    if rows_axis == 4:
        apart = chunk ^ z
        between = (apart == 1) | (apart == 2)
        return jnp.where(((z == 1) | (z == 2)) & between, apart, 3 - apart)
    order = chunk - z - 1
    return jnp.where(order < 0, order + rows_axis, order)


def cell_ids(counts, rows, cols, z, me, rows_axis, cols_axis, chunk_tiles):
    chunk = rows // chunk_tiles
    local = rows - chunk * chunk_tiles
    order = send_order(chunk, z, rows_axis)
    block = cols // chunk_tiles
    col_local = cols - block * chunk_tiles
    hop = me // 2 - block // 2
    hop = jnp.where(hop < 0, hop + cols_axis // 2, hop)
    near = 2 * hop + jnp.abs(block % 2 - me % 2)
    cell = ((order * cols_axis + near) * chunk_tiles + col_local) * chunk_tiles + local
    slot = lax.broadcasted_iota(jnp.int32, rows.shape, 1)
    return jnp.where(slot < counts, cell, -1)


def densify_lanes(
    axes, first, cell_ref, values_ref, pick_ref, dense_ref, copies, held
):
    cols_axis, chunk_tiles, chunks = axes
    cells, slots = pick_ref.shape
    steps = values_ref.shape[1] // (2 * LANES)
    for begin, copy in copies:
        copy.start()
    cell = cell_ref[...] - first * (cells // chunks)
    index = lax.broadcasted_iota(jnp.int32, (cells, slots), 0)
    pick_ref[...] = jnp.where(index == cell, 1.0, 0.0).astype(pick_ref.dtype)

    part_cells = 256
    per_chunk = cells // chunks
    halves = part_cells // (2 * SUB)
    low = lax.broadcasted_iota(jnp.int32, (halves, SUB, LANES), 2) < TILE

    def product(step, part):
        lane = pl.multiple_of(step * 2 * LANES, 2 * LANES)
        return jnp.dot(
            pick_ref[part : part + part_cells, :],
            values_ref[:, pl.ds(lane, 2 * LANES)],
            preferred_element_type=jnp.float32,
        )

    def place(step, part, summed):
        chunk, column = divmod(part, per_chunk)
        for pair in range(2):
            block = summed[:, pair * LANES : (pair + 1) * LANES]
            block = block.reshape(halves, 2, SUB, LANES)
            left, right = block[:, 0], block[:, 1]
            even = jnp.where(low, left, pltpu.roll(right, TILE, 2))
            odd = jnp.where(low, pltpu.roll(left, TILE, 2), right)
            both = jnp.concatenate([even, odd], axis=1).astype(jnp.bfloat16)
            for k in range(halves):
                lanes = pl.ds((column // (2 * SUB) + k) * LANES, LANES)
                dense_ref[chunk, 2 * step + pair, :, lanes] = both[k]

    def await_copies(step):
        for begin, copy in copies:
            pl.when(step == begin)(copy.wait)

    parts = range(0, cells, part_cells)
    even_ref, odd_ref = held

    def body(turn, carry):
        step = 2 * turn
        await_copies(step)
        before = jnp.maximum(step - 1, 0)
        for part in parts:
            even_ref[part : part + part_cells, :] = product(step, part)
            place(before, part, odd_ref[part : part + part_cells, :])
        for part in parts:
            odd_ref[part : part + part_cells, :] = product(step + 1, part)
            place(step, part, even_ref[part : part + part_cells, :])
        return carry

    lax.fori_loop(0, steps // 2, body, 0)
    for part in parts:
        place(steps - 1, part, odd_ref[part : part + part_cells, :])


def value_copies(values_hbm, values_ref, sems):
    width = values_ref.shape[1]
    cuts = [0, width // 8, width // 4, width // 2, width * 3 // 4, width]
    copies = []
    for k in range(len(cuts) - 1):
        lanes = pl.ds(cuts[k], cuts[k + 1] - cuts[k])
        copy = pltpu.make_async_copy(values_hbm.at[:, lanes], values_ref.at[:, lanes], sems.at[k])
        copies.append((cuts[k] // (2 * LANES), copy))
    return copies


def densify_kernel(axes, first, cell_ref, values_hbm, out_ref, values_ref, pick_ref, sems, *held):
    copies = value_copies(values_hbm, values_ref, sems)
    densify_lanes(axes, first, cell_ref, values_ref, pick_ref, out_ref, copies, held)


def densify_apply_kernel(axes, first, cell_ref, values_hbm, *refs):
    blocks, (out_ref, dense_ref, values_ref, pick_ref, sems, *held) = refs[:-7], refs[-7:]
    copies = value_copies(values_hbm, values_ref, sems)
    densify_lanes(axes, first, cell_ref, values_ref, pick_ref, dense_ref, copies, held)
    total = apply_blocks(dense_ref[0].reshape(out_ref.shape[0], -1), blocks)
    out_ref[...] = total.astype(out_ref.dtype)


def apply_blocks(dense, blocks):
    total = None
    depth = blocks[0].shape[0]
    for k, block in enumerate(blocks):
        part = jnp.dot(
            dense[:, k * depth : (k + 1) * depth], block[...], preferred_element_type=jnp.float32
        )
        total = part if total is None else total + part
    return total


def apply_kernel(chunks, dense_ref, *refs):
    for place, out_ref in enumerate(refs[-chunks:]):
        total = apply_blocks(dense_ref[place].reshape(out_ref.shape[0], -1), refs[:-chunks])
        out_ref[...] = total.astype(out_ref.dtype)


IN_VMEM = pl.BlockSpec(memory_space=pltpu.VMEM)
IN_HBM = pl.BlockSpec(memory_space=pltpu.HBM)


def call(kernel, name, out_shape, operands, flops, scratch=(), in_specs=None, limit=VMEM_LIMIT, weigh=2):
    return pl.pallas_call(
        kernel,
        in_specs=in_specs or [IN_VMEM] * len(operands),
        out_specs=jax.tree.map(lambda leaf: IN_VMEM, out_shape),
        out_shape=out_shape,
        scratch_shapes=list(scratch),
        compiler_params=pltpu.CompilerParams(vmem_limit_bytes=limit),
        cost_estimate=pl.CostEstimate(
            flops=weigh * flops,
            bytes_accessed=sum(x.size * x.dtype.itemsize for x in operands),
            transcendentals=0,
        ),
        name=name,
    )(*operands)


def densify(axes, position, cell, values, blocks=(), dtype=None):
    cols_axis, chunk_tiles, chunks = axes
    slots, width = values.shape
    source_rows = cols_axis * chunk_tiles * TILE
    cells = chunks * chunk_tiles * cols_axis * chunk_tiles
    piece = chunk_tiles * TILE
    dense_shape = (chunks, width // LANES, 2 * SUB, source_rows)
    flops = 2 * cells * slots * width
    scratch = [
        pltpu.VMEM(values.shape, values.dtype),
        pltpu.VMEM((cells, slots), jnp.bfloat16),
        pltpu.SemaphoreType.DMA((5,)),
        pltpu.VMEM((cells, 2 * LANES), jnp.float32),
        pltpu.VMEM((cells, 2 * LANES), jnp.float32),
    ]
    in_specs = [IN_VMEM, IN_HBM] + [IN_VMEM] * len(blocks)
    operands = (cell, values, *blocks)
    if not blocks:
        kernel = functools.partial(densify_kernel, axes, position)
        dense = jax.ShapeDtypeStruct(dense_shape, jnp.bfloat16)
        return call(kernel, "densify", dense, operands, flops, scratch, in_specs, FIRST_VMEM_LIMIT)
    kernel = functools.partial(densify_apply_kernel, axes, position)
    scratch = [pltpu.VMEM(dense_shape, jnp.bfloat16)] + scratch
    out = jax.ShapeDtypeStruct((piece, blocks[0].shape[1]), dtype)
    return call(
        kernel, "densify_apply", out, operands, flops, scratch, in_specs, LATER_VMEM_LIMIT, 1
    )


def apply(dense, blocks, dtypes):
    piece = dense.shape[1] * dense.shape[2]
    feat_width = blocks[0].shape[1]
    outs = tuple(jax.ShapeDtypeStruct((piece, feat_width), dtype) for dtype in dtypes)
    flops = 2 * len(outs) * piece * dense.shape[3] * feat_width
    kernel = functools.partial(apply_kernel, len(outs))
    return call(kernel, "apply", outs, (dense, *blocks), flops)


def gather_blocks(features, cols_axis, first):
    swap = [(k, k ^ 1) for k in range(cols_axis)]
    shift = [(k, (k + 2) % cols_axis) for k in range(cols_axis)]
    held = [features]
    for hop in range(1, cols_axis // 2):
        held.append(lax.ppermute(held[-1], "col", shift))
    blocks = [features, lax.ppermute(features, "col", swap)]
    for block in held[1:]:
        block, first = lax.optimization_barrier((block, first))
        blocks += [block, lax.ppermute(block, "col", swap)]
    return blocks, first


def finish_kernel(chunk_tiles, own_ref, *refs):
    weight_ref, bias_ref, out_ref = refs[-3:]
    total = own_ref[...]
    for ref in refs[:-3]:
        total = total + ref[...].astype(jnp.float32)
    hidden = total.astype(jnp.bfloat16)
    mixed = jnp.dot(hidden, weight_ref[...], preferred_element_type=jnp.float32) + bias_ref[...]
    mixed = jnp.maximum(mixed, 0.0)
    mixed = mixed.reshape(TILE, chunk_tiles, mixed.shape[1])
    for k in range(chunk_tiles):
        out_ref[k * TILE : (k + 1) * TILE, :] = mixed[:, k, :].astype(jnp.bfloat16)


def finish(own, received, weight, bias, chunk_tiles):
    kernel = functools.partial(finish_kernel, chunk_tiles)
    out = jax.ShapeDtypeStruct(own.shape, jnp.bfloat16)
    flops = 2 * own.shape[0] * weight.size
    return call(kernel, "finish", out, (own, *received, weight, bias), flops)


def on_device(features, tile_values, tile_rows, tile_cols, counts, weight, bias):
    piece, feat_width = features.shape[1:]
    rows_axis, cols_axis = lax.axis_size("row"), lax.axis_size("col")
    chunk_tiles = piece // TILE
    slots = tile_values.shape[2]
    width = TILE * TILE
    z = lax.axis_index("row")
    cell = cell_ids(
        counts,
        tile_rows.reshape(1, slots),
        tile_cols.reshape(1, slots),
        z,
        lax.axis_index("col"),
        rows_axis,
        cols_axis,
        chunk_tiles,
    )
    values = tile_values.reshape(slots, width)
    axes = (cols_axis, chunk_tiles, 1)

    head = min(2, rows_axis - 1)
    dense = densify((cols_axis, chunk_tiles, head), 0, cell, values)
    blocks, dense = gather_blocks(features.reshape(piece, feat_width), cols_axis, dense)
    if rows_axis == 4:
        inner = (z == 1) | (z == 2)
        part, second = apply(dense, blocks, (jnp.bfloat16, jnp.bfloat16))
        passed = lax.ppermute(part, "row", [(0, 1), (3, 2)])
        crossed = lax.ppermute(part, "row", [(1, 2), (2, 1)])
        early = lax.ppermute(second, "row", [(0, 2), (3, 1), (1, 0), (2, 3)])
        joined = densify(axes, 2, cell, values, blocks, jnp.float32)
        joined = joined + jnp.where(inner, passed.astype(jnp.float32), 0.0)
        joined, cell = lax.optimization_barrier((joined.astype(jnp.bfloat16), cell))
        late = lax.ppermute(joined, "row", [(0, 1), (3, 2), (1, 3), (2, 0)])
        received = [late, crossed, early]
    else:
        received = []
        parts = list(apply(dense, blocks, (jnp.bfloat16,) * head))
        for position in range(rows_axis - 1):
            if position < head:
                part = parts[position]
            else:
                part = densify(axes, position, cell, values, blocks, jnp.bfloat16)
            to = [(d, (d + position + 1) % rows_axis) for d in range(rows_axis)]
            received.append(lax.ppermute(part, "row", to))
    own = densify(axes, rows_axis - 1, cell, values, blocks, jnp.float32)
    bias = bias.reshape(1, feat_width)
    out = finish(own, received, weight, bias, chunk_tiles)
    return out.reshape(1, piece, feat_width)


def solution(mesh):
    in_specs = (
        P(("groups", "row"), "col", None),
        P(("groups", "row"), "col", None, None),
        P(("groups", "row"), "col", None),
        P(("groups", "row"), "col", None),
        P(("groups", "row"), "col"),
        P(),
        P(),
    )
    out_specs = P(("groups", "col"), "row", None)
    return jax.shard_map(
        on_device, mesh=mesh, in_specs=in_specs, out_specs=out_specs, check_vma=False
    )
```
